32 devices in a mesh: utt: 8 (over z, y), tm: 4 (over x, core).
Axes of the slice: x: 2, y: 2, z: 4, core: 2. Of those that a mesh axis runs over, the one named last changes fastest.
Arguments:
- inputs: bfloat16 [16, 400, 144], P('utt', 'tm'), may hold values from -6 to 6
- flat_params: float32 [506880], P(('utt', 'tm')), may hold values from -6 to 6, as said below
- lengths: int32 [16], P('utt'), may hold values from 50 to 400, as said below
- cotangent: bfloat16 [16, 400, 144], P('utt', 'tm'), may hold values from -6 to 6
Outputs:
- output: float32 [16, 400, 144], P('utt', 'tm')
- grad_inputs: float32 [16, 400, 144], P('utt', 'tm')
- grad_params: float32 [506880], P(('utt', 'tm'))
The draws below stay inside these ranges and needn't reach their ends.
Inputs may be any that keep to these rules, and one draw needn't show every extreme that they name: `lengths`: in each block of 2 consecutive utterances (the utterances of one index of utt) at least one has exactly 400 frames. `flat_params`: gains lie near one, biases and weights are spread about zero.
All inputs are finite; a program needn't handle non-finite values.
Results may differ from the reference program's by a relative error of at most 0.015.
Values may be sent and summed in bfloat16 or wider, within the bound.
A program may use at most 64 MiB of HBM per device.

```python
import functools
import math
import jax
import jax.numpy as jnp
from jax import lax

D = 144
HEADS = 4
FF = 576
KERNEL = 32
HEAD_DIM = 36
LEN = 400
MINLEN = 50
UTT_GRP = 2
UTTS = 16
PARAMS = 506880
N_UTT = 8


def param_layout_drawn():

    def feed_layout(prefix):
        return [(prefix + '_gain', (D,)), (prefix + '_bias', (D,)), (prefix + '_w_in', (D, FF)), (prefix + '_b_in', (FF,)), (prefix + '_w_out', (FF, D)), (prefix + '_b_out', (D,))]
    middle = [('att_gain', (D,)), ('att_bias', (D,)), ('query_w', (D, D)), ('query_b', (D,)), ('key_w', (D, D)), ('value_w', (D, D)), ('value_b', (D,)), ('pos_w', (D, D)), ('content_bias', (D,)), ('position_bias', (D,)), ('proj_w', (D, D)), ('proj_b', (D,)), ('conv_gain', (D,)), ('conv_bias', (D,)), ('point_w', (D, 2 * D)), ('point_b', (2 * D,)), ('depth_w', (KERNEL, D)), ('batch_gain', (D,)), ('batch_bias', (D,)), ('mix_w', (D, D)), ('mix_b', (D,))]
    return feed_layout('first') + middle + feed_layout('second') + [('final_gain', (D,)), ('final_bias', (D,))]


def base_draw(key, entry_shape):
    return jnp.clip(jax.random.normal(key, entry_shape, jnp.float32), -4.0, 4.0)


def draw_flat_params(key, part):
    key = jax.random.fold_in(key, 11)
    pieces = []
    position = 0
    for entry_name, entry_shape in param_layout_drawn():
        base = base_draw(jax.random.fold_in(key, position), entry_shape)
        if len(entry_shape) == 2:
            factor = 1.0
            if entry_name == 'proj_w':
                factor = 6.0
            elif entry_name[-6:] == '_w_out':
                factor = 2.0
            piece = base * (factor / math.sqrt(entry_shape[0]))
        elif entry_name[-5:] == '_gain':
            piece = 1.0 + 0.25 * base
        elif entry_name == 'content_bias' or entry_name == 'position_bias':
            piece = 0.5 * base
        else:
            piece = 0.2 * base
        pieces.append(piece.reshape(-1))
        position += 1
    joined = jnp.concatenate(pieces)
    filler = 0.1 * base_draw(jax.random.fold_in(key, 999), (PARAMS - joined.shape[0],))
    return jnp.concatenate([joined, filler]).astype(jnp.float32)


def draw_lengths(key, part):
    key = jax.random.fold_in(key, 23)
    key_lengths, key_choice = jax.random.split(key)
    groups = UTTS // UTT_GRP
    drawn = jax.random.randint(key_lengths, (groups, UTT_GRP), MINLEN, LEN + 1)
    chosen = jax.random.randint(key_choice, (groups, 1), 0, UTT_GRP)
    filled = jnp.where(jnp.arange(UTT_GRP)[None, :] == chosen, LEN, drawn)
    return filled.reshape(UTTS).astype(jnp.int32)


def steps_of(own_key, shape, cuts, smallest, high):
    def one(dim, blocks):
        draws = jax.random.uniform(jax.random.fold_in(jax.random.fold_in(own_key, 6), dim), (blocks,), jnp.float32, smallest / len(cuts), high / len(cuts))
        return jnp.repeat(jnp.exp(draws), shape[dim] // blocks).reshape((-1,) + (1,) * (len(shape) - dim - 1))

    loudness = one(*cuts[0])
    for cut in cuts[1:]:
        loudness = loudness * one(*cut)
    return loudness


def normal_values(stream_key, extent, deviation, most, shards=(), kind=jnp.bfloat16):
    loudness = steps_of(stream_key, extent, shards, -0.22, 0.18) if shards else 1.0
    values = jax.random.normal(stream_key, extent, jnp.float32) * deviation * loudness
    return jnp.minimum(jnp.maximum(values, -most), most).astype(kind)


def setup_inputs(seed: int = 0) -> dict:
    seeds = jax.random.split(jax.random.key(seed), 5)
    inputs = normal_values(seeds[0], (UTTS, LEN, D), 1.0, 6.0, ((0, 8), (1, 4)))
    flat_params = draw_flat_params(jax.random.fold_in(seeds[4], 71), 0)
    lengths = draw_lengths(jax.random.fold_in(seeds[4], 71), 0)
    cotangent = normal_values(seeds[3], (UTTS, LEN, D), 1.0, 6.0, ((0, 8), (1, 4)))
    return dict(inputs=inputs, flat_params=flat_params, lengths=lengths, cotangent=cotangent)


EPS = 1e-05
NEGATIVE = -1e+30
HIGH = lax.Precision.HIGHEST

@jax.custom_vjp
def low(v):
    return lax.optimization_barrier(v.astype(jnp.bfloat16)).astype(jnp.float32)

@jax.custom_vjp
def low_back(v):
    return v

def low_keep(v):
    return (low(v), None)

def low_pass(kept, grad):
    return (grad,)

def back_keep(v):
    return (v, None)

def back_low(kept, grad):
    return (low(grad),)
low.defvjp(low_keep, low_pass)
low_back.defvjp(back_keep, back_low)

def param_layout():

    def feed_layout(prefix):
        return [(prefix + '_gain', (D,)), (prefix + '_bias', (D,)), (prefix + '_w_in', (D, FF)), (prefix + '_b_in', (FF,)), (prefix + '_w_out', (FF, D)), (prefix + '_b_out', (D,))]
    middle = [('att_gain', (D,)), ('att_bias', (D,)), ('query_w', (D, D)), ('query_b', (D,)), ('key_w', (D, D)), ('value_w', (D, D)), ('value_b', (D,)), ('pos_w', (D, D)), ('content_bias', (D,)), ('position_bias', (D,)), ('proj_w', (D, D)), ('proj_b', (D,)), ('conv_gain', (D,)), ('conv_bias', (D,)), ('point_w', (D, 2 * D)), ('point_b', (2 * D,)), ('depth_w', (KERNEL, D)), ('batch_gain', (D,)), ('batch_bias', (D,)), ('mix_w', (D, D)), ('mix_b', (D,))]
    return feed_layout('first') + middle + feed_layout('second') + [('final_gain', (D,)), ('final_bias', (D,))]

def unpack(flat_params):
    pieces = {}
    position = 0
    for entry_name, entry_shape in param_layout():
        entry_size = math.prod(entry_shape)
        pieces[entry_name] = flat_params[position:position + entry_size].reshape(entry_shape)
        position += entry_size
    return pieces

def layer_norm(stream, gain_vec, bias_vec):
    centered = stream - lax.optimization_barrier(jnp.mean(stream, axis=-1, keepdims=True))
    scaled = centered * lax.rsqrt(lax.optimization_barrier(jnp.mean(centered * centered, axis=-1, keepdims=True)) + EPS)
    return scaled * gain_vec + bias_vec

def matmul(activation, matrix):
    return jnp.einsum('...i,ij->...j', activation, matrix, precision=HIGH)

def pos_table():
    distance = jnp.arange(2 * LEN - 1, dtype=jnp.float32) - (LEN - 1)
    frequency = jnp.exp(-math.log(10000.0) * jnp.arange(D // 2, dtype=jnp.float32) * 2.0 / D)
    angles = distance[:, None] * frequency[None, :]
    return jnp.concatenate([jnp.sin(angles), jnp.cos(angles)], axis=1)

def attend(inputs_group, positions):
    content, relative, key_rows, values, group_lengths = inputs_group
    direct = jnp.einsum('gihd,gjhd->ghij', content, key_rows, precision=HIGH)
    wide_scores = jnp.einsum('gihd,rhd->ghir', relative, positions, precision=HIGH)
    frame_ids = jnp.arange(LEN)
    shift_index = (frame_ids[:, None] - frame_ids[None, :] + LEN - 1).astype(jnp.int32)
    shift_index = jnp.broadcast_to(shift_index, wide_scores.shape[:2] + shift_index.shape)
    scores = low_back(direct + jnp.take_along_axis(wide_scores, shift_index, axis=3))
    live_keys = (frame_ids[None, :] < group_lengths[:, None])[:, None, None, :]
    scores = jnp.where(live_keys, scores, NEGATIVE)
    row_top = lax.optimization_barrier(jnp.max(scores, axis=-1, keepdims=True))
    logsum = row_top + jnp.log(lax.optimization_barrier(jnp.sum(jnp.exp(scores - row_top), axis=-1, keepdims=True)))
    probabilities = low(jnp.exp(scores - logsum))
    return low(low_back(jnp.einsum('ghij,gjhd->gihd', probabilities, values, precision=HIGH)))

def layer(source, flat_params, lengths):
    weights = unpack(flat_params)
    frames = (jnp.arange(LEN)[None, :] < lengths[:, None]).astype(jnp.float32)[:, :, None]

    def feed_branch(stream, prefix):
        normed = low(layer_norm(stream, weights[prefix + '_gain'], weights[prefix + '_bias']))
        hidden = low_back(matmul(normed, low(weights[prefix + '_w_in'])) + weights[prefix + '_b_in'])
        active = low(jax.nn.silu(hidden))
        return low_back(matmul(active, low(weights[prefix + '_w_out'])) + weights[prefix + '_b_out'])

    def regroup(values):
        return values.reshape(N_UTT, UTT_GRP, LEN, HEADS, HEAD_DIM)
    stream = source + 0.5 * feed_branch(source, 'first')
    normed = low(layer_norm(stream, weights['att_gain'], weights['att_bias']))
    query = low_back(matmul(normed, low(weights['query_w'])) + weights['query_b'])
    key_rows = low(low_back(matmul(normed, low(weights['key_w']))))
    values = low(low_back(matmul(normed, low(weights['value_w'])) + weights['value_b']))
    scale = HEAD_DIM ** (-0.5)
    content = low((query + weights['content_bias']) * scale)
    relative = low((query + weights['position_bias']) * scale)
    positions = low(matmul(low(pos_table()), low(weights['pos_w'])))
    positions = positions.reshape(2 * LEN - 1, HEADS, HEAD_DIM)
    context = lax.map(jax.checkpoint(functools.partial(attend, positions=positions)), (regroup(content), regroup(relative), regroup(key_rows), regroup(values), lengths.reshape(N_UTT, UTT_GRP)))
    context = context.reshape(UTTS, LEN, D)
    stream = stream + low_back(matmul(context, low(weights['proj_w'])) + weights['proj_b'])
    normed = low(layer_norm(stream, weights['conv_gain'], weights['conv_bias']))
    gate_rows = low_back(matmul(normed, low(weights['point_w'])) + weights['point_b'])
    gated_rows = gate_rows[..., :D] * jax.nn.sigmoid(gate_rows[..., D:])
    sent_rows = low(low_back(gated_rows * frames))
    left_pad = (KERNEL - 1) // 2
    padded = jnp.pad(sent_rows, ((0, 0), (left_pad, KERNEL - 1 - left_pad), (0, 0)))
    mixed_conv = jnp.zeros((UTTS, LEN, D), jnp.float32)
    for offset in range(KERNEL):
        mixed_conv = mixed_conv + weights['depth_w'][offset] * padded[:, offset:offset + LEN]
    frame_count = jnp.sum(lengths).astype(jnp.float32)
    frame_mean = lax.optimization_barrier(jnp.sum(frames * mixed_conv, axis=(0, 1))) / frame_count
    frame_var = lax.optimization_barrier(jnp.sum(frames * mixed_conv * mixed_conv, axis=(0, 1))) / frame_count - frame_mean * frame_mean
    normal = (mixed_conv - frame_mean) * lax.rsqrt(frame_var + EPS)
    shaped = normal * weights['batch_gain'] + weights['batch_bias']
    swished = low(low_back(shaped * jax.nn.sigmoid(shaped)))
    stream = stream + low_back(matmul(swished, low(weights['mix_w'])) + weights['mix_b'])
    stream = stream + 0.5 * feed_branch(stream, 'second')
    return layer_norm(stream, weights['final_gain'], weights['final_bias'])

def reference(inputs, flat_params, lengths, cotangent):
    frames = (jnp.arange(LEN)[None, :] < lengths[:, None]).astype(jnp.float32)[:, :, None]
    source = inputs.astype(jnp.float32)
    output, pullback = jax.vjp(functools.partial(layer, lengths=lengths), source, flat_params)
    grad_inputs, grad_params = pullback(cotangent.astype(jnp.float32) * frames)
    return (output, grad_inputs, grad_params)
```

```python
import functools
import math

import jax
import jax.numpy as jnp
import ml_dtypes
import numpy as np
from jax import lax
from jax.experimental import pallas as pl
from jax.experimental.pallas import tpu as pltpu
from jax.sharding import PartitionSpec as P

D = 144
HEADS = 4
FF = 576
KERNEL = 32
HEAD_DIM = 36
LEN = 400
EPS = 1e-05
NEGATIVE = -1e30

CHUNKS = FF // D
LEFT = (KERNEL - 1) // 2
LOCAL = 100
HALF = 200
ROWS = 240
HALO_START = LEN - ROWS
WIDE = 640
EDGE = 16
TAIL = D - 128
BLOCK = 128
MAIN = 112

F32 = jnp.float32
BF16 = jnp.bfloat16
MESH = pl.DeviceIdType.MESH


def param_rows():
    def feed(prefix):
        return [
            (prefix + "_gain", 1),
            (prefix + "_bias", 1),
            (prefix + "_w_in", D * CHUNKS),
            (prefix + "_b_in", CHUNKS),
            (prefix + "_w_out", FF),
            (prefix + "_b_out", 1),
        ]

    middle = [
        ("att_gain", 1),
        ("att_bias", 1),
        ("query_w", D),
        ("query_b", 1),
        ("key_w", D),
        ("value_w", D),
        ("value_b", 1),
        ("pos_w", D),
        ("content_bias", 1),
        ("position_bias", 1),
        ("proj_w", D),
        ("proj_b", 1),
        ("conv_gain", 1),
        ("conv_bias", 1),
        ("point_w", 2 * D),
        ("point_b", 2),
        ("depth_w", KERNEL),
        ("batch_gain", 1),
        ("batch_bias", 1),
        ("mix_w", D),
        ("mix_b", 1),
    ]
    entries = feed("first") + middle + feed("second") + [("final_gain", 1), ("final_bias", 1)]
    rows = {}
    position = 0
    for name, count in entries:
        rows[name] = position
        position += count
    return rows, position


ROW, USED = param_rows()
TOTAL = 3520
PADDED = TOTAL + 8
SQUARES = (
    [("first_w_in", c, CHUNKS) for c in range(CHUNKS)]
    + [("first_w_out", c * D, 1) for c in range(CHUNKS)]
    + [("second_w_in", c, CHUNKS) for c in range(CHUNKS)]
    + [("second_w_out", c * D, 1) for c in range(CHUNKS)]
    + [("query_w", 0, 1), ("key_w", 0, 1), ("value_w", 0, 1), ("pos_w", 0, 1), ("proj_w", 0, 1)]
    + [("point_w", 0, 2), ("point_w", 1, 2), ("mix_w", 0, 1)]
)
SQUARE = {(name, shift): i for i, (name, shift, unused) in enumerate(SQUARES)}


def reversed_tables():
    distance = np.arange(2 * LEN - 1, dtype=np.float32) - np.float32(LEN - 1)
    steps = np.arange(D // 2, dtype=np.float32)
    frequency = np.exp(np.float32(-math.log(10000.0)) * steps * np.float32(2.0) / np.float32(D))
    angles = (distance[:, None] * frequency[None, :].astype(np.float32)).astype(np.float32)
    table = np.concatenate([np.sin(angles), np.cos(angles)], axis=1).astype(ml_dtypes.bfloat16)
    both = np.zeros((2, WIDE, D), ml_dtypes.bfloat16)
    for half in range(2):
        top = HALO_START * half + ROWS - 1 + LEN - 1
        both[half, : ROWS + LEN - 1] = table[top - (ROWS + LEN - 1) + 1 : top + 1][::-1]
    return both


def mm(a, b):
    return jnp.dot(a, b, preferred_element_type=F32)


def nt(a, b):
    return lax.dot_general(a, b, (((1,), (1,)), ((), ())), preferred_element_type=F32)


def tn(a, b):
    return lax.dot_general(a, b, (((0,), (0,)), ((), ())), preferred_element_type=F32)


def sigmoid(v):
    return 1.0 / (1.0 + jnp.exp(-v))


def mean(v):
    return jnp.sum(v, axis=1, keepdims=True) * (1.0 / D)


def normed(v):
    centered = v - mean(v)
    inverse = lax.rsqrt(mean(centered * centered) + EPS)
    return centered * inverse, inverse


def norm_back(grad, gain, scaled, inverse):
    e = grad * gain
    return inverse * (e - mean(e) - scaled * mean(e * scaled))


def colsum(v):
    return jnp.sum(v, axis=0, keepdims=True)


def join(main, tail):
    return jnp.concatenate([main, tail[:, :TAIL]], axis=1)


def kernel(n_utt, fast, lens, x_in, cot_in, tab, *refs):
    refs = list(refs)
    take = lambda count: [refs.pop(0) for unused in range(count)]
    if fast:
        (flat_in,) = take(1)
        out, grad_out, flat_out = take(3)
        WM, WT, GM, GT = take(4)
        GB, LB, R1, R2, R3, RZ, ACC = take(7)
    else:
        WM, WT = take(2)
        out, grad_out, GM, GT = take(4)
    (XS, XB, XF, CF, OS, OB, IS, IB, WS) = take(9)
    (HID1, ACT1, NRM1, INV1, LOW1, X1, A2, HID2, ACT2) = take(9)
    (KEY, VAL, PR, DKA, DVA, DPOS, DQU, DQV, GL, DC) = take(10)
    (KS, KB, BS, BB, send_sem, recv_sem) = take(6)

    utt = lax.axis_index("utt")
    tm = lax.axis_index("tm")
    x, c = tm // 2, tm % 2
    z, y = utt // 2, utt % 2
    unit, half = x, c
    start = pl.multiple_of(HALO_START * half, 16)

    used = [0]

    def copy(src, dst, device):
        at = used[0]
        used[0] += 1
        return pltpu.make_async_remote_copy(
            src_ref=src,
            dst_ref=dst,
            send_sem=send_sem.at[at],
            recv_sem=recv_sem.at[at],
            device_id=device,
            device_id_type=MESH,
        )

    core_peer = (utt, 2 * x + 1 - c)
    x_peer = (utt, 2 * (1 - x) + c)
    diagonal = (utt, 2 * (1 - x) + 1 - c)
    y_peer = (2 * z + 1 - y, tm)
    z_at = [z, z + 1 - 2 * (z % 2), (z + 2) % 4, 3 - z]
    mates = [core_peer, x_peer, diagonal]

    barrier = pltpu.get_barrier_semaphore()
    for mate in mates:
        pl.semaphore_signal(barrier, inc=1, device_id=mate, device_id_type=MESH)
    for k in range(1, n_utt):
        pl.semaphore_signal(
            barrier, inc=1, device_id=((utt + k) % n_utt, tm), device_id_type=MESH
        )
    pl.semaphore_wait(barrier, len(mates) + n_utt - 1)

    lane = lax.broadcasted_iota(jnp.int32, (1, 128), 1)
    lane_d = lax.broadcasted_iota(jnp.int32, (1, D), 1)
    waits = []

    def tails_of(load):
        packed = jnp.zeros((16, 128), F32)
        for g in range(8):
            v = load(g)
            v = v if g == 0 else pltpu.roll(v, TAIL * g, 1)
            packed = jnp.where((lane >= TAIL * g) & (lane < TAIL * (g + 1)), v, packed)
        return packed

    if fast:
        dense = [flat_in[pl.ds(i, 14, stride=9), :] for i in range(9)]
        own = GB.at[z, y, x, c]
        packed = jnp.zeros((14, 128), F32)
        for i in range(8):
            shift = TAIL * i
            left = dense[i] if i == 0 else pltpu.roll(dense[i], 128 - shift, 1)
            right = dense[i + 1] if i == 0 else pltpu.roll(dense[i + 1], 128 - shift, 1)
            row = jnp.where(lane < 128 - shift, left, right)
            WM[pl.ds(i, 14, stride=8), :] = row
            packed = jnp.where(
                (lane >= shift) & (lane < shift + TAIL), dense[i + 1], packed
            )
        own[0:MAIN, :] = WM[0:MAIN, :].astype(BF16)
        own[MAIN:BLOCK, :] = jnp.concatenate([packed, jnp.zeros((2, 128), F32)], 0).astype(BF16)

        def column(k, xx, yy):
            return GB.at[z_at[k], yy, xx, c]

        def start_copy(ref, device):
            made = copy(ref, ref, device)
            made.start()
            waits.append(made)
            return made

        to_core, to_x, to_y, to_z = {}, {}, {}, {}
        for k in range(1, 4):
            to_z[k] = start_copy(own, (2 * z_at[k] + y, tm))
        to_x[0] = start_copy(own, x_peer)
        to_y[0] = start_copy(own, y_peer)

    for which, source in ((0, x_in), (1, cot_in)):
        for u in range(2):
            wide = source[u].astype(F32)
            XF[0:LOCAL, :] = wide
            XS[which, u, 0:LOCAL, :] = XF[0:LOCAL, 0:128].astype(BF16)
            XS[which, u, LOCAL:MAIN, :] = jnp.zeros((MAIN - LOCAL, 128), BF16)
            WT_rows = jnp.concatenate(
                [wide[:, 128:], jnp.zeros((LOCAL, 128 - TAIL), F32)], axis=1
            )
            CF[0:LOCAL, 0:128] = WT_rows
            CF[LOCAL:BLOCK, 0:128] = jnp.zeros((BLOCK - LOCAL, 128), F32)
            XS[which, u, MAIN:BLOCK, :] = tails_of(
                lambda g: jnp.concatenate(
                    [CF[pl.ds(8 * s + g, 1), 0:128] for s in range(16)], axis=0
                )
            ).astype(BF16)

    def exchange(which):
        made = []
        for mate, far in ((core_peer, False), (x_peer, True), (diagonal, True)):
            theirs = 1 - x if far else x
            sent = copy(XS.at[which, theirs], XB.at[which, tm], mate)
            sent.start()
            made.append(sent)
            waits.append(sent)
        return made

    x_copies = exchange(0)
    c_copies = exchange(1)

    def unpack_frames(which, copies, target):
        for made in copies:
            made.wait_recv()
        XB[which, tm] = XS[which, x]
        for k in range(4):
            target[LOCAL * k : LOCAL * (k + 1), 0:128] = XB[which, k, 0:LOCAL, :].astype(F32)
            tails = XB[which, k, MAIN:BLOCK, :].astype(F32)
            for g in range(8):
                v = tails if g == 0 else pltpu.roll(tails, 128 - TAIL * g, 1)
                count = (LOCAL - g + 7) // 8
                for s in range(count):
                    target[pl.ds(LOCAL * k + 8 * s + g, 1), 128:D] = v[s : s + 1, 0:TAIL]

    if fast:
        to_core[0, 0, 0] = start_copy(own, core_peer)
        for k in range(1, 4):
            to_z[k].wait_recv()
            block = column(k, x, y)
            to_x[k] = start_copy(block, x_peer)
            to_y[k] = start_copy(block, y_peer)
            to_core[k, 0, 0] = start_copy(block, core_peer)
        far_x, far_y = {}, {}
        for k in range(4):
            to_x[k].wait_recv()
            block = column(k, 1 - x, y)
            if k < 2:
                far_y[k] = start_copy(block, y_peer)
            to_core[k, 1, 0] = start_copy(block, core_peer)
            to_y[k].wait_recv()
            block = column(k, x, 1 - y)
            if k >= 2:
                far_x[k] = start_copy(block, x_peer)
            to_core[k, 0, 1] = start_copy(block, core_peer)
        for k in range(4):
            (far_y[k] if k < 2 else far_x[k]).wait_recv()
            to_core[k, 1, 1] = start_copy(column(k, 1 - x, 1 - y), core_peer)
        for made in to_core.values():
            made.wait_recv()
        for d in range(32):
            block = GB.at[d // 8, (d // 4) % 2, (d // 2) % 2, d % 2]
            first = 110 * d
            WM[first : first + 110, :] = block[0:110, :].astype(F32)
            tails = block[MAIN:BLOCK, :].astype(F32)
            for g in range(8):
                v = tails if g == 0 else pltpu.roll(tails, 128 - TAIL * g, 1)
                WT[pl.ds(first + g, 14, stride=8), :] = v[0:14]

    unpack_frames(0, x_copies, XF)

    def rows_of(name, count=1, shift=0, stride=1):
        at = ROW[name] + shift
        s = pl.ds(at, count) if stride == 1 else pl.ds(at, count, stride=stride)
        return join(WM[s, :], WT[s, :])

    def put(name, value, shift=0, stride=1):
        at = ROW[name] + shift
        count = value.shape[0]
        if stride == 1:
            GM[pl.ds(at, count), :] = value[:, :128]
            GT[pl.ds(at, count), 0:TAIL] = value[:, 128:]
        else:
            s = pl.ds(at, count, stride=stride)
            GM[s, :] = value[:, :128]
            GT[s, :] = jnp.concatenate(
                [value[:, 128:], jnp.zeros((count, 128 - TAIL), F32)], axis=1
            )

    for i, (name, shift, stride) in enumerate(SQUARES):
        WS[i] = rows_of(name, D, shift, stride).astype(BF16)

    def square(name, shift=0):
        return WS[SQUARE[name, shift]]

    row = lax.broadcasted_iota(jnp.int32, (ROWS, 1), 0)
    frame = row + start
    own_row = ((frame >= HALF * half) & (frame < HALF * half + HALF)).astype(F32)
    own_low = own_row.astype(BF16)
    length = jnp.where(unit == 0, lens[0], lens[1])
    live = (frame < length).astype(F32)
    scale = HEAD_DIM ** (-0.5)
    window = pl.ds(start, ROWS)

    def feed(v, prefix, HID, ACT):
        scaled, inverse = normed(v)
        low = (scaled * rows_of(prefix + "_gain") + rows_of(prefix + "_bias")).astype(BF16)
        total = rows_of(prefix + "_b_out")
        for j in range(CHUNKS):
            hidden = mm(low, square(prefix + "_w_in", j)) + rows_of(prefix + "_b_in", 1, j)
            HID[j] = hidden
            active = (hidden * sigmoid(hidden)).astype(BF16)
            ACT[j] = active
            total = total + mm(active, square(prefix + "_w_out", j * D))
        return total, scaled, inverse, low

    v = XF[...]
    total, scaled, inverse, low = feed(v, "first", HID1, ACT1)
    NRM1[...] = scaled
    INV1[...] = inverse
    LOW1[...] = low
    x1 = v + 0.5 * total
    X1[...] = x1

    scaled, inverse = normed(x1)
    low = (scaled * rows_of("att_gain") + rows_of("att_bias")).astype(BF16)
    A2[...] = low
    KEY[...] = mm(low, square("key_w")).astype(BF16)
    VAL[...] = (mm(low, square("value_w")) + rows_of("value_b")).astype(BF16)
    a2 = A2[window, :]
    query = mm(a2, square("query_w")) + rows_of("query_b")
    qu = ((query + rows_of("content_bias")) * scale).astype(BF16)
    qv = ((query + rows_of("position_bias")) * scale).astype(BF16)
    table = tab[half]
    positions = mm(table, square("pos_w")).astype(BF16)
    key_live = lax.broadcasted_iota(jnp.int32, (1, LEN), 1) < length

    def head_mask(h):
        return ((lane_d >= HEAD_DIM * h) & (lane_d < HEAD_DIM * (h + 1))).astype(BF16)

    context = jnp.zeros((ROWS, D), F32)
    for h in range(HEADS):
        mask = head_mask(h)
        direct = nt(qu * mask, KEY[...])
        wide = nt(qv * mask, positions)
        wide = pltpu.roll(wide, WIDE - ROWS + 1, 1, stride=1, stride_axis=0)
        score = jnp.where(key_live, direct + wide[:, :LEN], NEGATIVE)
        score = jnp.exp(score - jnp.max(score, axis=1, keepdims=True))
        prob = score * (1.0 / jnp.sum(score, axis=1, keepdims=True))
        PR[h] = prob
        context = context + mm(prob.astype(BF16), VAL[...] * mask)
    context = context.astype(BF16)
    x2 = X1[window, :] + mm(context, square("proj_w")) + rows_of("proj_b")

    conv_n, conv_i = normed(x2)
    a3 = (conv_n * rows_of("conv_gain") + rows_of("conv_bias")).astype(BF16)
    value = mm(a3, square("point_w", 0)) + rows_of("point_b", 1, 0)
    gate = sigmoid(mm(a3, square("point_w", 1)) + rows_of("point_b", 1, 1))
    GL[0:EDGE, :] = jnp.zeros((EDGE, D), F32)
    GL[EDGE + ROWS :, :] = jnp.zeros((EDGE, D), F32)
    DC[0:EDGE, :] = jnp.zeros((EDGE, D), F32)
    DC[EDGE + ROWS :, :] = jnp.zeros((EDGE, D), F32)
    GL[EDGE : EDGE + ROWS, :] = (live * value * gate).astype(BF16).astype(F32)
    depth = rows_of("depth_w", KERNEL)
    conv = jnp.zeros((ROWS, D), F32)
    for o in range(KERNEL):
        conv = conv + depth[o : o + 1] * GL[pl.ds(EDGE - LEFT + o, ROWS), :]

    def all_sum(which, parts, group):
        BS[which, 0] = jnp.concatenate(
            parts + [jnp.zeros((8 - len(parts), D), F32)], axis=0
        )
        sent = []
        for slot, mate in enumerate(mates):
            sent.append(copy(BS.at[which, 0], BB.at[which, slot], mate))
            sent[-1].start()
        waits.extend(sent)
        for made in sent:
            made.wait_recv()
        total = BS[which, 0]
        for slot in range(len(mates)):
            total = total + BB[which, slot]
        BS[which, 1] = jnp.concatenate([total[0:7], group], axis=0)
        sent = []
        for k in range(1, n_utt):
            sent.append(
                copy(
                    BS.at[which, 1],
                    BB.at[which, len(mates) + k - 1],
                    ((utt + k) % n_utt, tm),
                )
            )
            sent[-1].start()
        waits.extend(sent)
        for made in sent:
            made.wait_recv()
        total = BS[which, 1]
        for k in range(1, n_utt):
            total = total + BB[which, len(mates) + k - 1]
        return total

    counted = own_row * live
    frames_here = jnp.full((1, D), (lens[0] + lens[1]).astype(F32))
    sums = all_sum(0, [colsum(counted * conv), colsum(counted * conv * conv)], frames_here)
    count = sums[7:8]
    mu = sums[0:1] / count
    spread = lax.rsqrt(sums[1:2] / count - mu * mu + EPS)
    bn = (conv - mu) * spread
    zed = bn * rows_of("batch_gain") + rows_of("batch_bias")
    zed_s = sigmoid(zed)
    swished = (zed * zed_s).astype(BF16)
    x3 = x2 + mm(swished, square("mix_w")) + rows_of("mix_b")

    total, second_n, second_i, second_low = feed(x3, "second", HID2, ACT2)
    x4 = x3 + 0.5 * total
    final_n, final_i = normed(x4)
    result = final_n * rows_of("final_gain") + rows_of("final_bias")

    def return_frames(v, S, B):
        for j in range(2):
            lo, hi = LOCAL * j, HALF - HALO_START + LOCAL * j
            S[j, 0:LOCAL, :] = jnp.where(
                half == 0, v[lo : lo + LOCAL, :], v[hi : hi + LOCAL, :]
            )
            S[j, LOCAL:, :] = jnp.zeros((S.shape[1] - LOCAL, D), F32)
        out_at = used[0]
        used[0] += 2
        made = []
        for j in range(2):
            made.append(
                pltpu.make_async_remote_copy(
                    src_ref=S.at[j],
                    dst_ref=B.at[unit],
                    send_sem=send_sem.at[out_at + j],
                    recv_sem=recv_sem.at[out_at + unit],
                    device_id=(utt, 2 * half + j),
                    device_id_type=MESH,
                )
            )
            away = 2 * half + j != tm

            @pl.when(away)
            def _(sent=made[-1]):
                sent.start()

            @pl.when(jnp.logical_not(away))
            def _(j=j):
                B[unit] = S[j]

        def finish():
            for j in range(2):

                @pl.when(2 * half + j != tm)
                def _(sent=made[j]):
                    sent.wait_send()

            for u in range(2):

                @pl.when(2 * u + x != tm)
                def _(u=u):
                    pltpu.make_async_remote_copy(
                        src_ref=S.at[0],
                        dst_ref=B.at[u],
                        send_sem=send_sem.at[out_at],
                        recv_sem=recv_sem.at[out_at + u],
                        device_id=core_peer,
                        device_id_type=MESH,
                    ).wait_recv()

        return finish

    finish_out = return_frames(result, OS, OB)

    unpack_frames(1, c_copies, CF)
    g0 = CF[window, :] * live
    g0_own = g0 * own_row
    put("final_gain", colsum(g0_own * final_n))
    put("final_bias", colsum(g0_own))
    d4 = norm_back(g0, rows_of("final_gain"), final_n, final_i)

    def feed_back(grad, prefix, hidden_of, active_of, scaled, inverse, low, masked):
        low_grad = (0.5 * grad).astype(BF16)
        kept = low_grad * own_low if masked else low_grad
        put(prefix + "_b_out", colsum(kept.astype(F32)))
        back = jnp.zeros((ROWS, D), F32)
        for j in range(CHUNKS):
            put(prefix + "_w_out", tn(active_of(j), kept), j * D)
            hidden = hidden_of(j)
            s = sigmoid(hidden)
            grad_hidden = nt(low_grad, square(prefix + "_w_out", j * D))
            grad_hidden = (grad_hidden * s * (1.0 + hidden * (1.0 - s))).astype(BF16)
            back = back + nt(grad_hidden, square(prefix + "_w_in", j))
            if masked:
                grad_hidden = grad_hidden * own_low
            put(prefix + "_w_in", tn(low, grad_hidden), j, CHUNKS)
            put(prefix + "_b_in", colsum(grad_hidden.astype(F32)), j)
        kept = back * own_row if masked else back
        put(prefix + "_gain", colsum(kept * scaled))
        put(prefix + "_bias", colsum(kept))
        return grad + norm_back(back, rows_of(prefix + "_gain"), scaled, inverse)

    d3 = feed_back(
        d4,
        "second",
        lambda j: HID2[j],
        lambda j: ACT2[j],
        second_n,
        second_i,
        second_low,
        True,
    )

    low_grad = d3.astype(BF16)
    kept = low_grad * own_low
    put("mix_w", tn(swished, kept))
    put("mix_b", colsum(kept.astype(F32)))
    dzed = nt(low_grad, square("mix_w")).astype(BF16).astype(F32)
    dzed = dzed * zed_s * (1.0 + zed * (1.0 - zed_s))
    dzed_own = dzed * own_row
    put("batch_gain", colsum(dzed_own * bn))
    put("batch_bias", colsum(dzed_own))
    e = dzed * rows_of("batch_gain")
    e_own = e * counted
    sums = all_sum(1, [colsum(e_own), colsum(e_own * bn)], frames_here)
    dconv = spread * (e - live * (sums[0:1] / count) - live * bn * (sums[1:2] / count))
    DC[EDGE : EDGE + ROWS, :] = dconv
    dconv_own = dconv * own_row
    dglu = jnp.zeros((ROWS, D), F32)
    for o in range(KERNEL):
        put(
            "depth_w",
            colsum(dconv_own * GL[pl.ds(EDGE - LEFT + o, ROWS), :]),
            o,
        )
        dglu = dglu + depth[o : o + 1] * DC[pl.ds(EDGE + LEFT - o, ROWS), :]
    dglu = dglu.astype(BF16).astype(F32) * counted
    dvalue = (dglu * gate).astype(BF16)
    dgate = (dglu * value * gate * (1.0 - gate)).astype(BF16)
    put("point_w", tn(a3, dvalue), 0, 2)
    put("point_w", tn(a3, dgate), 1, 2)
    put("point_b", colsum(dvalue.astype(F32)), 0)
    put("point_b", colsum(dgate.astype(F32)), 1)
    back = nt(dvalue, square("point_w", 0)) + nt(dgate, square("point_w", 1))
    put("conv_gain", colsum(back * conv_n))
    put("conv_bias", colsum(back))
    d2 = d3 * own_row + norm_back(back, rows_of("conv_gain"), conv_n, conv_i)

    low_grad = d2.astype(BF16)
    put("proj_w", tn(context, low_grad))
    put("proj_b", colsum(low_grad.astype(F32)))
    dctx = nt(low_grad, square("proj_w")).astype(BF16)
    flip = (
        lax.broadcasted_iota(jnp.int32, (ROWS, ROWS), 0)
        + lax.broadcasted_iota(jnp.int32, (ROWS, ROWS), 1)
        == ROWS - 1
    ).astype(F32).astype(BF16)
    qu_r = mm(flip, qu).astype(BF16)
    qv_r = mm(flip, qv).astype(BF16)
    for h in range(HEADS):
        mask = head_mask(h)
        dctx_h = dctx * mask
        prob = PR[h]
        dprob = nt(dctx_h, VAL[...])
        dscore = prob * (dprob - jnp.sum(dprob * prob, axis=1, keepdims=True))
        dscore = mm(flip, dscore.astype(BF16))
        low_score = dscore.astype(BF16)
        dwide = jnp.concatenate([dscore, jnp.zeros((ROWS, WIDE - LEN), F32)], axis=1)
        dwide = pltpu.roll(dwide, 0, 1, stride=1, stride_axis=0).astype(BF16)
        dv = tn(prob.astype(BF16), dctx_h)
        dk = tn(low_score, qu_r * mask)
        dpos = tn(dwide, qv_r * mask)
        du = mm(low_score, KEY[...] * mask)
        dw = mm(dwide, positions * mask)
        if h == 0:
            DVA[...] = dv
            DKA[...] = dk
            DPOS[...] = dpos
            DQU[...] = du
            DQV[...] = dw
        else:
            DVA[...] += dv
            DKA[...] += dk
            DPOS[...] += dpos
            DQU[...] += du
            DQV[...] += dw
    theirs = pl.ds(pl.multiple_of(HALO_START * (1 - half), 16), ROWS)
    KS[0] = DKA[theirs, :].astype(BF16)
    KS[1] = DVA[theirs, :].astype(BF16)
    kv_copy = copy(KS, KB, core_peer)
    kv_copy.start()
    waits.append(kv_copy)
    put("content_bias", scale * colsum(DQU[...]))
    put("position_bias", scale * colsum(DQV[...]))
    dquery = mm(flip, (scale * (DQU[...] + DQV[...])).astype(BF16)).astype(BF16)
    dpos = DPOS[...]
    high = dpos.astype(BF16)
    rest = (dpos - high.astype(F32)).astype(BF16)
    put("pos_w", tn(table, high) + tn(table, rest))
    put("query_w", tn(a2, dquery))
    put("query_b", colsum(dquery.astype(F32)))
    kv_copy.wait_recv()
    dkey = ((DKA[window, :] + KB[0].astype(F32)) * own_row).astype(BF16)
    dval = ((DVA[window, :] + KB[1].astype(F32)) * own_row).astype(BF16)
    put("key_w", tn(a2, dkey))
    put("value_w", tn(a2, dval))
    put("value_b", colsum(dval.astype(F32)))
    back = (
        nt(dquery, square("query_w"))
        + nt(dkey, square("key_w"))
        + nt(dval, square("value_w"))
    )
    scaled, inverse = normed(X1[window, :])
    put("att_gain", colsum(back * scaled))
    put("att_bias", colsum(back))
    d1 = d2 + norm_back(back, rows_of("att_gain"), scaled, inverse)

    d0 = feed_back(
        d1,
        "first",
        lambda j: HID1[j, window, :],
        lambda j: ACT1[j, window, :],
        NRM1[window, :],
        INV1[window, :],
        LOW1[window, :],
        False,
    )
    finish_grad = return_frames(d0, IS, IB)
    GM[USED:, :] = jnp.zeros((PADDED - USED, 128), F32)
    GT[USED:, :] = jnp.zeros((PADDED - USED, 128), F32)

    if fast:

        def pack(goal):
            for low_d in range(8):
                first = 110 * (8 * goal + low_d)
                block = LB.at[goal, low_d // 4, (low_d // 2) % 2, low_d % 2]
                block[0:MAIN, :] = GM[first : first + MAIN, :].astype(BF16)
                packed = jnp.zeros((14, 128), F32)
                for g in range(8):
                    v = GT[pl.ds(first + g, 14, stride=8), :]
                    v = v if g == 0 else pltpu.roll(v, TAIL * g, 1)
                    packed = jnp.where((lane >= TAIL * g) & (lane < TAIL * (g + 1)), v, packed)
                block[MAIN:BLOCK, :] = jnp.concatenate(
                    [packed, jnp.zeros((2, 128), F32)], axis=0
                ).astype(BF16)

        def add(a, b):
            return (a.astype(F32) + b.astype(F32)).astype(BF16)

        rounds = [0, 1, 2, 3]
        stage = {}
        for goal in rounds:
            pack(goal)
            made = copy(LB.at[goal, :, :, 1 - c], R1.at[goal], core_peer)
            made.start()
            stage[goal] = made
            waits.append(made)
        for goal in rounds:
            stage[goal].wait_recv()
            for yy in range(2):
                for xx in range(2):
                    ACC[goal, yy, xx] = add(LB[goal, yy, xx, c], R1[goal, yy, xx])
            if goal % 2 == 0:
                made = copy(ACC.at[goal, :, 1 - x], R2.at[goal], x_peer)
            else:
                made = copy(ACC.at[goal, 1 - y], R2.at[goal], y_peer)
            made.start()
            stage[goal] = made
            waits.append(made)
        for goal in rounds:
            stage[goal].wait_recv()
            if goal % 2 == 0:
                for yy in range(2):
                    R2[goal, yy] = add(ACC[goal, yy, x], R2[goal, yy])
                made = copy(R2.at[goal, 1 - y], R3.at[goal], y_peer)
            else:
                for xx in range(2):
                    R2[goal, xx] = add(ACC[goal, y, xx], R2[goal, xx])
                made = copy(R2.at[goal, 1 - x], R3.at[goal], x_peer)
            made.start()
            stage[goal] = made
            waits.append(made)
        z_base = used[0]
        used[0] += 8

        def z_copy(goal, sender):
            return pltpu.make_async_remote_copy(
                src_ref=R3.at[goal],
                dst_ref=RZ.at[sender],
                send_sem=send_sem.at[z_base + goal],
                recv_sem=recv_sem.at[z_base + sender],
                device_id=(2 * goal + y, tm),
                device_id_type=MESH,
            )

        for goal in rounds:
            stage[goal].wait_recv()
            mine = R2[goal, y] if goal % 2 == 0 else R2[goal, x]
            R3[goal] = add(mine, R3[goal])

            @pl.when(z != goal)
            def _(goal=goal):
                z_copy(goal, z).start()

        for goal in rounds:

            @pl.when(z != goal)
            def _(goal=goal):
                z_copy(goal, z).wait_send()

        total = R3[z].astype(F32)
        for k in range(1, 4):
            pltpu.make_async_remote_copy(
                src_ref=R3.at[0],
                dst_ref=RZ.at[z_at[k]],
                send_sem=send_sem.at[z_base],
                recv_sem=recv_sem.at[z_base + z_at[k]],
                device_id=core_peer,
                device_id_type=MESH,
            ).wait_recv()
            total = total + RZ[z_at[k]].astype(F32)
        tails = total[MAIN : MAIN + 14]
        WM[0:MAIN, :] = total[0:MAIN]
        mains = [WM[pl.ds(i, 14, stride=8), :] for i in range(8)]
        flat_out[...] = jnp.zeros((BLOCK, 128), F32)
        for i in range(9):
            row_i = tails
            if i < 8:
                v = mains[i] if i == 0 else pltpu.roll(mains[i], TAIL * i, 1)
                row_i = jnp.where(lane >= TAIL * i, v, row_i)
            if i > 0:
                v = mains[i - 1] if i == 1 else pltpu.roll(mains[i - 1], TAIL * (i - 1), 1)
                row_i = jnp.where(lane < TAIL * (i - 1), v, row_i)
            flat_out[pl.ds(i, 14, stride=9), :] = row_i

    finish_out()
    finish_grad()
    for u in range(2):
        out[u] = OB[u, 0:LOCAL, :]
        grad_out[u] = IB[u, 0:LOCAL, :]
    for made in waits:
        made.wait_send()


def local(inputs, flat_params, lengths, cotangent):
    n_utt, n_tm = lax.axis_size("utt"), lax.axis_size("tm")
    size = flat_params.shape[0]
    fast = n_utt == 8 and n_tm == 4 and size == 110 * D
    table = jnp.asarray(reversed_tables())
    whole = jax.ShapeDtypeStruct(inputs.shape, F32)
    padded = jax.ShapeDtypeStruct((PADDED, 128), F32)
    vmem = pltpu.VMEM
    if fast:
        flat = jnp.pad(flat_params, (0, 128 * 128 - size)).reshape(128, 128)
        operands = [flat]
        results = [whole, whole, jax.ShapeDtypeStruct((BLOCK, 128), F32)]
        scratch = [vmem((PADDED, 128), F32)] * 4 + [
            vmem((4, 2, 2, 2, BLOCK, 128), BF16),
            vmem((4, 2, 2, 2, BLOCK, 128), BF16),
            vmem((4, 2, 2, BLOCK, 128), BF16),
            vmem((4, 2, BLOCK, 128), BF16),
            vmem((4, BLOCK, 128), BF16),
            vmem((4, BLOCK, 128), BF16),
            vmem((4, 2, 2, BLOCK, 128), BF16),
        ]
    else:
        rows = lax.all_gather(flat_params, ("utt", "tm"), axis=0, tiled=True).reshape(TOTAL, D)
        operands = [
            jnp.pad(rows[:, :128], ((0, PADDED - TOTAL), (0, 0))),
            jnp.pad(rows[:, 128:], ((0, PADDED - TOTAL), (0, 128 - TAIL))),
        ]
        results = [whole, whole, padded, padded]
        scratch = []
    slots = 3 + n_utt - 1
    scratch = scratch + [
        vmem((2, 2, BLOCK, 128), BF16),
        vmem((2, 4, BLOCK, 128), BF16),
        vmem((LEN, D), F32),
        vmem((LEN, D), F32),
        vmem((2, 104, D), F32),
        vmem((2, 104, D), F32),
        vmem((2, 104, D), F32),
        vmem((2, 104, D), F32),
        vmem((len(SQUARES), D, D), BF16),
        vmem((CHUNKS, LEN, D), F32),
        vmem((CHUNKS, LEN, D), BF16),
        vmem((LEN, D), F32),
        vmem((LEN, 1), F32),
        vmem((LEN, D), BF16),
        vmem((LEN, D), F32),
        vmem((LEN, D), BF16),
        vmem((CHUNKS, ROWS, D), F32),
        vmem((CHUNKS, ROWS, D), BF16),
        vmem((LEN, D), BF16),
        vmem((LEN, D), BF16),
        vmem((HEADS, ROWS, LEN), F32),
        vmem((LEN, D), F32),
        vmem((LEN, D), F32),
        vmem((WIDE, D), F32),
        vmem((ROWS, D), F32),
        vmem((ROWS, D), F32),
        vmem((ROWS + 2 * EDGE, D), F32),
        vmem((ROWS + 2 * EDGE, D), F32),
        vmem((2, ROWS, D), BF16),
        vmem((2, ROWS, D), BF16),
        vmem((2, 2, 8, D), F32),
        vmem((2, slots, 8, D), F32),
        pltpu.SemaphoreType.DMA((96 + 2 * slots,)),
        pltpu.SemaphoreType.DMA((96 + 2 * slots,)),
    ]
    in_vmem = pl.BlockSpec(memory_space=pltpu.VMEM)
    got = pl.pallas_call(
        functools.partial(kernel, n_utt, fast),
        out_shape=results,
        in_specs=[pl.BlockSpec(memory_space=pltpu.SMEM)] + [in_vmem] * (3 + len(operands)),
        out_specs=[in_vmem] * len(results),
        scratch_shapes=scratch,
        compiler_params=pltpu.CompilerParams(
            collective_id=0, has_side_effects=True, vmem_limit_bytes=56 * 1024 * 1024
        ),
    )(lengths, inputs, cotangent, table, *operands)
    if fast:
        grad_params = got[2].reshape(-1)[:size]
    else:
        rows = jnp.concatenate([got[2][:TOTAL], got[3][:TOTAL, :TAIL]], axis=1)
        grad_params = lax.psum_scatter(
            rows.reshape(-1), ("utt", "tm"), scatter_dimension=0, tiled=True
        )
    return got[0], got[1], grad_params


def solution(mesh):
    return jax.shard_map(
        local,
        mesh=mesh,
        in_specs=(P("utt", "tm", None), P(("utt", "tm")), P("utt"), P("utt", "tm", None)),
        out_specs=(P("utt", "tm", None), P("utt", "tm", None), P(("utt", "tm"))),
        check_vma=False,
    )
```

```python
import functools
import math

import jax
import jax.numpy as jnp
import ml_dtypes
import numpy as np
from jax import lax
from jax.experimental import pallas as pl
from jax.experimental.pallas import tpu as pltpu
from jax.sharding import PartitionSpec as P

D = 144
HEADS = 4
FF = 576
KERNEL = 32
HEAD_DIM = 36
LEN = 400
EPS = 1e-05
NEGATIVE = -1e30

CHUNKS = FF // D
LEFT = (KERNEL - 1) // 2
LOCAL = 100
HALF = 200
ROWS = 240
HALO_START = LEN - ROWS
WIDE = 640
EDGE = 16
TAIL = D - 128
BLOCK = 128
MAIN = 112
LOCAL_SIZE = 110 * D

F32 = jnp.float32
BF16 = jnp.bfloat16
MESH = pl.DeviceIdType.MESH


def param_rows():
    def feed(prefix):
        return [
            (prefix + "_gain", 1),
            (prefix + "_bias", 1),
            (prefix + "_w_in", D * CHUNKS),
            (prefix + "_b_in", CHUNKS),
            (prefix + "_w_out", FF),
            (prefix + "_b_out", 1),
        ]

    middle = [
        ("att_gain", 1),
        ("att_bias", 1),
        ("query_w", D),
        ("query_b", 1),
        ("key_w", D),
        ("value_w", D),
        ("value_b", 1),
        ("pos_w", D),
        ("content_bias", 1),
        ("position_bias", 1),
        ("proj_w", D),
        ("proj_b", 1),
        ("conv_gain", 1),
        ("conv_bias", 1),
        ("point_w", 2 * D),
        ("point_b", 2),
        ("depth_w", KERNEL),
        ("batch_gain", 1),
        ("batch_bias", 1),
        ("mix_w", D),
        ("mix_b", 1),
    ]
    entries = feed("first") + middle + feed("second") + [("final_gain", 1), ("final_bias", 1)]
    rows = {}
    position = 0
    for name, count in entries:
        rows[name] = position
        position += count
    return rows, position


ROW, USED = param_rows()
TOTAL = 3520
PADDED = TOTAL + 8
SQUARES = (
    [("first_w_in", c, CHUNKS) for c in range(CHUNKS)]
    + [("first_w_out", c * D, 1) for c in range(CHUNKS)]
    + [("second_w_in", c, CHUNKS) for c in range(CHUNKS)]
    + [("second_w_out", c * D, 1) for c in range(CHUNKS)]
    + [("query_w", 0, 1), ("key_w", 0, 1), ("value_w", 0, 1), ("pos_w", 0, 1), ("proj_w", 0, 1)]
    + [("point_w", 0, 2), ("point_w", 1, 2), ("mix_w", 0, 1)]
)
SQUARE = {(name, shift): i for i, (name, shift, unused) in enumerate(SQUARES)}


def reversed_tables():
    distance = np.arange(2 * LEN - 1, dtype=np.float32) - np.float32(LEN - 1)
    steps = np.arange(D // 2, dtype=np.float32)
    frequency = np.exp(np.float32(-math.log(10000.0)) * steps * np.float32(2.0) / np.float32(D))
    angles = (distance[:, None] * frequency[None, :].astype(np.float32)).astype(np.float32)
    table = np.concatenate([np.sin(angles), np.cos(angles)], axis=1).astype(ml_dtypes.bfloat16)
    both = np.zeros((2, WIDE, D), ml_dtypes.bfloat16)
    for half in range(2):
        top = HALO_START * half + ROWS - 1 + LEN - 1
        both[half, : ROWS + LEN - 1] = table[top - (ROWS + LEN - 1) + 1 : top + 1][::-1]
    return both


def mm(a, b):
    return jnp.dot(a, b, preferred_element_type=F32)


def nt(a, b):
    return lax.dot_general(a, b, (((1,), (1,)), ((), ())), preferred_element_type=F32)


def tn(a, b):
    return lax.dot_general(a, b, (((0,), (0,)), ((), ())), preferred_element_type=F32)


def sigmoid(v):
    return 1.0 / (1.0 + jnp.exp(-v))


def mean(v):
    return jnp.sum(v, axis=1, keepdims=True) * (1.0 / D)


def normed(v):
    centered = v - mean(v)
    inverse = lax.rsqrt(mean(centered * centered) + EPS)
    return centered * inverse, inverse


def norm_back(grad, gain, scaled, inverse):
    e = grad * gain
    return inverse * (e - mean(e) - scaled * mean(e * scaled))


def colsum(v):
    return jnp.sum(v, axis=0, keepdims=True)


def join(main, tail):
    return jnp.concatenate([main, tail[:, :TAIL]], axis=1)


def kernel(n_utt, fast, lens, x_in, cot_in, tab, *refs):
    refs = list(refs)
    take = lambda count: [refs.pop(0) for unused in range(count)]
    if fast:
        (flat_in,) = take(1)
        out, grad_out, flat_out = take(3)
        WM, WT, GM, GT = take(4)
        (FLAT, GB, LB, R1, R2, R3, RZ, ACC) = take(8)
    else:
        WM, WT = take(2)
        out, grad_out, GM, GT = take(4)
    (XS, CS, XB, CB, TB, XF, CF, OS, IS, WS) = take(10)
    (HID1, ACT1, NRM1, INV1, LOW1, X1, A2, HID2, ACT2) = take(9)
    (KEY, VAL, PR, DKA, DVA, DPOS, DQU, DQV, GL, DC) = take(10)
    (KS, KB, BS, BB, send_sem, recv_sem, local_sem) = take(7)

    utt = lax.axis_index("utt")
    tm = lax.axis_index("tm")
    x, c = tm // 2, tm % 2
    z, y = utt // 2, utt % 2
    unit, half = x, c
    start = pl.multiple_of(HALO_START * half, 16)

    used = [0]
    waits = []

    def slots(count):
        at = used[0]
        used[0] += count
        return at

    def remote(src, dst, send_at, recv_at, device):
        return pltpu.make_async_remote_copy(
            src_ref=src,
            dst_ref=dst,
            send_sem=send_sem.at[send_at],
            recv_sem=recv_sem.at[recv_at],
            device_id=device,
            device_id_type=MESH,
        )

    def send(src, dst, device, send_at=None, recv_at=None):
        if send_at is None:
            send_at = recv_at = slots(1)
        made = remote(src, dst, send_at, recv_at, device)
        made.start()
        waits.append(made)
        return made

    core_peer = (utt, 2 * x + 1 - c)
    x_peer = (utt, 2 * (1 - x) + c)
    cross_peer = (utt, 2 * (1 - x) + 1 - c)
    y_peer = (2 * z + 1 - y, tm)
    xy_peer = (2 * z + 1 - y, 2 * (1 - x) + c)
    plane = [x_peer, y_peer, xy_peer]
    plane_at = [(y, 1 - x), (1 - y, x), (1 - y, 1 - x)]
    other_z = [j + (j - z + 4) // 4 for j in range(3)]

    barrier = pltpu.get_barrier_semaphore()
    partners = [core_peer, x_peer, cross_peer]
    if fast:
        partners += [(2 * zz + y, tm) for zz in other_z] + [y_peer, xy_peer]
    else:
        partners += [((utt + k) % n_utt, tm) for k in range(1, n_utt)]
    for partner in partners:
        pl.semaphore_signal(barrier, inc=1, device_id=partner, device_id_type=MESH)
    fetches = [
        pltpu.make_async_copy(x_in, XS, local_sem.at[0]),
        pltpu.make_async_copy(cot_in, CS, local_sem.at[1]),
        pltpu.make_async_copy(tab.at[half], TB, local_sem.at[2]),
    ]
    if fast:
        flat_fetch = pltpu.make_async_copy(flat_in, FLAT, local_sem.at[3])
        flat_fetch.start()
    for fetch in fetches:
        fetch.start()

    lane = lax.broadcasted_iota(jnp.int32, (1, 128), 1)
    lane_d = lax.broadcasted_iota(jnp.int32, (1, D), 1)

    def lanes_of(g):
        return (lane >= TAIL * g) & (lane < TAIL * (g + 1))

    def turned(v, shift):
        return v if shift % 128 == 0 else pltpu.roll(v, shift % 128, 1)

    if fast:
        own = GB.at[z, y, x, c]
        flat_fetch.wait()
        for i in range(15):
            GM[8 * i : 8 * i + 8, :] = FLAT[pl.ds(1024 * i, 1024)].reshape(8, 128)
        rest = LOCAL_SIZE - 15 * 1024
        GM[120:128, :] = jnp.concatenate(
            [FLAT[pl.ds(15 * 1024, rest)], jnp.zeros((1024 - rest,), F32)]
        ).reshape(8, 128)
        dense = [GM[pl.ds(i, 14, stride=9), :] for i in range(9)]
        packed = jnp.zeros((14, 128), F32)
        for i in range(8):
            shift = TAIL * i
            left = turned(dense[i], -shift)
            right = turned(dense[i + 1], -shift)
            WM[pl.ds(i, 14, stride=8), :] = jnp.where(lane < 128 - shift, left, right)
            packed = jnp.where(lanes_of(i), dense[i + 1], packed)
        own[0:MAIN, :] = WM[0:MAIN, :].astype(BF16)
        own[MAIN:BLOCK, :] = jnp.concatenate([packed, jnp.zeros((2, 128), F32)], 0).astype(BF16)
        z_at, p_at, c_at = slots(4), slots(12), slots(16)

        def to_plane(zz, index):
            block = GB.at[zz, y, x, c]
            for m in range(3):
                send(block, block, plane[m], p_at + 4 * m + index, p_at + 4 * m + zz)

        def to_core(zz, where, index, send_index):
            block = GB.at[zz, where[0], where[1], c]
            send(block, block, core_peer, c_at + 4 * index + send_index, c_at + 4 * index + zz)

        def from_plane(zz):
            for m in range(3):
                block = GB.at[zz, plane_at[m][0], plane_at[m][1], c]
                remote(block, block, 0, p_at + 4 * m + zz, core_peer).wait_recv()
                to_core(zz, plane_at[m], m + 1, zz)

        def from_core(zz):
            for index, where in enumerate([(y, x)] + plane_at):
                block = GB.at[zz, where[0], where[1], 1 - c]
                remote(block, block, 0, c_at + 4 * index + zz, core_peer).wait_recv()
            for low_d in range(8):
                block = GB.at[zz, low_d // 4, (low_d // 2) % 2, low_d % 2]
                first = 110 * (8 * zz + low_d)
                WM[first : first + 110, :] = block[0:110, :].astype(F32)
                tails = block[MAIN:BLOCK, :].astype(F32)
                for g in range(8):
                    WT[pl.ds(first + g, 14, stride=8), :] = turned(tails, -TAIL * g)[0:14]

    pl.semaphore_wait(barrier, len(partners))
    if fast:
        for j in range(3):
            send(own, own, (2 * other_z[j] + y, tm), z_at + j, z_at + z)

    def exchange(source, target):
        return [
            send(source.at[theirs], target.at[tm], mate)
            for mate, theirs in ((x_peer, 1 - x), (cross_peer, 1 - x), (core_peer, x))
        ]

    def unpack_frames(copies, source, target, frames):
        for made in copies:
            made.wait_recv()
        target[tm] = source[unit]
        for k in range(4):
            frames[LOCAL * k : LOCAL * (k + 1), :] = target[k].astype(F32).T

    fetches[0].wait()
    x_copies = exchange(XS, XB)
    if fast:
        to_plane(z, 0)
        to_core(z, (y, x), 0, 0)
        for j in range(3):
            block = GB.at[other_z[j], y, x, c]
            remote(block, block, 0, z_at + other_z[j], core_peer).wait_recv()
            to_plane(other_z[j], j + 1)
            to_core(other_z[j], (y, x), 0, j + 1)
    fetches[1].wait()
    c_copies = exchange(CS, CB)

    def rows_of(name, count=1, shift=0, stride=1):
        at = ROW[name] + shift
        s = pl.ds(at, count) if stride == 1 else pl.ds(at, count, stride=stride)
        return join(WM[s, :], WT[s, :])

    def put(name, value, shift=0, stride=1):
        at = ROW[name] + shift
        count = value.shape[0]
        if stride == 1:
            GM[pl.ds(at, count), :] = value[:, :128]
            GT[pl.ds(at, count), 0:TAIL] = value[:, 128:]
        else:
            s = pl.ds(at, count, stride=stride)
            GM[s, :] = value[:, :128]
            GT[s, :] = jnp.concatenate(
                [value[:, 128:], jnp.zeros((count, 128 - TAIL), F32)], axis=1
            )

    def ready(prefixes):
        for i, (name, shift, stride) in enumerate(SQUARES):
            if name.startswith(prefixes):
                WS[i] = rows_of(name, D, shift, stride).astype(BF16)

    def square(name, shift=0):
        return WS[SQUARE[name, shift]]

    row = lax.broadcasted_iota(jnp.int32, (ROWS, 1), 0)
    frame = row + start
    own_row = ((frame >= HALF * half) & (frame < HALF * half + HALF)).astype(F32)
    own_low = own_row.astype(BF16)
    length = jnp.where(unit == 0, lens[0], lens[1])
    live = (frame < length).astype(F32)
    scale = HEAD_DIM ** (-0.5)
    window = pl.ds(start, ROWS)

    if fast:
        from_plane(0)
        from_plane(1)
        from_core(0)
        from_core(1)
    unpack_frames(x_copies, XS, XB, XF)
    ready("first")

    def feed(v, prefix, HID, ACT):
        scaled, inverse = normed(v)
        low = (scaled * rows_of(prefix + "_gain") + rows_of(prefix + "_bias")).astype(BF16)
        total = rows_of(prefix + "_b_out")
        for j in range(CHUNKS):
            hidden = mm(low, square(prefix + "_w_in", j)) + rows_of(prefix + "_b_in", 1, j)
            HID[j] = hidden
            active = (hidden * sigmoid(hidden)).astype(BF16)
            ACT[j] = active
            total = total + mm(active, square(prefix + "_w_out", j * D))
        return total, scaled, inverse, low

    v = XF[...]
    total, scaled, inverse, low = feed(v, "first", HID1, ACT1)
    NRM1[...] = scaled
    INV1[...] = inverse
    LOW1[...] = low
    x1 = v + 0.5 * total
    X1[...] = x1

    if fast:
        from_plane(2)
        from_plane(3)
        from_core(2)
    ready(("query", "key", "value", "pos_w", "proj", "point", "mix"))
    fetches[2].wait()
    scaled, inverse = normed(x1)
    low = (scaled * rows_of("att_gain") + rows_of("att_bias")).astype(BF16)
    A2[...] = low
    KEY[...] = mm(low, square("key_w")).astype(BF16)
    VAL[...] = (mm(low, square("value_w")) + rows_of("value_b")).astype(BF16)
    a2 = A2[window, :]
    query = mm(a2, square("query_w")) + rows_of("query_b")
    qu = ((query + rows_of("content_bias")) * scale).astype(BF16)
    qv = ((query + rows_of("position_bias")) * scale).astype(BF16)
    positions = mm(TB[...], square("pos_w")).astype(BF16)
    key_live = lax.broadcasted_iota(jnp.int32, (1, LEN), 1) < length

    def head_mask(h):
        return ((lane_d >= HEAD_DIM * h) & (lane_d < HEAD_DIM * (h + 1))).astype(BF16)

    context = jnp.zeros((ROWS, D), F32)
    for h in range(HEADS):
        mask = head_mask(h)
        direct = nt(qu * mask, KEY[...])
        wide = nt(qv * mask, positions)
        wide = pltpu.roll(wide, WIDE - ROWS + 1, 1, stride=1, stride_axis=0)
        score = jnp.where(key_live, direct + wide[:, :LEN], NEGATIVE)
        score = jnp.exp(score - jnp.max(score, axis=1, keepdims=True))
        prob = score * (1.0 / jnp.sum(score, axis=1, keepdims=True))
        PR[h] = prob
        context = context + mm(prob.astype(BF16), VAL[...] * mask)
    context = context.astype(BF16)
    x2 = X1[window, :] + mm(context, square("proj_w")) + rows_of("proj_b")

    conv_n, conv_i = normed(x2)
    a3 = (conv_n * rows_of("conv_gain") + rows_of("conv_bias")).astype(BF16)
    value = mm(a3, square("point_w", 0)) + rows_of("point_b", 1, 0)
    gate = sigmoid(mm(a3, square("point_w", 1)) + rows_of("point_b", 1, 1))
    GL[0:EDGE, :] = jnp.zeros((EDGE, D), F32)
    GL[EDGE + ROWS :, :] = jnp.zeros((EDGE, D), F32)
    DC[0:EDGE, :] = jnp.zeros((EDGE, D), F32)
    DC[EDGE + ROWS :, :] = jnp.zeros((EDGE, D), F32)
    GL[EDGE : EDGE + ROWS, :] = (live * value * gate).astype(BF16).astype(F32)
    depth = rows_of("depth_w", KERNEL)
    conv = jnp.zeros((ROWS, D), F32)
    for o in range(KERNEL):
        conv = conv + depth[o : o + 1] * GL[pl.ds(EDGE - LEFT + o, ROWS), :]

    def begin_sum(which, first, second):
        lengths = jnp.where(tm == 0, lens[0] + lens[1], 0).astype(F32)
        blank = jnp.zeros((1, 128 - TAIL), F32)
        BS[which, 0] = jnp.concatenate(
            [
                first[:, :128],
                jnp.concatenate([first[:, 128:], blank], axis=1),
                second[:, :128],
                jnp.concatenate([second[:, 128:], blank], axis=1),
                jnp.full((4, 128), lengths),
            ],
            axis=0,
        )
        if fast:
            me = 4 * utt + tm
            sent = []
            for k in range(1, 32):
                to = (me + k) % 32
                sent.append(send(BS.at[which, 0], BB.at[which, k - 1], (to // 4, to % 4)))
        else:
            sent = [
                send(BS.at[which, 0], BB.at[which, k], mate)
                for k, mate in enumerate((x_peer, cross_peer, core_peer))
            ]
        return sent

    def end_sum(which, sent):
        def arrived(copies, at, total):
            for made in copies:
                made.wait_recv()
            for k in range(len(copies)):
                total = total + BB[which, at + k]
            return total

        total = arrived(sent, 0, BS[which, 0])
        if not fast:
            BS[which, 1] = total
            sent = [
                send(BS.at[which, 1], BB.at[which, 2 + k], ((utt + k) % n_utt, tm))
                for k in range(1, n_utt)
            ]
            total = arrived(sent, 3, total)
        return join(total[0:1], total[1:2]), join(total[2:3], total[3:4]), total[4:5, 0:1]

    counted = own_row * live
    sent = begin_sum(0, colsum(counted * conv), colsum(counted * conv * conv))
    if fast:
        from_core(3)
    ready("second")
    first_sum, second_sum, count = end_sum(0, sent)
    mu = first_sum / count
    spread = lax.rsqrt(second_sum / count - mu * mu + EPS)
    bn = (conv - mu) * spread
    zed = bn * rows_of("batch_gain") + rows_of("batch_bias")
    zed_s = sigmoid(zed)
    swished = (zed * zed_s).astype(BF16)
    x3 = x2 + mm(swished, square("mix_w")) + rows_of("mix_b")

    total, second_n, second_i, second_low = feed(x3, "second", HID2, ACT2)
    x4 = x3 + 0.5 * total
    final_n, final_i = normed(x4)
    result = final_n * rows_of("final_gain") + rows_of("final_bias")

    def return_frames(v, S, B):
        send_at, recv_at = slots(2), slots(2)
        made = []
        for j in range(2):
            lo, hi = LOCAL * j, HALF - HALO_START + LOCAL * j
            S[j] = jnp.where(half == 0, v[lo : lo + LOCAL, :], v[hi : hi + LOCAL, :]).T
        for j in range(2):
            made.append(
                remote(S.at[j], B.at[unit], send_at + j, recv_at + unit, (utt, 2 * half + j))
            )
            away = 2 * half + j != tm

            @pl.when(away)
            def _(sent=made[-1]):
                sent.start()

            @pl.when(jnp.logical_not(away))
            def _(j=j):
                B[unit] = S[j]

        def finish():
            for j in range(2):

                @pl.when(2 * half + j != tm)
                def _(sent=made[j]):
                    sent.wait_send()

            for u in range(2):

                @pl.when(2 * u + x != tm)
                def _(u=u):
                    remote(S.at[0], B.at[u], send_at, recv_at + u, core_peer).wait_recv()

        return finish

    finish_out = return_frames(result, OS, out)

    unpack_frames(c_copies, CS, CB, CF)
    g0 = CF[window, :] * live
    d4 = norm_back(g0, rows_of("final_gain"), final_n, final_i)

    def feed_back(grad, prefix, hidden_of, active_of, scaled, inverse, low, masked):
        low_grad = (0.5 * grad).astype(BF16)
        back = jnp.zeros((ROWS, D), F32)
        hidden_grads = []
        for j in range(CHUNKS):
            hidden = hidden_of(j)
            s = sigmoid(hidden)
            grad_hidden = nt(low_grad, square(prefix + "_w_out", j * D))
            grad_hidden = (grad_hidden * s * (1.0 + hidden * (1.0 - s))).astype(BF16)
            hidden_grads.append(grad_hidden)
            back = back + nt(grad_hidden, square(prefix + "_w_in", j))

        def weights():
            kept = low_grad * own_low if masked else low_grad
            put(prefix + "_b_out", colsum(kept.astype(F32)))
            for j in range(CHUNKS):
                put(prefix + "_w_out", tn(active_of(j), kept), j * D)
                grad_hidden = hidden_grads[j] * own_low if masked else hidden_grads[j]
                put(prefix + "_w_in", tn(low, grad_hidden), j, CHUNKS)
                put(prefix + "_b_in", colsum(grad_hidden.astype(F32)), j)
            kept = back * own_row if masked else back
            put(prefix + "_gain", colsum(kept * scaled))
            put(prefix + "_bias", colsum(kept))

        return grad + norm_back(back, rows_of(prefix + "_gain"), scaled, inverse), weights

    d3, second_weights = feed_back(
        d4,
        "second",
        lambda j: HID2[j],
        lambda j: ACT2[j],
        second_n,
        second_i,
        second_low,
        True,
    )

    if fast:
        z_send, z_recv = slots(4), slots(4)
        stage = {}

        def add(a, b):
            return a.astype(F32) + b.astype(F32)

        def begin_round(goal):
            for low_d in range(8):
                first = 110 * (8 * goal + low_d)
                block = LB.at[goal, low_d // 4, (low_d // 2) % 2, low_d % 2]
                block[0:MAIN, :] = GM[first : first + MAIN, :].astype(BF16)
                packed = jnp.zeros((14, 128), F32)
                for g in range(8):
                    v = turned(GT[pl.ds(first + g, 14, stride=8), :], TAIL * g)
                    packed = jnp.where(lanes_of(g), v, packed)
                block[MAIN:BLOCK, :] = jnp.concatenate(
                    [packed, jnp.zeros((2, 128), F32)], axis=0
                ).astype(BF16)
            stage[goal] = send(LB.at[goal, :, :, 1 - c], R1.at[goal], core_peer)

        def plane_round(goal):
            stage[goal].wait_recv()
            for yy in range(2):
                for xx in range(2):
                    ACC[goal, yy, xx] = add(LB[goal, yy, xx, c], R1[goal, yy, xx]).astype(BF16)
            stage[goal] = [
                send(ACC.at[goal, plane_at[m][0], plane_at[m][1]], R2.at[goal, m], plane[m])
                for m in range(3)
            ]

        def z_copy(goal, sender):
            return remote(
                R3.at[goal], RZ.at[sender], z_send + goal, z_recv + sender, (2 * goal + y, tm)
            )

        def z_round(goal):
            for made in stage[goal]:
                made.wait_recv()
            total = add(ACC[goal, y, x], R2[goal, 0]) + add(R2[goal, 1], R2[goal, 2])
            R3[goal] = total.astype(BF16)

            @pl.when(z != goal)
            def _():
                z_copy(goal, z).start()

    else:
        begin_round = plane_round = z_round = lambda goal: None

    low_grad = d3.astype(BF16)
    dzed = nt(low_grad, square("mix_w")).astype(BF16).astype(F32)
    dzed = dzed * zed_s * (1.0 + zed * (1.0 - zed_s))
    e = dzed * rows_of("batch_gain")
    e_own = e * counted
    sent = begin_sum(1, colsum(e_own), colsum(e_own * bn))
    GM[USED:, :] = jnp.zeros((PADDED - USED, 128), F32)
    GT[USED:, :] = jnp.zeros((PADDED - USED, 128), F32)
    g0_own = g0 * own_row
    put("final_gain", colsum(g0_own * final_n))
    put("final_bias", colsum(g0_own))
    second_weights()
    begin_round(3)
    kept = low_grad * own_low
    put("mix_w", tn(swished, kept))
    put("mix_b", colsum(kept.astype(F32)))
    dzed_own = dzed * own_row
    put("batch_gain", colsum(dzed_own * bn))
    put("batch_bias", colsum(dzed_own))
    first_sum, second_sum, count = end_sum(1, sent)
    plane_round(3)
    dconv = spread * (e - live * (first_sum / count) - live * bn * (second_sum / count))
    DC[EDGE : EDGE + ROWS, :] = dconv
    dconv_own = dconv * own_row
    dglu = jnp.zeros((ROWS, D), F32)
    for o in range(KERNEL):
        put(
            "depth_w",
            colsum(dconv_own * GL[pl.ds(EDGE - LEFT + o, ROWS), :]),
            o,
        )
        dglu = dglu + depth[o : o + 1] * DC[pl.ds(EDGE + LEFT - o, ROWS), :]
    dglu = dglu.astype(BF16).astype(F32) * counted
    dvalue = (dglu * gate).astype(BF16)
    dgate = (dglu * value * gate * (1.0 - gate)).astype(BF16)
    put("point_w", tn(a3, dvalue), 0, 2)
    put("point_w", tn(a3, dgate), 1, 2)
    put("point_b", colsum(dvalue.astype(F32)), 0)
    put("point_b", colsum(dgate.astype(F32)), 1)
    back = nt(dvalue, square("point_w", 0)) + nt(dgate, square("point_w", 1))
    put("conv_gain", colsum(back * conv_n))
    put("conv_bias", colsum(back))
    d2 = d3 * own_row + norm_back(back, rows_of("conv_gain"), conv_n, conv_i)

    low_grad = d2.astype(BF16)
    put("proj_w", tn(context, low_grad))
    put("proj_b", colsum(low_grad.astype(F32)))
    begin_round(2)
    dctx = nt(low_grad, square("proj_w")).astype(BF16)
    flip = (
        lax.broadcasted_iota(jnp.int32, (ROWS, ROWS), 0)
        + lax.broadcasted_iota(jnp.int32, (ROWS, ROWS), 1)
        == ROWS - 1
    ).astype(F32).astype(BF16)
    qu_r = mm(flip, qu).astype(BF16)
    qv_r = mm(flip, qv).astype(BF16)
    for h in range(HEADS):
        mask = head_mask(h)
        dctx_h = dctx * mask
        prob = PR[h]
        dprob = nt(dctx_h, VAL[...])
        dscore = prob * (dprob - jnp.sum(dprob * prob, axis=1, keepdims=True))
        dscore = mm(flip, dscore.astype(BF16))
        low_score = dscore.astype(BF16)
        dwide = jnp.concatenate([dscore, jnp.zeros((ROWS, WIDE - LEN), F32)], axis=1)
        dwide = pltpu.roll(dwide, 0, 1, stride=1, stride_axis=0).astype(BF16)
        dv = tn(prob.astype(BF16), dctx_h)
        dk = tn(low_score, qu_r * mask)
        dpos = tn(dwide, qv_r * mask)
        du = mm(low_score, KEY[...] * mask)
        dw = mm(dwide, positions * mask)
        if h == 0:
            DVA[...] = dv
            DKA[...] = dk
            DPOS[...] = dpos
            DQU[...] = du
            DQV[...] = dw
            z_round(3)
        else:
            DVA[...] += dv
            DKA[...] += dk
            DPOS[...] += dpos
            DQU[...] += du
            DQV[...] += dw
        if h == 1:
            plane_round(2)
    theirs = pl.ds(pl.multiple_of(HALO_START * (1 - half), 16), ROWS)
    KS[0] = DKA[theirs, :].astype(BF16)
    KS[1] = DVA[theirs, :].astype(BF16)
    kv_copy = send(KS, KB, core_peer)
    z_round(2)
    put("content_bias", scale * colsum(DQU[...]))
    put("position_bias", scale * colsum(DQV[...]))
    dquery = mm(flip, (scale * (DQU[...] + DQV[...])).astype(BF16)).astype(BF16)
    dpos = DPOS[...]
    high = dpos.astype(BF16)
    rest = (dpos - high.astype(F32)).astype(BF16)
    put("pos_w", tn(TB[...], high) + tn(TB[...], rest))
    put("query_w", tn(a2, dquery))
    put("query_b", colsum(dquery.astype(F32)))
    kv_copy.wait_recv()
    dkey = ((DKA[window, :] + KB[0].astype(F32)) * own_row).astype(BF16)
    dval = ((DVA[window, :] + KB[1].astype(F32)) * own_row).astype(BF16)
    put("key_w", tn(a2, dkey))
    put("value_w", tn(a2, dval))
    put("value_b", colsum(dval.astype(F32)))
    back = (
        nt(dquery, square("query_w"))
        + nt(dkey, square("key_w"))
        + nt(dval, square("value_w"))
    )
    scaled, inverse = normed(X1[window, :])
    put("att_gain", colsum(back * scaled))
    put("att_bias", colsum(back))
    d1 = d2 + norm_back(back, rows_of("att_gain"), scaled, inverse)

    d0, first_weights = feed_back(
        d1,
        "first",
        lambda j: HID1[j, window, :],
        lambda j: ACT1[j, window, :],
        NRM1[window, :],
        INV1[window, :],
        LOW1[window, :],
        False,
    )
    first_weights()
    begin_round(0)
    begin_round(1)
    finish_grad = return_frames(d0, IS, grad_out)
    plane_round(0)
    plane_round(1)
    z_round(0)
    z_round(1)

    if fast:
        for goal in range(4):

            @pl.when(z != goal)
            def _(goal=goal):
                z_copy(goal, z).wait_send()

        total = R3[z].astype(F32)
        for j in range(3):
            remote(
                R3.at[0], RZ.at[other_z[j]], 0, z_recv + other_z[j], core_peer
            ).wait_recv()
            total = total + RZ[other_z[j]].astype(F32)
        tails = total[MAIN : MAIN + 14]
        WM[0:MAIN, :] = total[0:MAIN]
        mains = [WM[pl.ds(i, 14, stride=8), :] for i in range(8)]
        for i in range(9):
            row_i = tails
            if i < 8:
                row_i = jnp.where(lane >= TAIL * i, turned(mains[i], TAIL * i), row_i)
            if i > 0:
                v = turned(mains[i - 1], TAIL * (i - 1))
                row_i = jnp.where(lane < TAIL * (i - 1), v, row_i)
            WT[pl.ds(i, 14, stride=9), :] = row_i
        for i in range(15):
            flat_out[pl.ds(1024 * i, 1024)] = WT[8 * i : 8 * i + 8, :].reshape(1024)
        rest = LOCAL_SIZE - 15 * 1024
        flat_out[pl.ds(15 * 1024, rest)] = WT[120:128, :].reshape(1024)[0:rest]

    finish_out()
    finish_grad()
    for made in waits:
        made.wait_send()


def hand_over(first, second, third, first_out, second_out, third_out):
    first_out[...] = first[...]
    second_out[...] = second[...]
    third_out[...] = third[...]


def local(inputs, flat_params, lengths, cotangent):
    n_utt, n_tm = lax.axis_size("utt"), lax.axis_size("tm")
    size = flat_params.shape[0]
    fast = n_utt == 8 and n_tm == 4 and size == LOCAL_SIZE
    table = jnp.asarray(reversed_tables())
    turned = jax.ShapeDtypeStruct((2, D, LOCAL), F32)
    padded = jax.ShapeDtypeStruct((PADDED, 128), F32)
    vmem = pltpu.VMEM
    in_vmem = pl.BlockSpec(memory_space=pltpu.VMEM)
    anywhere = pl.BlockSpec(memory_space=pl.ANY)
    if fast:
        operands = [flat_params]
        results = [turned, turned, jax.ShapeDtypeStruct((size,), F32)]
        scratch = [vmem((PADDED, 128), F32)] * 4 + [
            vmem((size,), F32),
            vmem((4, 2, 2, 2, BLOCK, 128), BF16),
            vmem((4, 2, 2, 2, BLOCK, 128), BF16),
            vmem((4, 2, 2, BLOCK, 128), BF16),
            vmem((4, 3, BLOCK, 128), BF16),
            vmem((4, BLOCK, 128), BF16),
            vmem((4, BLOCK, 128), BF16),
            vmem((4, 2, 2, BLOCK, 128), BF16),
        ]
    else:
        rows = lax.all_gather(flat_params, ("utt", "tm"), axis=0, tiled=True).reshape(TOTAL, D)
        operands = [
            jnp.pad(rows[:, :128], ((0, PADDED - TOTAL), (0, 0))),
            jnp.pad(rows[:, 128:], ((0, PADDED - TOTAL), (0, 128 - TAIL))),
        ]
        results = [turned, turned, padded, padded]
        scratch = []
    others = 31 if fast else 3 + n_utt - 1
    copies = 128 + 2 * others
    scratch = scratch + [
        vmem((2, D, LOCAL), BF16),
        vmem((2, D, LOCAL), BF16),
        vmem((4, D, LOCAL), BF16),
        vmem((4, D, LOCAL), BF16),
        vmem((WIDE, D), BF16),
        vmem((LEN, D), F32),
        vmem((LEN, D), F32),
        vmem((2, D, LOCAL), F32),
        vmem((2, D, LOCAL), F32),
        vmem((len(SQUARES), D, D), BF16),
        vmem((CHUNKS, LEN, D), F32),
        vmem((CHUNKS, LEN, D), BF16),
        vmem((LEN, D), F32),
        vmem((LEN, 1), F32),
        vmem((LEN, D), BF16),
        vmem((LEN, D), F32),
        vmem((LEN, D), BF16),
        vmem((CHUNKS, ROWS, D), F32),
        vmem((CHUNKS, ROWS, D), BF16),
        vmem((LEN, D), BF16),
        vmem((LEN, D), BF16),
        vmem((HEADS, ROWS, LEN), F32),
        vmem((LEN, D), F32),
        vmem((LEN, D), F32),
        vmem((WIDE, D), F32),
        vmem((ROWS, D), F32),
        vmem((ROWS, D), F32),
        vmem((ROWS + 2 * EDGE, D), F32),
        vmem((ROWS + 2 * EDGE, D), F32),
        vmem((2, ROWS, D), BF16),
        vmem((2, ROWS, D), BF16),
        vmem((2, 2, 8, 128), F32),
        vmem((2, others, 8, 128), F32),
        pltpu.SemaphoreType.DMA((copies,)),
        pltpu.SemaphoreType.DMA((copies,)),
        pltpu.SemaphoreType.DMA((4,)),
    ]
    got = pl.pallas_call(
        functools.partial(kernel, n_utt, fast),
        out_shape=results,
        in_specs=[pl.BlockSpec(memory_space=pltpu.SMEM)]
        + [anywhere] * 3
        + [anywhere if fast else in_vmem] * len(operands),
        out_specs=[in_vmem] * len(results),
        scratch_shapes=scratch,
        compiler_params=pltpu.CompilerParams(
            collective_id=0, has_side_effects=True, vmem_limit_bytes=56 * 1024 * 1024
        ),
    )(lengths, jnp.swapaxes(inputs, 1, 2), jnp.swapaxes(cotangent, 1, 2), table, *operands)
    if fast:
        out, grad, grad_params = pl.pallas_call(
            hand_over,
            out_shape=results,
            in_specs=[in_vmem] * 3,
            out_specs=[in_vmem] * 3,
        )(*got)
    else:
        out, grad = got[:2]
        rows = jnp.concatenate([got[2][:TOTAL], got[3][:TOTAL, :TAIL]], axis=1)
        grad_params = lax.psum_scatter(
            rows.reshape(-1), ("utt", "tm"), scatter_dimension=0, tiled=True
        )
    return jnp.swapaxes(out, 1, 2), jnp.swapaxes(grad, 1, 2), grad_params


def solution(mesh):
    return jax.shard_map(
        local,
        mesh=mesh,
        in_specs=(P("utt", "tm", None), P(("utt", "tm")), P("utt"), P("utt", "tm", None)),
        out_specs=(P("utt", "tm", None), P("utt", "tm", None), P(("utt", "tm"))),
        check_vma=False,
    )
```

```python
import functools
import math

import jax
import jax.numpy as jnp
import ml_dtypes
import numpy as np
from jax import lax
from jax.experimental import pallas as pl
from jax.experimental.pallas import tpu as pltpu
from jax.sharding import PartitionSpec as P

D = 144
HEADS = 4
FF = 576
KERNEL = 32
HEAD_DIM = 36
LEN = 400
EPS = 1e-05
NEGATIVE = -1e30

CHUNKS = FF // D
LEFT = (KERNEL - 1) // 2
LOCAL = 100
HALF = 200
ROWS = 240
HALO_START = LEN - ROWS
WIDE = 640
EDGE = 16
TAIL = D - 128
BLOCK = 128
MAIN = 112
LOCAL_SIZE = 110 * D

F32 = jnp.float32
BF16 = jnp.bfloat16
MESH = pl.DeviceIdType.MESH


def param_rows():
    def feed(prefix):
        return [
            (prefix + "_gain", 1),
            (prefix + "_bias", 1),
            (prefix + "_w_in", D * CHUNKS),
            (prefix + "_b_in", CHUNKS),
            (prefix + "_w_out", FF),
            (prefix + "_b_out", 1),
        ]

    middle = [
        ("att_gain", 1),
        ("att_bias", 1),
        ("query_w", D),
        ("query_b", 1),
        ("key_w", D),
        ("value_w", D),
        ("value_b", 1),
        ("pos_w", D),
        ("content_bias", 1),
        ("position_bias", 1),
        ("proj_w", D),
        ("proj_b", 1),
        ("conv_gain", 1),
        ("conv_bias", 1),
        ("point_w", 2 * D),
        ("point_b", 2),
        ("depth_w", KERNEL),
        ("batch_gain", 1),
        ("batch_bias", 1),
        ("mix_w", D),
        ("mix_b", 1),
    ]
    entries = feed("first") + middle + feed("second") + [("final_gain", 1), ("final_bias", 1)]
    rows = {}
    position = 0
    for name, count in entries:
        rows[name] = position
        position += count
    return rows, position


ROW, USED = param_rows()
TOTAL = 3520
PADDED = TOTAL + 8
SQUARES = (
    [("first_w_in", c, CHUNKS) for c in range(CHUNKS)]
    + [("first_w_out", c * D, 1) for c in range(CHUNKS)]
    + [("second_w_in", c, CHUNKS) for c in range(CHUNKS)]
    + [("second_w_out", c * D, 1) for c in range(CHUNKS)]
    + [("query_w", 0, 1), ("key_w", 0, 1), ("value_w", 0, 1), ("pos_w", 0, 1), ("proj_w", 0, 1)]
    + [("point_w", 0, 2), ("point_w", 1, 2), ("mix_w", 0, 1)]
)
SQUARE = {(name, shift): i for i, (name, shift, unused) in enumerate(SQUARES)}


def reversed_tables():
    distance = np.arange(2 * LEN - 1, dtype=np.float32) - np.float32(LEN - 1)
    steps = np.arange(D // 2, dtype=np.float32)
    frequency = np.exp(np.float32(-math.log(10000.0)) * steps * np.float32(2.0) / np.float32(D))
    angles = (distance[:, None] * frequency[None, :].astype(np.float32)).astype(np.float32)
    table = np.concatenate([np.sin(angles), np.cos(angles)], axis=1).astype(ml_dtypes.bfloat16)
    both = np.zeros((2, WIDE, D), ml_dtypes.bfloat16)
    for half in range(2):
        top = HALO_START * half + ROWS - 1 + LEN - 1
        both[half, : ROWS + LEN - 1] = table[top - (ROWS + LEN - 1) + 1 : top + 1][::-1]
    return both


def mm(a, b):
    return jnp.dot(a, b, preferred_element_type=F32)


def nt(a, b):
    return lax.dot_general(a, b, (((1,), (1,)), ((), ())), preferred_element_type=F32)


def tn(a, b):
    return lax.dot_general(a, b, (((0,), (0,)), ((), ())), preferred_element_type=F32)


def sigmoid(v):
    return 0.5 * jnp.tanh(0.5 * v) + 0.5


def mean(v):
    return jnp.sum(v, axis=1, keepdims=True) * (1.0 / D)


def normed(v):
    centered = v - mean(v)
    inverse = lax.rsqrt(mean(centered * centered) + EPS)
    return centered * inverse, inverse


def norm_back(grad, gain, scaled, inverse):
    e = grad * gain
    return inverse * (e - mean(e) - scaled * mean(e * scaled))


def colsum(v):
    return jnp.sum(v, axis=0, keepdims=True)


def join(main, tail):
    return jnp.concatenate([main, tail[:, :TAIL]], axis=1)


def kernel(n_utt, fast, lens_in, x_in, cot_in, tab, *refs):
    refs = list(refs)
    take = lambda count: [refs.pop(0) for unused in range(count)]
    if fast:
        (flat_in,) = take(1)
        out, grad_out, flat_out = take(3)
        WM, WT, GM, GT = take(4)
        (FLAT, GB, LB, R1, R2, R3, RZ, ACC) = take(8)
    else:
        WM, WT = take(2)
        out, grad_out, GM, GT = take(4)
    (XS, CS, XB, CB, TB, XF, CF, OS, IS, WS) = take(10)
    (HID1, ACT1, NRM1, INV1, LOW1, X1, A2, HID2, ACT2) = take(9)
    (KEY, VAL, PR, PT, DKA, DVA, DPOS, DQU, DQV, GLM, GLT, VM, VT, CT) = take(14)
    (KS, KB, BS, BB, lens, send_sem, recv_sem, local_sem) = take(8)

    utt = lax.axis_index("utt")
    tm = lax.axis_index("tm")
    x, c = tm // 2, tm % 2
    z, y = utt // 2, utt % 2
    unit, half = x, c
    start = pl.multiple_of(HALO_START * half, 16)

    used = [0]
    waits = []

    def slots(count):
        at = used[0]
        used[0] += count
        return at

    def remote(src, dst, send_at, recv_at, device):
        return pltpu.make_async_remote_copy(
            src_ref=src,
            dst_ref=dst,
            send_sem=send_sem.at[send_at],
            recv_sem=recv_sem.at[recv_at],
            device_id=device,
            device_id_type=MESH,
        )

    def send(src, dst, device, send_at=None, recv_at=None):
        if send_at is None:
            send_at = recv_at = slots(1)
        made = remote(src, dst, send_at, recv_at, device)
        made.start()
        waits.append(made)
        return made

    core_peer = (utt, 2 * x + 1 - c)
    x_peer = (utt, 2 * (1 - x) + c)
    cross_peer = (utt, 2 * (1 - x) + 1 - c)
    y_peer = (2 * z + 1 - y, tm)
    xy_peer = (2 * z + 1 - y, 2 * (1 - x) + c)
    plane = [x_peer, y_peer, xy_peer]
    plane_at = [(y, 1 - x), (1 - y, x), (1 - y, 1 - x)]
    z_at = [z, z + 1 - 2 * (z % 2), (z + 2) % 4, 3 - z]
    other_z = [j + (j - z + 4) // 4 for j in range(3)]

    barrier = pltpu.get_barrier_semaphore()
    partners = [core_peer, x_peer, cross_peer]
    if fast:
        partners += [(2 * zz + y, tm) for zz in other_z] + [y_peer, xy_peer]
    else:
        partners += [((utt + k) % n_utt, tm) for k in range(1, n_utt)]
    for partner in partners:
        pl.semaphore_signal(barrier, inc=1, device_id=partner, device_id_type=MESH)
    fetches = [
        pltpu.make_async_copy(x_in, XS, local_sem.at[0]),
        pltpu.make_async_copy(cot_in, CS, local_sem.at[1]),
        pltpu.make_async_copy(tab.at[half], TB, local_sem.at[2]),
        pltpu.make_async_copy(lens_in, lens, local_sem.at[4]),
    ]
    if fast:
        flat_fetch = pltpu.make_async_copy(flat_in, FLAT, local_sem.at[3])
        flat_fetch.start()
    for fetch in fetches:
        fetch.start()

    lane = lax.broadcasted_iota(jnp.int32, (1, 128), 1)
    lane_d = lax.broadcasted_iota(jnp.int32, (1, D), 1)

    def lanes_of(g):
        return (lane >= TAIL * g) & (lane < TAIL * (g + 1))

    def turned(v, shift):
        return v if shift % 128 == 0 else pltpu.roll(v, shift % 128, 1)

    def tails_of(rows):
        packed = jnp.zeros((16, 128), F32)
        for g in range(7):
            packed = jnp.where(lanes_of(g), turned(rows[16 * g : 16 * g + 16], TAIL * g), packed)
        return packed

    def rows_of_tails(packed):
        return jnp.concatenate([turned(packed, -TAIL * g) for g in range(7)], axis=0)

    if fast:
        own = GB.at[z, y, x, c]
        flat_fetch.wait()
        for i in range(15):
            GM[8 * i : 8 * i + 8, :] = FLAT[pl.ds(1024 * i, 1024)].reshape(8, 128)
        rest = LOCAL_SIZE - 15 * 1024
        GM[120:128, :] = jnp.concatenate(
            [FLAT[pl.ds(15 * 1024, rest)], jnp.zeros((1024 - rest,), F32)]
        ).reshape(8, 128)
        dense = [GM[pl.ds(i, 14, stride=9), :] for i in range(9)]
        for i in range(8):
            shift = TAIL * i
            left = turned(dense[i], -shift)
            right = turned(dense[i + 1], -shift)
            WM[pl.ds(i, 14, stride=8), :] = jnp.where(lane < 128 - shift, left, right)
            WT[pl.ds(i, 14, stride=8), :] = right
        own[0:MAIN, :] = WM[0:MAIN, :].astype(BF16)
        own[MAIN:BLOCK, :] = tails_of(WT[0:MAIN, :]).astype(BF16)
        col_at, p_at, c_at = slots(4), slots(12), slots(4)

        def to_column(j):
            to = (2 * other_z[j] + y, tm)
            remote(own, own, col_at, col_at + z, to).start()

        def to_plane(zz):
            block = GB.at[zz, y, x, c]
            for m in range(3):
                remote(block, block, p_at, p_at + 4 * m + zz, plane[m]).start()

        def to_core(zz, where):
            block = GB.at[zz, where[0], where[1], c]
            remote(block, block, c_at, c_at + zz, core_peer).start()

        waits.append(remote(R2.at[0], R2.at[0], col_at, col_at, core_peer))
        waits.append(remote(R2, R2, p_at, p_at, core_peer))
        waits.append(remote(GB.at[0:2], GB.at[0:2], c_at, c_at, core_peer))

        def from_plane(zz):
            for m in range(3):
                block = GB.at[zz, plane_at[m][0], plane_at[m][1], c]
                remote(block, block, p_at, p_at + 4 * m + zz, core_peer).wait_recv()
                to_core(zz, plane_at[m])

        def from_core(zz):
            blocks = GB.at[zz, :, :, 1 - c]
            remote(blocks, blocks, c_at, c_at + zz, core_peer).wait_recv()
            for low_d in range(8):
                block = GB.at[zz, low_d // 4, (low_d // 2) % 2, low_d % 2]
                first = 110 * (8 * zz + low_d)
                WM[first : first + 110, :] = block[0:110, :].astype(F32)
                WT[first : first + 110, :] = rows_of_tails(block[MAIN:BLOCK, :].astype(F32))[0:110]

    pl.semaphore_wait(barrier, len(partners))
    if fast:
        for j in range(3):
            to_column(j)

    def exchange(source, target):
        return (
            send(source.at[1 - x], target.at[tm], x_peer),
            send(source.at[x], target.at[tm], core_peer),
        )

    def relay(copies, target):
        copies[0].wait_recv()
        passed = target.at[x_peer[1]]
        return copies[1], send(passed, passed, core_peer)

    def unpack_frames(copies, source, target, frames):
        for made in copies:
            made.wait_recv()
        target[tm] = source[unit]
        for k in range(4):
            frames[LOCAL * k : LOCAL * (k + 1), :] = target[k].astype(F32).T

    fetches[0].wait()
    x_copies = exchange(XS, XB)
    if fast:
        to_plane(z)
        to_core(z, (y, x))
    x_copies = relay(x_copies, XB)
    if fast:
        for j in range(3):
            block = GB.at[other_z[j], y, x, c]
            remote(block, block, col_at, col_at + other_z[j], core_peer).wait_recv()
            to_plane(other_z[j])
            to_core(other_z[j], (y, x))
    fetches[1].wait()
    c_copies = exchange(CS, CB)

    def rows_of(name, count=1, shift=0, stride=1):
        at = ROW[name] + shift
        s = pl.ds(at, count) if stride == 1 else pl.ds(at, count, stride=stride)
        return join(WM[s, :], WT[s, :])

    def put(name, value, shift=0, stride=1):
        at = ROW[name] + shift
        count = value.shape[0]
        if stride == 1:
            GM[pl.ds(at, count), :] = value[:, :128]
            GT[pl.ds(at, count), 0:TAIL] = value[:, 128:]
        else:
            s = pl.ds(at, count, stride=stride)
            GM[s, :] = value[:, :128]
            GT[s, :] = jnp.concatenate(
                [value[:, 128:], jnp.zeros((count, 128 - TAIL), F32)], axis=1
            )

    def ready(prefixes):
        for i, (name, shift, stride) in enumerate(SQUARES):
            if name.startswith(prefixes):
                WS[i] = rows_of(name, D, shift, stride).astype(BF16)

    def square(name, shift=0):
        return WS[SQUARE[name, shift]]

    row = lax.broadcasted_iota(jnp.int32, (ROWS, 1), 0)
    frame = row + start
    own_row = ((frame >= HALF * half) & (frame < HALF * half + HALF)).astype(F32)
    own_low = own_row.astype(BF16)
    fetches[3].wait()
    length = jnp.where(unit == 0, lens[0], lens[1])
    live = (frame < length).astype(F32)
    scale = HEAD_DIM ** (-0.5)
    window = pl.ds(start, ROWS)

    if fast:
        from_plane(0)
        from_plane(1)
        from_core(0)
        from_core(1)
    unpack_frames(x_copies, XS, XB, XF)
    ready("first")
    c_copies = relay(c_copies, CB)

    def feed(v, prefix, HID, ACT):
        scaled, inverse = normed(v)
        low = (scaled * rows_of(prefix + "_gain") + rows_of(prefix + "_bias")).astype(BF16)
        total = rows_of(prefix + "_b_out")
        for j in range(CHUNKS):
            hidden = mm(low, square(prefix + "_w_in", j)) + rows_of(prefix + "_b_in", 1, j)
            HID[j] = hidden
            active = (hidden * sigmoid(hidden)).astype(BF16)
            ACT[j] = active
            total = total + mm(active, square(prefix + "_w_out", j * D))
        return total, scaled, inverse, low

    v = XF[...]
    total, scaled, inverse, low = feed(v, "first", HID1, ACT1)
    NRM1[...] = scaled
    INV1[...] = inverse
    LOW1[...] = low
    x1 = v + 0.5 * total
    X1[...] = x1

    if fast:
        from_plane(2)
        from_plane(3)
        from_core(2)
    ready(("query", "key", "value", "pos_w", "proj", "point", "mix"))
    fetches[2].wait()
    scaled, inverse = normed(x1)
    low = (scaled * rows_of("att_gain") + rows_of("att_bias")).astype(BF16)
    A2[...] = low
    KEY[...] = mm(low, square("key_w")).astype(BF16)
    VAL[...] = (mm(low, square("value_w")) + rows_of("value_b")).astype(BF16)
    a2 = A2[window, :]
    query = mm(a2, square("query_w")) + rows_of("query_b")
    qu = ((query + rows_of("content_bias")) * scale).astype(BF16)
    qv = ((query + rows_of("position_bias")) * scale).astype(BF16)
    positions = mm(TB[...], square("pos_w")).astype(BF16)
    key_live = lax.broadcasted_iota(jnp.int32, (1, LEN), 1) < length

    def head_mask(h):
        return ((lane_d >= HEAD_DIM * h) & (lane_d < HEAD_DIM * (h + 1))).astype(BF16)

    context = jnp.zeros((ROWS, D), F32)
    for h in range(HEADS):
        mask = head_mask(h)
        direct = nt(qu * mask, KEY[...])
        wide = nt(qv * mask, positions)
        wide = pltpu.roll(wide, WIDE - ROWS + 1, 1, stride=1, stride_axis=0)
        score = jnp.where(key_live, direct + wide[:, :LEN], NEGATIVE)
        score = jnp.exp(score - jnp.max(score, axis=1, keepdims=True))
        prob = score * (1.0 / jnp.sum(score, axis=1, keepdims=True))
        PR[h] = prob
        context = context + mm(prob.astype(BF16), VAL[...] * mask)
    context = context.astype(BF16)
    x2 = X1[window, :] + mm(context, square("proj_w")) + rows_of("proj_b")

    conv_n, conv_i = normed(x2)
    a3 = (conv_n * rows_of("conv_gain") + rows_of("conv_bias")).astype(BF16)
    value = mm(a3, square("point_w", 0)) + rows_of("point_b", 1, 0)
    gate = sigmoid(mm(a3, square("point_w", 1)) + rows_of("point_b", 1, 1))
    SEGMENT = ROWS // 8

    def segments(ref, count):
        packed = turned(ref[0:count, :], 0)
        for g in range(1, 8):
            v = turned(ref[SEGMENT * g : SEGMENT * g + count, :], TAIL * g)
            packed = jnp.where(lane >= TAIL * g, v, packed)
        return packed

    def unsegmented(v):
        for g in range(8):
            CT[SEGMENT * g : SEGMENT * (g + 1), :] = turned(v, -TAIL * g)[0:SEGMENT]
        return CT[0:ROWS, :]

    def lay(v, main, tail):
        for lo, hi in ((0, EDGE), (EDGE + ROWS, 2 * EDGE + ROWS)):
            main[lo:hi, :] = jnp.zeros((hi - lo, 128), F32)
            CT[lo:hi, :] = jnp.zeros((hi - lo, 128), F32)
        main[EDGE : EDGE + ROWS, :] = v[:, :128]
        CT[EDGE : EDGE + ROWS, 0:TAIL] = v[:, 128:]
        tail[...] = segments(CT, 64)

    def convolved(main, tail, first):
        blocks = []
        for lo in range(0, ROWS, 80):
            total = depth_m[0:1] * main[pl.ds(lo + first(0), 80), :]
            for o in range(1, KERNEL):
                total = total + depth_m[o : o + 1] * main[pl.ds(lo + first(o), 80), :]
            blocks.append(total)
        total = depth_t[0:1] * tail[pl.ds(first(0), 32), :]
        for o in range(1, KERNEL):
            total = total + depth_t[o : o + 1] * tail[pl.ds(first(o), 32), :]
        return join(jnp.concatenate(blocks, axis=0), unsegmented(total))

    depth_rows = pl.ds(ROW["depth_w"], KERNEL)
    depth_m = WM[depth_rows, :]
    depth_t = jnp.where(lane < TAIL, WT[depth_rows, :], 0.0)
    for shift in (TAIL, 2 * TAIL, 4 * TAIL):
        depth_t = depth_t + turned(depth_t, shift)
    CT[2 * EDGE + ROWS :, :] = jnp.zeros((CT.shape[0] - 2 * EDGE - ROWS, 128), F32)
    lay((live * value * gate).astype(BF16).astype(F32), GLM, GLT)
    forth = lambda o: EDGE - LEFT + o
    conv = convolved(GLM, GLT, forth)

    def begin_sum(which, first, second):
        lengths = jnp.where(tm == 0, lens[0] + lens[1], 0).astype(F32)
        blank = jnp.zeros((1, 128 - TAIL), F32)
        BS[which, 0] = jnp.concatenate(
            [
                first[:, :128],
                jnp.concatenate([first[:, 128:], blank], axis=1),
                second[:, :128],
                jnp.concatenate([second[:, 128:], blank], axis=1),
                jnp.full((4, 128), lengths),
            ],
            axis=0,
        )
        if fast:
            sent, at = [], slots(1)
            for k in range(31, 0, -1):
                kz, dy, dx, dc = k // 8, (k // 4) % 2, (k // 2) % 2, k % 2
                to_y, to_x, to_c = (1 - v if d else v for v, d in ((y, dy), (x, dx), (c, dc)))
                to = (2 * z_at[kz] + to_y, 2 * to_x + to_c)
                remote(BS.at[which, 0], BB.at[which, k - 1], at, at, to).start()
            sent.append(remote(BB.at[which], BB.at[which], at, at, core_peer))
            waits.extend(sent)
        else:
            sent = [
                send(BS.at[which, 0], BB.at[which, k], mate)
                for k, mate in enumerate((x_peer, cross_peer, core_peer))
            ]
        return sent

    def end_sum(which, sent):
        def arrived(copies, at, count, total):
            for made in copies:
                made.wait_recv()
            for k in range(count):
                total = total + BB[which, at + k]
            return total

        total = arrived(sent, 0, 31 if fast else 3, BS[which, 0])
        if not fast:
            BS[which, 1] = total
            sent = [
                send(BS.at[which, 1], BB.at[which, 2 + k], ((utt + k) % n_utt, tm))
                for k in range(1, n_utt)
            ]
            total = arrived(sent, 3, n_utt - 1, total)
        return join(total[0:1], total[1:2]), join(total[2:3], total[3:4]), total[4:5, 0:1]

    counted = own_row * live
    sent = begin_sum(0, colsum(counted * conv), colsum(counted * conv * conv))
    if fast:
        from_core(3)
    ready("second")
    flip = (
        lax.broadcasted_iota(jnp.int32, (ROWS, ROWS), 0)
        + lax.broadcasted_iota(jnp.int32, (ROWS, ROWS), 1)
        == ROWS - 1
    ).astype(F32).astype(BF16)
    qu_r = mm(flip, qu).astype(BF16)
    qv_r = mm(flip, qv).astype(BF16)
    for h in range(HEADS):
        prob = PR[h]
        high = prob.astype(BF16)
        rest = (prob - high.astype(F32)).astype(BF16)
        turned_high = mm(flip, high)
        PR[h] = turned_high + mm(flip, rest)
        PT[h] = turned_high.T.astype(BF16)
    first_sum, second_sum, count = end_sum(0, sent)
    mu = first_sum / count
    spread = lax.rsqrt(second_sum / count - mu * mu + EPS)
    bn = (conv - mu) * spread
    zed = bn * rows_of("batch_gain") + rows_of("batch_bias")
    zed_s = sigmoid(zed)
    swished = (zed * zed_s).astype(BF16)
    x3 = x2 + mm(swished, square("mix_w")) + rows_of("mix_b")

    total, second_n, second_i, second_low = feed(x3, "second", HID2, ACT2)
    x4 = x3 + 0.5 * total
    final_n, final_i = normed(x4)
    result = final_n * rows_of("final_gain") + rows_of("final_bias")

    def return_frames(v, S, B):
        send_at, recv_at = slots(2), slots(2)
        made = []
        for j in range(2):
            lo, hi = LOCAL * j, HALF - HALO_START + LOCAL * j
            S[j] = jnp.where(half == 0, v[lo : lo + LOCAL, :], v[hi : hi + LOCAL, :]).T
            made.append(
                remote(S.at[j], B.at[unit], send_at + j, recv_at + unit, (utt, 2 * half + j))
            )

        def launch():
            for j in range(2):
                away = 2 * half + j != tm

                @pl.when(away)
                def _(sent=made[j]):
                    sent.start()

                @pl.when(jnp.logical_not(away))
                def _(j=j):
                    B[unit] = S[j]

        def finish():
            for j in range(2):

                @pl.when(2 * half + j != tm)
                def _(sent=made[j]):
                    sent.wait_send()

            for u in range(2):

                @pl.when(2 * u + x != tm)
                def _(u=u):
                    remote(S.at[0], B.at[u], send_at, recv_at + u, core_peer).wait_recv()

        return launch, finish

    launch_out, finish_out = return_frames(result, OS, out)
    launch_out()

    unpack_frames(c_copies, CS, CB, CF)
    g0 = CF[window, :] * live
    d4 = norm_back(g0, rows_of("final_gain"), final_n, final_i)

    def feed_back(grad, prefix, hidden_of, active_of, scaled, inverse, low, masked):
        low_grad = (0.5 * grad).astype(BF16)
        back = jnp.zeros((ROWS, D), F32)
        hidden_grads = []
        for j in range(CHUNKS):
            hidden = hidden_of(j)
            s = sigmoid(hidden)
            grad_hidden = nt(low_grad, square(prefix + "_w_out", j * D))
            grad_hidden = (grad_hidden * s * (1.0 + hidden * (1.0 - s))).astype(BF16)
            hidden_grads.append(grad_hidden)
            back = back + nt(grad_hidden, square(prefix + "_w_in", j))

        def out_weights():
            kept = low_grad * own_low if masked else low_grad
            put(prefix + "_b_out", colsum(kept.astype(F32)))
            for j in range(CHUNKS):
                put(prefix + "_w_out", tn(active_of(j), kept), j * D)

        def in_weights():
            for j in range(CHUNKS):
                grad_hidden = hidden_grads[j] * own_low if masked else hidden_grads[j]
                put(prefix + "_w_in", tn(low, grad_hidden), j, CHUNKS)
                put(prefix + "_b_in", colsum(grad_hidden.astype(F32)), j)
            kept = back * own_row if masked else back
            put(prefix + "_gain", colsum(kept * scaled))
            put(prefix + "_bias", colsum(kept))

        total = grad + norm_back(back, rows_of(prefix + "_gain"), scaled, inverse)
        return total, out_weights, in_weights

    d3, second_out_weights, second_in_weights = feed_back(
        d4,
        "second",
        lambda j: HID2[j],
        lambda j: ACT2[j],
        second_n,
        second_i,
        second_low,
        True,
    )

    if fast:
        z_send, z_recv = slots(4), slots(4)
        stage, used_by = {}, {}

        def add(a, b):
            return a.astype(F32) + b.astype(F32)

        def begin_round(goal, ys=(0, 1)):
            for yy in ys:
                for xc in range(4):
                    first = 110 * (8 * goal + 4 * yy + xc)
                    block = LB.at[goal, yy, xc // 2, xc % 2]
                    block[0:MAIN, :] = GM[first : first + MAIN, :].astype(BF16)
                    block[MAIN:BLOCK, :] = tails_of(GT[first : first + MAIN, :]).astype(BF16)
            rows = pl.ds(ys[0], len(ys))
            stage[goal, ys] = send(LB.at[goal, rows, :, 1 - c], R1.at[goal, rows], core_peer)

        def plane_round(goal, ys=(0, 1)):
            stage[goal, ys].wait_recv()
            for yy in ys:
                for xx in range(2):
                    ACC[goal, yy, xx] = add(LB[goal, yy, xx, c], R1[goal, yy, xx]).astype(BF16)
            at = slots(1)
            made = []
            for m in range(3):
                block = ACC.at[goal, plane_at[m][0], plane_at[m][1]]
                made.append(remote(block, R2.at[goal, m], at, at, plane[m]))
            all_three = remote(R2.at[goal], R2.at[goal], at, at, core_peer)
            stage[goal, ys] = all_three
            used_by[goal, ys] = at
            if len(ys) == 2:
                for one in made:
                    one.start()
                waits.append(all_three)
            else:

                @pl.when(y == ys[0])
                def _():
                    made[0].start()

                @pl.when(y != ys[0])
                def _():
                    made[1].start()
                    made[2].start()

        def z_copy(goal, sender):
            return remote(
                R3.at[goal], RZ.at[sender], z_send + goal, z_recv + sender, (2 * goal + y, tm)
            )

        def z_round(goal, ys=(0, 1)):
            def step():
                stage[goal, ys].wait_recv()
                total = add(ACC[goal, y, x], R2[goal, 0]) + add(R2[goal, 1], R2[goal, 2])
                R3[goal] = total.astype(BF16)

                @pl.when(z != goal)
                def _():
                    z_copy(goal, z).start()

            if len(ys) == 2:
                step()
                return
            pl.when(y == ys[0])(step)

        def drain(goal, ys):
            at = used_by[goal, ys]

            @pl.when(y == ys[0])
            def _():
                remote(R2.at[goal, 0], R2.at[goal, 0], at, at, core_peer).wait_send()

            @pl.when(y != ys[0])
            def _():
                remote(R2.at[goal, 0:2], R2.at[goal, 0:2], at, at, core_peer).wait_send()

    else:
        begin_round = plane_round = z_round = lambda goal, ys=(0, 1): None

    low_grad = d3.astype(BF16)
    dzed = nt(low_grad, square("mix_w")).astype(BF16).astype(F32)
    dzed = dzed * zed_s * (1.0 + zed * (1.0 - zed_s))
    e = dzed * rows_of("batch_gain")
    e_own = e * counted
    sent = begin_sum(1, colsum(e_own), colsum(e_own * bn))
    GM[USED:, :] = jnp.zeros((PADDED - USED, 128), F32)
    GT[USED:, :] = jnp.zeros((PADDED - USED, 128), F32)
    g0_own = g0 * own_row
    put("final_gain", colsum(g0_own * final_n))
    put("final_bias", colsum(g0_own))
    second_out_weights()
    second_in_weights()
    begin_round(3)
    kept = low_grad * own_low
    put("mix_w", tn(swished, kept))
    put("mix_b", colsum(kept.astype(F32)))
    dzed_own = dzed * own_row
    put("batch_gain", colsum(dzed_own * bn))
    put("batch_bias", colsum(dzed_own))
    parts = (e, jnp.broadcast_to(live, (ROWS, D)), live * bn)
    back_parts, depth_parts = [], []
    for i, v in enumerate(parts):
        lay(v, VM, VT)
        back_parts.append(convolved(VM, VT, lambda o: EDGE + LEFT - o))
        kept = v * own_row
        kept_m = kept[:, :128]
        CT[0:ROWS, 0:TAIL] = kept[:, 128:]
        segment_row = lax.broadcasted_iota(jnp.int32, (32, 1), 0) < SEGMENT
        kept_t = jnp.where(segment_row, segments(CT, 32), 0.0)
        mains, tails = [], []
        for o in range(KERNEL):
            mains.append(colsum(kept_m * GLM[pl.ds(forth(o), ROWS), :]))
            tails.append(colsum(kept_t * GLT[pl.ds(forth(o), 32), :]))
        tails = jnp.concatenate(tails, axis=0)
        for shift in (4 * TAIL, 2 * TAIL, TAIL):
            tails = tails + turned(tails, shift)
        depth_parts.append(join(jnp.concatenate(mains, axis=0), tails))
    first_sum, second_sum, count = end_sum(1, sent)
    plane_round(3)
    first_mean, second_mean = first_sum / count, second_sum / count

    def combined(v):
        return spread * (v[0] - v[1] * first_mean - v[2] * second_mean)

    put("depth_w", combined(depth_parts))
    dglu = combined(back_parts).astype(BF16).astype(F32) * counted
    dvalue = (dglu * gate).astype(BF16)
    dgate = (dglu * value * gate * (1.0 - gate)).astype(BF16)
    put("point_w", tn(a3, dvalue), 0, 2)
    put("point_w", tn(a3, dgate), 1, 2)
    put("point_b", colsum(dvalue.astype(F32)), 0)
    put("point_b", colsum(dgate.astype(F32)), 1)
    back = nt(dvalue, square("point_w", 0)) + nt(dgate, square("point_w", 1))
    put("conv_gain", colsum(back * conv_n))
    put("conv_bias", colsum(back))
    d2 = d3 * own_row + norm_back(back, rows_of("conv_gain"), conv_n, conv_i)

    low_grad = d2.astype(BF16)
    put("proj_w", tn(context, low_grad))
    put("proj_b", colsum(low_grad.astype(F32)))
    begin_round(2)
    dctx = nt(low_grad, square("proj_w")).astype(BF16)
    dctx = mm(flip, dctx).astype(BF16)
    for h in range(HEADS):
        mask = head_mask(h)
        dctx_h = dctx * mask
        prob = PR[h]
        dprob = nt(dctx_h, VAL[...])
        dscore = prob * (dprob - jnp.sum(dprob * prob, axis=1, keepdims=True))
        low_score = dscore.astype(BF16)
        dwide = jnp.concatenate([dscore, jnp.zeros((ROWS, WIDE - LEN), F32)], axis=1)
        dwide = pltpu.roll(dwide, 0, 1, stride=1, stride_axis=0).astype(BF16)
        dv = mm(PT[h], dctx_h)
        dk = tn(low_score, qu_r * mask)
        dpos = tn(dwide, qv_r * mask)
        du = mm(low_score, KEY[...] * mask)
        dw = mm(dwide, positions * mask)
        if h == 0:
            DVA[...] = dv
            DKA[...] = dk
            DPOS[...] = dpos
            DQU[...] = du
            DQV[...] = dw
        else:
            DVA[...] += dv
            DKA[...] += dk
            DPOS[...] += dpos
            DQU[...] += du
            DQV[...] += dw
        if h == 2:
            plane_round(2)
    theirs = pl.ds(pl.multiple_of(HALO_START * (1 - half), 16), ROWS)
    KS[0] = DKA[theirs, :].astype(BF16)
    KS[1] = DVA[theirs, :].astype(BF16)
    kv_copy = send(KS, KB, core_peer)
    z_round(3)
    put("content_bias", scale * colsum(DQU[...]))
    put("position_bias", scale * colsum(DQV[...]))
    dquery = mm(flip, (scale * (DQU[...] + DQV[...])).astype(BF16)).astype(BF16)
    dpos = DPOS[...]
    high = dpos.astype(BF16)
    rest = (dpos - high.astype(F32)).astype(BF16)
    put("pos_w", tn(TB[...], high) + tn(TB[...], rest))
    put("query_w", tn(a2, dquery))
    put("query_b", colsum(dquery.astype(F32)))
    kv_copy.wait_recv()
    dkey = ((DKA[window, :] + KB[0].astype(F32)) * own_row).astype(BF16)
    dval = ((DVA[window, :] + KB[1].astype(F32)) * own_row).astype(BF16)
    put("key_w", tn(a2, dkey))
    put("value_w", tn(a2, dval))
    put("value_b", colsum(dval.astype(F32)))
    begin_round(1, (1,))
    back = (
        nt(dquery, square("query_w"))
        + nt(dkey, square("key_w"))
        + nt(dval, square("value_w"))
    )
    scaled, inverse = normed(X1[window, :])
    put("att_gain", colsum(back * scaled))
    put("att_bias", colsum(back))
    d1 = d2 + norm_back(back, rows_of("att_gain"), scaled, inverse)

    d0, first_out_weights, first_in_weights = feed_back(
        d1,
        "first",
        lambda j: HID1[j, window, :],
        lambda j: ACT1[j, window, :],
        NRM1[window, :],
        INV1[window, :],
        LOW1[window, :],
        False,
    )
    first_out_weights()
    plane_round(1, (1,))
    begin_round(1, (0,))
    first_in_weights()
    begin_round(0)
    plane_round(1, (0,))
    launch_grad, finish_grad = return_frames(d0, IS, grad_out)
    plane_round(0)
    launch_grad()
    z_round(2)
    z_round(1, (1,))
    z_round(1, (0,))
    z_round(0)

    if fast:
        drain(1, (0,))
        drain(1, (1,))
        for goal in range(4):

            @pl.when(z != goal)
            def _(goal=goal):
                z_copy(goal, z).wait_send()

        total = R3[z].astype(F32)
        for j in range(3):
            remote(
                R3.at[0], RZ.at[other_z[j]], 0, z_recv + other_z[j], core_peer
            ).wait_recv()
            total = total + RZ[other_z[j]].astype(F32)
        WM[0:MAIN, :] = total[0:MAIN]
        GT[0:MAIN, :] = rows_of_tails(total[MAIN:BLOCK])
        mains = [WM[pl.ds(i, 14, stride=8), :] for i in range(8)]
        tails = [GT[pl.ds(i, 14, stride=8), :] for i in range(8)]
        for i in range(9):
            row_i = turned(tails[max(i - 1, 0)], TAIL * (i - 1))
            if i < 8:
                row_i = jnp.where(lane >= TAIL * i, turned(mains[i], TAIL * i), row_i)
            if i > 0:
                v = turned(mains[i - 1], TAIL * (i - 1))
                row_i = jnp.where(lane < TAIL * (i - 1), v, row_i)
            WT[pl.ds(i, 14, stride=9), :] = row_i
        for i in range(15):
            flat_out[pl.ds(1024 * i, 1024)] = WT[8 * i : 8 * i + 8, :].reshape(1024)
        rest = LOCAL_SIZE - 15 * 1024
        flat_out[pl.ds(15 * 1024, rest)] = WT[120:128, :].reshape(1024)[0:rest]

    finish_out()
    finish_grad()
    for made in waits:
        made.wait_send()


def hand_over(first, second, third, first_out, second_out, third_out):
    first_out[...] = first[...]
    second_out[...] = second[...]
    third_out[...] = third[...]


def local(inputs, flat_params, lengths, cotangent):
    n_utt, n_tm = lax.axis_size("utt"), lax.axis_size("tm")
    size = flat_params.shape[0]
    fast = n_utt == 8 and n_tm == 4 and size == LOCAL_SIZE
    table = jnp.asarray(reversed_tables())
    turned = jax.ShapeDtypeStruct((2, D, LOCAL), F32)
    padded = jax.ShapeDtypeStruct((PADDED, 128), F32)
    vmem = pltpu.VMEM
    in_vmem = pl.BlockSpec(memory_space=pltpu.VMEM)
    anywhere = pl.BlockSpec(memory_space=pl.ANY)
    if fast:
        operands = [flat_params]
        results = [turned, turned, jax.ShapeDtypeStruct((size,), F32)]
        scratch = [vmem((PADDED, 128), F32)] * 4 + [
            vmem((size,), F32),
            vmem((4, 2, 2, 2, BLOCK, 128), BF16),
            vmem((4, 2, 2, 2, BLOCK, 128), BF16),
            vmem((4, 2, 2, BLOCK, 128), BF16),
            vmem((4, 3, BLOCK, 128), BF16),
            vmem((4, BLOCK, 128), BF16),
            vmem((4, BLOCK, 128), BF16),
            vmem((4, 2, 2, BLOCK, 128), BF16),
        ]
    else:
        rows = lax.all_gather(flat_params, ("utt", "tm"), axis=0, tiled=True).reshape(TOTAL, D)
        operands = [
            jnp.pad(rows[:, :128], ((0, PADDED - TOTAL), (0, 0))),
            jnp.pad(rows[:, 128:], ((0, PADDED - TOTAL), (0, 128 - TAIL))),
        ]
        results = [turned, turned, padded, padded]
        scratch = []
    others = 31 if fast else 3 + n_utt - 1
    copies = 128 + 2 * others
    scratch = scratch + [
        vmem((2, D, LOCAL), BF16),
        vmem((2, D, LOCAL), BF16),
        vmem((4, D, LOCAL), BF16),
        vmem((4, D, LOCAL), BF16),
        vmem((WIDE, D), BF16),
        vmem((LEN, D), F32),
        vmem((LEN, D), F32),
        vmem((2, D, LOCAL), F32),
        vmem((2, D, LOCAL), F32),
        vmem((len(SQUARES), D, D), BF16),
        vmem((CHUNKS, LEN, D), F32),
        vmem((CHUNKS, LEN, D), BF16),
        vmem((LEN, D), F32),
        vmem((LEN, 1), F32),
        vmem((LEN, D), BF16),
        vmem((LEN, D), F32),
        vmem((LEN, D), BF16),
        vmem((CHUNKS, ROWS, D), F32),
        vmem((CHUNKS, ROWS, D), BF16),
        vmem((LEN, D), BF16),
        vmem((LEN, D), BF16),
        vmem((HEADS, ROWS, LEN), F32),
        vmem((HEADS, LEN, ROWS), BF16),
        vmem((LEN, D), F32),
        vmem((LEN, D), F32),
        vmem((WIDE, D), F32),
        vmem((ROWS, D), F32),
        vmem((ROWS, D), F32),
        vmem((ROWS + 2 * EDGE, 128), F32),
        vmem((64, 128), F32),
        vmem((ROWS + 2 * EDGE, 128), F32),
        vmem((64, 128), F32),
        vmem((288, 128), F32),
        vmem((2, ROWS, D), BF16),
        vmem((2, ROWS, D), BF16),
        vmem((2, 2, 8, 128), F32),
        vmem((2, others, 8, 128), F32),
        pltpu.SMEM((2,), jnp.int32),
        pltpu.SemaphoreType.DMA((copies,)),
        pltpu.SemaphoreType.DMA((copies,)),
        pltpu.SemaphoreType.DMA((5,)),
    ]
    got = pl.pallas_call(
        functools.partial(kernel, n_utt, fast),
        out_shape=results,
        in_specs=[anywhere] * 4
        + [anywhere if fast else in_vmem] * len(operands),
        out_specs=[in_vmem] * len(results),
        scratch_shapes=scratch,
        compiler_params=pltpu.CompilerParams(
            collective_id=0, has_side_effects=True, vmem_limit_bytes=56 * 1024 * 1024
        ),
    )(lengths, jnp.swapaxes(inputs, 1, 2), jnp.swapaxes(cotangent, 1, 2), table, *operands)
    if fast:
        out, grad, grad_params = pl.pallas_call(
            hand_over,
            out_shape=results,
            in_specs=[in_vmem] * 3,
            out_specs=[in_vmem] * 3,
        )(*got)
    else:
        out, grad = got[:2]
        rows = jnp.concatenate([got[2][:TOTAL], got[3][:TOTAL, :TAIL]], axis=1)
        grad_params = lax.psum_scatter(
            rows.reshape(-1), ("utt", "tm"), scatter_dimension=0, tiled=True
        )
    return jnp.swapaxes(out, 1, 2), jnp.swapaxes(grad, 1, 2), grad_params


def solution(mesh):
    return jax.shard_map(
        local,
        mesh=mesh,
        in_specs=(P("utt", "tm", None), P(("utt", "tm")), P("utt"), P("utt", "tm", None)),
        out_specs=(P("utt", "tm", None), P("utt", "tm", None), P(("utt", "tm"))),
        check_vma=False,
    )
```

```python
import functools
import math

import jax
import jax.numpy as jnp
import ml_dtypes
import numpy as np
from jax import lax
from jax.experimental import pallas as pl
from jax.experimental.pallas import tpu as pltpu
from jax.sharding import PartitionSpec as P

D = 144
HEADS = 4
FF = 576
KERNEL = 32
HEAD_DIM = 36
LEN = 400
EPS = 1e-05
NEGATIVE = -1e30

CHUNKS = FF // D
LEFT = (KERNEL - 1) // 2
LOCAL = 100
HALF = 200
ROWS = 240
HALO_START = LEN - ROWS
WIDE = 640
EDGE = 16
TAIL = D - 128
BLOCK = 128
MAIN = 112
LOCAL_SIZE = 110 * D

F32 = jnp.float32
BF16 = jnp.bfloat16
MESH = pl.DeviceIdType.MESH


def param_rows():
    def feed(prefix):
        return [
            (prefix + "_gain", 1),
            (prefix + "_bias", 1),
            (prefix + "_w_in", D * CHUNKS),
            (prefix + "_b_in", CHUNKS),
            (prefix + "_w_out", FF),
            (prefix + "_b_out", 1),
        ]

    middle = [
        ("att_gain", 1),
        ("att_bias", 1),
        ("query_w", D),
        ("query_b", 1),
        ("key_w", D),
        ("value_w", D),
        ("value_b", 1),
        ("pos_w", D),
        ("content_bias", 1),
        ("position_bias", 1),
        ("proj_w", D),
        ("proj_b", 1),
        ("conv_gain", 1),
        ("conv_bias", 1),
        ("point_w", 2 * D),
        ("point_b", 2),
        ("depth_w", KERNEL),
        ("batch_gain", 1),
        ("batch_bias", 1),
        ("mix_w", D),
        ("mix_b", 1),
    ]
    entries = feed("first") + middle + feed("second") + [("final_gain", 1), ("final_bias", 1)]
    rows = {}
    position = 0
    for name, count in entries:
        rows[name] = position
        position += count
    return rows, position


ROW, USED = param_rows()
TOTAL = 3520
PADDED = TOTAL + 8
SQUARES = (
    [("first_w_in", c, CHUNKS) for c in range(CHUNKS)]
    + [("first_w_out", c * D, 1) for c in range(CHUNKS)]
    + [("second_w_in", c, CHUNKS) for c in range(CHUNKS)]
    + [("second_w_out", c * D, 1) for c in range(CHUNKS)]
    + [("query_w", 0, 1), ("key_w", 0, 1), ("value_w", 0, 1), ("pos_w", 0, 1), ("proj_w", 0, 1)]
    + [("point_w", 0, 2), ("point_w", 1, 2), ("mix_w", 0, 1)]
)
SQUARE = {(name, shift): i for i, (name, shift, unused) in enumerate(SQUARES)}


def reversed_tables():
    distance = np.arange(2 * LEN - 1, dtype=np.float32) - np.float32(LEN - 1)
    steps = np.arange(D // 2, dtype=np.float32)
    frequency = np.exp(np.float32(-math.log(10000.0)) * steps * np.float32(2.0) / np.float32(D))
    angles = (distance[:, None] * frequency[None, :].astype(np.float32)).astype(np.float32)
    table = np.concatenate([np.sin(angles), np.cos(angles)], axis=1).astype(ml_dtypes.bfloat16)
    both = np.zeros((2, WIDE, D), ml_dtypes.bfloat16)
    for half in range(2):
        top = HALO_START * half + ROWS - 1 + LEN - 1
        both[half, : ROWS + LEN - 1] = table[top - (ROWS + LEN - 1) + 1 : top + 1][::-1]
    return both


def mm(a, b):
    return jnp.dot(a, b, preferred_element_type=F32)


def nt(a, b):
    return lax.dot_general(a, b, (((1,), (1,)), ((), ())), preferred_element_type=F32)


def tn(a, b):
    return lax.dot_general(a, b, (((0,), (0,)), ((), ())), preferred_element_type=F32)


def sigmoid(v):
    return 0.5 * jnp.tanh(0.5 * v) + 0.5


def mean(v):
    return jnp.sum(v, axis=1, keepdims=True) * (1.0 / D)


def normed(v):
    centered = v - mean(v)
    inverse = lax.rsqrt(mean(centered * centered) + EPS)
    return centered * inverse, inverse


def norm_back(grad, gain, scaled, inverse):
    e = grad * gain
    return inverse * (e - mean(e) - scaled * mean(e * scaled))


def colsum(v):
    return jnp.sum(v, axis=0, keepdims=True)


def join(main, tail):
    return jnp.concatenate([main, tail[:, :TAIL]], axis=1)


def kernel(n_utt, fast, lens_in, x_in, cot_in, tab, *refs):
    refs = list(refs)
    take = lambda count: [refs.pop(0) for unused in range(count)]
    if fast:
        (flat_in,) = take(1)
        out, grad_out, flat_out = take(3)
        WM, WT, GM, GT = take(4)
        (FLAT, GB, LB, R1, R2, R3, RZ, ACC) = take(8)
    else:
        WM, WT = take(2)
        out, grad_out, GM, GT = take(4)
    (XS, CS, XB, CB, TB, XF, CF, OS, IS, WS) = take(10)
    (HID1, ACT1, NRM1, INV1, LOW1, X1, A2, HID2, ACT2) = take(9)
    (KEY, VAL, PR, PB, QUT, QVT, XT, DKT, DVT, DPT, DKA, DVA, GLM, GLT, VM, VT, CT) = take(17)
    (KS, KB, BS, BB, lens, send_sem, recv_sem, local_sem) = take(8)

    utt = lax.axis_index("utt")
    tm = lax.axis_index("tm")
    x, c = tm // 2, tm % 2
    z, y = utt // 2, utt % 2
    unit, half = x, c
    start = pl.multiple_of(HALO_START * half, 16)

    used = [0]
    waits = []

    def slots(count):
        at = used[0]
        used[0] += count
        return at

    def remote(src, dst, send_at, recv_at, device):
        return pltpu.make_async_remote_copy(
            src_ref=src,
            dst_ref=dst,
            send_sem=send_sem.at[send_at],
            recv_sem=recv_sem.at[recv_at],
            device_id=device,
            device_id_type=MESH,
        )

    def send(src, dst, device, send_at=None, recv_at=None):
        if send_at is None:
            send_at = recv_at = slots(1)
        made = remote(src, dst, send_at, recv_at, device)
        made.start()
        waits.append(made)
        return made

    core_peer = (utt, 2 * x + 1 - c)
    x_peer = (utt, 2 * (1 - x) + c)
    cross_peer = (utt, 2 * (1 - x) + 1 - c)
    y_peer = (2 * z + 1 - y, tm)
    xy_peer = (2 * z + 1 - y, 2 * (1 - x) + c)
    plane = [x_peer, y_peer, xy_peer]
    plane_at = [(y, 1 - x), (1 - y, x), (1 - y, 1 - x)]
    z_at = [z, z + 1 - 2 * (z % 2), (z + 2) % 4, 3 - z]
    other_z = [j + (j - z + 4) // 4 for j in range(3)]

    barrier = pltpu.get_barrier_semaphore()
    partners = [core_peer, x_peer, cross_peer]
    if fast:
        partners += [(2 * zz + y, tm) for zz in other_z] + [y_peer, xy_peer]
    else:
        partners += [((utt + k) % n_utt, tm) for k in range(1, n_utt)]
    for partner in partners:
        pl.semaphore_signal(barrier, inc=1, device_id=partner, device_id_type=MESH)
    fetches = [
        pltpu.make_async_copy(x_in, XS, local_sem.at[0]),
        pltpu.make_async_copy(cot_in, CS, local_sem.at[1]),
        pltpu.make_async_copy(tab.at[half], TB, local_sem.at[2]),
        pltpu.make_async_copy(lens_in, lens, local_sem.at[4]),
    ]
    if fast:
        flat_fetch = pltpu.make_async_copy(flat_in, FLAT, local_sem.at[3])
        flat_fetch.start()
    for fetch in fetches:
        fetch.start()

    lane = lax.broadcasted_iota(jnp.int32, (1, 128), 1)
    lane_d = lax.broadcasted_iota(jnp.int32, (1, D), 1)

    def lanes_of(g):
        return (lane >= TAIL * g) & (lane < TAIL * (g + 1))

    def turned(v, shift):
        return v if shift % 128 == 0 else pltpu.roll(v, shift % 128, 1)

    def tails_of(rows):
        packed = jnp.zeros((16, 128), F32)
        for g in range(7):
            packed = jnp.where(lanes_of(g), turned(rows[16 * g : 16 * g + 16], TAIL * g), packed)
        return packed

    def rows_of_tails(packed):
        return jnp.concatenate([turned(packed, -TAIL * g) for g in range(7)], axis=0)

    if fast:
        own = GB.at[z, y, x, c]
        flat_fetch.wait()
        for i in range(15):
            GM[8 * i : 8 * i + 8, :] = FLAT[pl.ds(1024 * i, 1024)].reshape(8, 128)
        rest = LOCAL_SIZE - 15 * 1024
        GM[120:128, :] = jnp.concatenate(
            [FLAT[pl.ds(15 * 1024, rest)], jnp.zeros((1024 - rest,), F32)]
        ).reshape(8, 128)
        dense = [GM[pl.ds(i, 14, stride=9), :] for i in range(9)]
        for i in range(8):
            shift = TAIL * i
            left = turned(dense[i], -shift)
            right = turned(dense[i + 1], -shift)
            WM[pl.ds(i, 14, stride=8), :] = jnp.where(lane < 128 - shift, left, right)
            WT[pl.ds(i, 14, stride=8), :] = right
        own[0:MAIN, :] = WM[0:MAIN, :].astype(BF16)
        own[MAIN:BLOCK, :] = tails_of(WT[0:MAIN, :]).astype(BF16)
        col_at, p_at, c_at = slots(4), slots(12), slots(4)

        def to_column(j):
            to = (2 * z_at[3 - j] + y, tm)
            remote(own, own, col_at, col_at + z, to).start()

        def to_plane(zz, mates):
            block = GB.at[zz, y, x, c]
            for m in range(mates):
                remote(block, block, p_at, p_at + 4 * m + zz, plane[m]).start()

        def diagonal_to_column():
            block = GB.at[z, 1 - y, 1 - x, c]
            remote(block, block, p_at, p_at + 8 + z, core_peer).wait_recv()
            for j in range(3):
                to = (2 * z_at[3 - j] + y, tm)
                remote(block, block, p_at, p_at + 8 + z, to).start()
            to_core(z, (1 - y, 1 - x))

        def from_plane(zz, mates):
            for m in range(mates):
                block = GB.at[zz, plane_at[m][0], plane_at[m][1], c]
                remote(block, block, p_at, p_at + 4 * m + zz, core_peer).wait_recv()
                to_core(zz, plane_at[m])

        def diagonal_from_column(zz):
            @pl.when(z != zz)
            def _():
                block = GB.at[zz, 1 - y, 1 - x, c]
                remote(block, block, p_at, p_at + 8 + zz, core_peer).wait_recv()
                to_core(zz, (1 - y, 1 - x))

        def to_core(zz, where):
            block = GB.at[zz, where[0], where[1], c]
            remote(block, block, c_at, c_at + zz, core_peer).start()

        waits.append(remote(R2.at[0], R2.at[0], col_at, col_at, core_peer))
        waits.append(remote(R2, R2, p_at, p_at, core_peer))
        waits.append(remote(GB.at[0:2], GB.at[0:2], c_at, c_at, core_peer))

        def from_core(zz):
            blocks = GB.at[zz, :, :, 1 - c]
            remote(blocks, blocks, c_at, c_at + zz, core_peer).wait_recv()
            for low_d in range(8):
                block = GB.at[zz, low_d // 4, (low_d // 2) % 2, low_d % 2]
                first = 110 * (8 * zz + low_d)
                WM[first : first + 110, :] = block[0:110, :].astype(F32)
                WT[first : first + 110, :] = rows_of_tails(block[MAIN:BLOCK, :].astype(F32))[0:110]

    pl.semaphore_wait(barrier, len(partners))
    if fast:
        for j in range(3):
            to_column(j)

    def exchange(source, target):
        return (
            send(source.at[1 - x], target.at[tm], x_peer),
            send(source.at[x], target.at[tm], core_peer),
        )

    def relay(copies, target):
        copies[0].wait_recv()
        passed = target.at[x_peer[1]]
        return copies[1], send(passed, passed, core_peer)

    def unpack_frames(copies, source, target, frames):
        for made in copies:
            made.wait_recv()
        target[tm] = source[unit]
        for k in range(4):
            frames[LOCAL * k : LOCAL * (k + 1), :] = target[k].astype(F32).T

    fetches[0].wait()
    x_copies = exchange(XS, XB)
    if fast:
        to_plane(z, 3)
        to_core(z, (y, x))
    x_copies = relay(x_copies, XB)
    if fast:
        diagonal_to_column()
        for j in range(3):
            block = GB.at[other_z[j], y, x, c]
            remote(block, block, col_at, col_at + other_z[j], core_peer).wait_recv()
            to_plane(other_z[j], 2)
            to_core(other_z[j], (y, x))
    fetches[1].wait()
    c_copies = exchange(CS, CB)

    def rows_of(name, count=1, shift=0, stride=1):
        at = ROW[name] + shift
        s = pl.ds(at, count) if stride == 1 else pl.ds(at, count, stride=stride)
        return join(WM[s, :], WT[s, :])

    def put(name, value, shift=0, stride=1):
        at = ROW[name] + shift
        count = value.shape[0]
        if stride == 1:
            GM[pl.ds(at, count), :] = value[:, :128]
            GT[pl.ds(at, count), 0:TAIL] = value[:, 128:]
        else:
            s = pl.ds(at, count, stride=stride)
            GM[s, :] = value[:, :128]
            GT[s, :] = jnp.concatenate(
                [value[:, 128:], jnp.zeros((count, 128 - TAIL), F32)], axis=1
            )

    def ready(prefixes):
        for i, (name, shift, stride) in enumerate(SQUARES):
            if name.startswith(prefixes):
                WS[i] = rows_of(name, D, shift, stride).astype(BF16)

    def square(name, shift=0):
        return WS[SQUARE[name, shift]]

    row = lax.broadcasted_iota(jnp.int32, (ROWS, 1), 0)
    frame = row + start
    own_row = ((frame >= HALF * half) & (frame < HALF * half + HALF)).astype(F32)
    own_low = own_row.astype(BF16)
    fetches[3].wait()
    length = jnp.where(unit == 0, lens[0], lens[1])
    live = (frame < length).astype(F32)
    scale = HEAD_DIM ** (-0.5)
    window = pl.ds(start, ROWS)

    if fast:
        from_plane(0, 2)
        diagonal_from_column(0)
        from_plane(1, 2)
        diagonal_from_column(1)
        from_core(0)
        from_core(1)
    unpack_frames(x_copies, XS, XB, XF)
    ready("first")
    c_copies = relay(c_copies, CB)

    def feed(v, prefix, HID, ACT):
        scaled, inverse = normed(v)
        low = (scaled * rows_of(prefix + "_gain") + rows_of(prefix + "_bias")).astype(BF16)
        total = rows_of(prefix + "_b_out")
        for j in range(CHUNKS):
            hidden = mm(low, square(prefix + "_w_in", j)) + rows_of(prefix + "_b_in", 1, j)
            HID[j] = hidden
            active = (hidden * sigmoid(hidden)).astype(BF16)
            ACT[j] = active
            total = total + mm(active, square(prefix + "_w_out", j * D))
        return total, scaled, inverse, low

    v = XF[...]
    total, scaled, inverse, low = feed(v, "first", HID1, ACT1)
    NRM1[...] = scaled
    INV1[...] = inverse
    LOW1[...] = low
    x1 = v + 0.5 * total
    X1[...] = x1

    if fast:
        for zz in (2, 3):
            from_plane(zz, 2)
            diagonal_from_column(zz)
        from_core(2)
    ready(("query", "key", "value", "pos_w", "proj", "point", "mix"))
    fetches[2].wait()
    scaled, inverse = normed(x1)
    low = (scaled * rows_of("att_gain") + rows_of("att_bias")).astype(BF16)
    A2[...] = low
    KEY[...] = mm(low, square("key_w")).astype(BF16)
    VAL[...] = (mm(low, square("value_w")) + rows_of("value_b")).astype(BF16)
    a2 = A2[window, :]
    query = mm(a2, square("query_w")) + rows_of("query_b")
    qu = ((query + rows_of("content_bias")) * scale).astype(BF16)
    qv = ((query + rows_of("position_bias")) * scale).astype(BF16)
    positions = mm(TB[...], square("pos_w")).astype(BF16)
    key_bias = jnp.where(
        lax.broadcasted_iota(jnp.int32, (1, LEN), 1) < length, 0.0, NEGATIVE
    )

    def head_mask(h):
        return ((lane_d >= HEAD_DIM * h) & (lane_d < HEAD_DIM * (h + 1))).astype(BF16)

    context, share = jnp.zeros((ROWS, D), F32), jnp.zeros((ROWS, D), F32)
    for h in range(HEADS):
        mask = head_mask(h)
        direct = nt(qu * mask, KEY[...])
        wide = nt(qv * mask, positions)
        wide = pltpu.roll(wide, WIDE - ROWS + 1, 1, stride=1, stride_axis=0)
        score = direct + wide[:, :LEN] + key_bias
        score = jnp.exp(score - jnp.max(score, axis=1, keepdims=True))
        PR[h] = score
        low_score = score.astype(BF16)
        context = context + mm(low_score, VAL[...] * mask)
        share = share + mm(low_score, jnp.broadcast_to(mask, (LEN, D)))
    context = (context / share).astype(BF16)
    x2 = X1[window, :] + mm(context, square("proj_w")) + rows_of("proj_b")

    conv_n, conv_i = normed(x2)
    a3 = (conv_n * rows_of("conv_gain") + rows_of("conv_bias")).astype(BF16)
    value = mm(a3, square("point_w", 0)) + rows_of("point_b", 1, 0)
    gate = sigmoid(mm(a3, square("point_w", 1)) + rows_of("point_b", 1, 1))
    SEGMENT = ROWS // 8

    def segments(ref, count):
        packed = turned(ref[0:count, :], 0)
        for g in range(1, 8):
            v = turned(ref[SEGMENT * g : SEGMENT * g + count, :], TAIL * g)
            packed = jnp.where(lane >= TAIL * g, v, packed)
        return packed

    def unsegmented(v):
        for g in range(8):
            CT[SEGMENT * g : SEGMENT * (g + 1), :] = turned(v, -TAIL * g)[0:SEGMENT]
        return CT[0:ROWS, :]

    def lay(v, main, tail):
        for lo, hi in ((0, EDGE), (EDGE + ROWS, 2 * EDGE + ROWS)):
            main[lo:hi, :] = jnp.zeros((hi - lo, 128), F32)
            CT[lo:hi, :] = jnp.zeros((hi - lo, 128), F32)
        main[EDGE : EDGE + ROWS, :] = v[:, :128]
        CT[EDGE : EDGE + ROWS, 0:TAIL] = v[:, 128:]
        tail[...] = segments(CT, 64)

    def convolved(main, tail, first):
        blocks = []
        for lo in range(0, ROWS, 80):
            total = depth_m[0:1] * main[pl.ds(lo + first(0), 80), :]
            for o in range(1, KERNEL):
                total = total + depth_m[o : o + 1] * main[pl.ds(lo + first(o), 80), :]
            blocks.append(total)
        total = depth_t[0:1] * tail[pl.ds(first(0), 32), :]
        for o in range(1, KERNEL):
            total = total + depth_t[o : o + 1] * tail[pl.ds(first(o), 32), :]
        return join(jnp.concatenate(blocks, axis=0), unsegmented(total))

    depth_rows = pl.ds(ROW["depth_w"], KERNEL)
    depth_m = WM[depth_rows, :]
    depth_t = jnp.where(lane < TAIL, WT[depth_rows, :], 0.0)
    for shift in (TAIL, 2 * TAIL, 4 * TAIL):
        depth_t = depth_t + turned(depth_t, shift)
    CT[2 * EDGE + ROWS :, :] = jnp.zeros((CT.shape[0] - 2 * EDGE - ROWS, 128), F32)
    lay((live * value * gate).astype(BF16).astype(F32), GLM, GLT)
    forth = lambda o: EDGE - LEFT + o
    conv = convolved(GLM, GLT, forth)

    def begin_sum(which, first, second):
        lengths = jnp.where(tm == 0, lens[0] + lens[1], 0).astype(F32)
        blank = jnp.zeros((1, 128 - TAIL), F32)
        BS[which, 0] = jnp.concatenate(
            [
                first[:, :128],
                jnp.concatenate([first[:, 128:], blank], axis=1),
                second[:, :128],
                jnp.concatenate([second[:, 128:], blank], axis=1),
                jnp.full((4, 128), lengths),
            ],
            axis=0,
        )
        if fast:
            sent, at = [], slots(1)
            for k in range(31, 0, -1):
                kz, dy, dx, dc = k // 8, (k // 4) % 2, (k // 2) % 2, k % 2
                to_y, to_x, to_c = (1 - v if d else v for v, d in ((y, dy), (x, dx), (c, dc)))
                to = (2 * z_at[kz] + to_y, 2 * to_x + to_c)
                remote(BS.at[which, 0], BB.at[which, k - 1], at, at, to).start()
            sent.append(remote(BB.at[which], BB.at[which], at, at, core_peer))
            waits.extend(sent)
        else:
            sent = [
                send(BS.at[which, 0], BB.at[which, k], mate)
                for k, mate in enumerate((x_peer, cross_peer, core_peer))
            ]
        return sent

    def end_sum(which, sent):
        def arrived(copies, at, count, total):
            for made in copies:
                made.wait_recv()
            for k in range(count):
                total = total + BB[which, at + k]
            return total

        total = arrived(sent, 0, 31 if fast else 3, BS[which, 0])
        if not fast:
            BS[which, 1] = total
            sent = [
                send(BS.at[which, 1], BB.at[which, 2 + k], ((utt + k) % n_utt, tm))
                for k in range(1, n_utt)
            ]
            total = arrived(sent, 3, n_utt - 1, total)
        return join(total[0:1], total[1:2]), join(total[2:3], total[3:4]), total[4:5, 0:1]

    counted = own_row * live
    sent = begin_sum(0, colsum(counted * conv), colsum(counted * conv * conv))
    if fast:
        from_core(3)
    ready("second")
    flip = (
        lax.broadcasted_iota(jnp.int32, (ROWS, ROWS), 0)
        + lax.broadcasted_iota(jnp.int32, (ROWS, ROWS), 1)
        == ROWS - 1
    ).astype(F32).astype(BF16)
    qu_r = mm(flip, qu).astype(BF16)
    qv_r = mm(flip, qv).astype(BF16)
    def transposed(v):
        return v.astype(F32).T.astype(BF16)

    for h in range(HEADS):
        prob = PR[h]
        prob = prob * (1.0 / jnp.sum(prob, axis=1, keepdims=True))
        high = prob.astype(BF16)
        rest = (prob - high.astype(F32)).astype(BF16)
        turned_high = mm(flip, high)
        PB[h] = turned_high.astype(BF16)
        PR[h] = turned_high + mm(flip, rest)
    for source, target in ((qu_r, QUT), (qv_r, QVT)):
        v = source.astype(F32).T
        for h in range(HEADS):
            target[h] = v[HEAD_DIM * h : HEAD_DIM * (h + 1)].astype(BF16)
    for j in range(CHUNKS):
        XT[j] = transposed(ACT1[j, window, :])
    for j, v in enumerate((LOW1[window, :], a2, a3, context)):
        XT[CHUNKS + j] = transposed(v)
    first_sum, second_sum, count = end_sum(0, sent)
    mu = first_sum / count
    spread = lax.rsqrt(second_sum / count - mu * mu + EPS)
    bn = (conv - mu) * spread
    zed = bn * rows_of("batch_gain") + rows_of("batch_bias")
    zed_s = sigmoid(zed)
    swished = (zed * zed_s).astype(BF16)
    x3 = x2 + mm(swished, square("mix_w")) + rows_of("mix_b")

    total, second_n, second_i, second_low = feed(x3, "second", HID2, ACT2)
    x4 = x3 + 0.5 * total
    final_n, final_i = normed(x4)
    result = final_n * rows_of("final_gain") + rows_of("final_bias")

    def return_frames(v, S, B):
        send_at, recv_at = slots(2), slots(2)
        made = []
        for j in range(2):
            lo, hi = LOCAL * j, HALF - HALO_START + LOCAL * j
            S[j] = jnp.where(half == 0, v[lo : lo + LOCAL, :], v[hi : hi + LOCAL, :]).T
            made.append(
                remote(S.at[j], B.at[unit], send_at + j, recv_at + unit, (utt, 2 * half + j))
            )

        def launch():
            for j in range(2):
                away = 2 * half + j != tm

                @pl.when(away)
                def _(sent=made[j]):
                    sent.start()

                @pl.when(jnp.logical_not(away))
                def _(j=j):
                    B[unit] = S[j]

        def finish():
            for j in range(2):

                @pl.when(2 * half + j != tm)
                def _(sent=made[j]):
                    sent.wait_send()

            for u in range(2):

                @pl.when(2 * u + x != tm)
                def _(u=u):
                    remote(S.at[0], B.at[u], send_at, recv_at + u, core_peer).wait_recv()

        return launch, finish

    launch_out, finish_out = return_frames(result, OS, out)
    launch_out()

    unpack_frames(c_copies, CS, CB, CF)
    g0 = CF[window, :] * live
    d4 = norm_back(g0, rows_of("final_gain"), final_n, final_i)

    def feed_back(grad, prefix, hidden_of, active_t, scaled, inverse, low_t, masked):
        low_grad = (0.5 * grad).astype(BF16)
        back = jnp.zeros((ROWS, D), F32)
        hidden_grads = []
        for j in range(CHUNKS):
            hidden = hidden_of(j)
            s = sigmoid(hidden)
            grad_hidden = nt(low_grad, square(prefix + "_w_out", j * D))
            grad_hidden = (grad_hidden * s * (1.0 + hidden * (1.0 - s))).astype(BF16)
            hidden_grads.append(grad_hidden)
            back = back + nt(grad_hidden, square(prefix + "_w_in", j))

        def out_weights():
            kept = low_grad * own_low if masked else low_grad
            put(prefix + "_b_out", colsum(kept.astype(F32)))
            for j in range(CHUNKS):
                put(prefix + "_w_out", mm(active_t(j), kept), j * D)

        def in_weights():
            for j in range(CHUNKS):
                grad_hidden = hidden_grads[j] * own_low if masked else hidden_grads[j]
                put(prefix + "_w_in", mm(low_t(), grad_hidden), j, CHUNKS)
                put(prefix + "_b_in", colsum(grad_hidden.astype(F32)), j)
            kept = back * own_row if masked else back
            put(prefix + "_gain", colsum(kept * scaled))
            put(prefix + "_bias", colsum(kept))

        total = grad + norm_back(back, rows_of(prefix + "_gain"), scaled, inverse)
        return total, out_weights, in_weights

    d3, second_out_weights, second_in_weights = feed_back(
        d4,
        "second",
        lambda j: HID2[j],
        lambda j: transposed(ACT2[j]),
        second_n,
        second_i,
        lambda: transposed(second_low),
        True,
    )

    if fast:
        z_send, z_recv = slots(4), slots(4)
        stage, used_by = {}, {}

        def add(a, b):
            return a.astype(F32) + b.astype(F32)

        def begin_round(goal, ys=(0, 1)):
            for yy in ys:
                for xc in range(4):
                    first = 110 * (8 * goal + 4 * yy + xc)
                    block = LB.at[goal, yy, xc // 2, xc % 2]
                    block[0:MAIN, :] = GM[first : first + MAIN, :].astype(BF16)
                    block[MAIN:BLOCK, :] = tails_of(GT[first : first + MAIN, :]).astype(BF16)
            rows = pl.ds(ys[0], len(ys))
            stage[goal, ys] = send(LB.at[goal, rows, :, 1 - c], R1.at[goal, rows], core_peer)

        def plane_round(goal, ys=(0, 1)):
            stage[goal, ys].wait_recv()
            for yy in ys:
                for xx in range(2):
                    ACC[goal, yy, xx] = add(LB[goal, yy, xx, c], R1[goal, yy, xx]).astype(BF16)
            at = slots(1)
            made = []
            for m in range(3):
                block = ACC.at[goal, plane_at[m][0], plane_at[m][1]]
                made.append(remote(block, R2.at[goal, m], at, at, plane[m]))
            all_three = remote(R2.at[goal], R2.at[goal], at, at, core_peer)
            stage[goal, ys] = all_three
            used_by[goal, ys] = at
            if len(ys) == 2:
                for one in made:
                    one.start()
                waits.append(all_three)
            else:

                @pl.when(y == ys[0])
                def _():
                    made[0].start()

                @pl.when(y != ys[0])
                def _():
                    made[1].start()
                    made[2].start()

        def z_copy(goal, sender):
            return remote(
                R3.at[goal], RZ.at[sender], z_send + goal, z_recv + sender, (2 * goal + y, tm)
            )

        def z_round(goal, ys=(0, 1)):
            def step():
                stage[goal, ys].wait_recv()
                total = add(ACC[goal, y, x], R2[goal, 0]) + add(R2[goal, 1], R2[goal, 2])
                R3[goal] = total.astype(BF16)

                @pl.when(z != goal)
                def _():
                    z_copy(goal, z).start()

            if len(ys) == 2:
                step()
                return
            pl.when(y == ys[0])(step)

        def drain(goal, ys):
            at = used_by[goal, ys]

            @pl.when(y == ys[0])
            def _():
                remote(R2.at[goal, 0], R2.at[goal, 0], at, at, core_peer).wait_send()

            @pl.when(y != ys[0])
            def _():
                remote(R2.at[goal, 0:2], R2.at[goal, 0:2], at, at, core_peer).wait_send()

    else:
        begin_round = plane_round = z_round = lambda goal, ys=(0, 1): None

    low_grad = d3.astype(BF16)
    dzed = nt(low_grad, square("mix_w")).astype(BF16).astype(F32)
    dzed = dzed * zed_s * (1.0 + zed * (1.0 - zed_s))
    e = dzed * rows_of("batch_gain")
    e_own = e * counted
    sent = begin_sum(1, colsum(e_own), colsum(e_own * bn))
    GM[USED:, :] = jnp.zeros((PADDED - USED, 128), F32)
    GT[USED:, :] = jnp.zeros((PADDED - USED, 128), F32)
    g0_own = g0 * own_row
    put("final_gain", colsum(g0_own * final_n))
    put("final_bias", colsum(g0_own))
    second_out_weights()
    second_in_weights()
    begin_round(3)
    kept = low_grad * own_low
    put("mix_w", tn(swished, kept))
    put("mix_b", colsum(kept.astype(F32)))
    dzed_own = dzed * own_row
    put("batch_gain", colsum(dzed_own * bn))
    put("batch_bias", colsum(dzed_own))
    parts = (e, jnp.broadcast_to(live, (ROWS, D)), live * bn)
    back_parts, depth_parts = [], []
    for i, v in enumerate(parts):
        lay(v, VM, VT)
        back_parts.append(convolved(VM, VT, lambda o: EDGE + LEFT - o))
        kept = v * own_row
        kept_m = kept[:, :128]
        CT[0:ROWS, 0:TAIL] = kept[:, 128:]
        segment_row = lax.broadcasted_iota(jnp.int32, (32, 1), 0) < SEGMENT
        kept_t = jnp.where(segment_row, segments(CT, 32), 0.0)
        mains, tails = [], []
        for o in range(KERNEL):
            mains.append(colsum(kept_m * GLM[pl.ds(forth(o), ROWS), :]))
            tails.append(colsum(kept_t * GLT[pl.ds(forth(o), 32), :]))
        tails = jnp.concatenate(tails, axis=0)
        for shift in (4 * TAIL, 2 * TAIL, TAIL):
            tails = tails + turned(tails, shift)
        depth_parts.append(join(jnp.concatenate(mains, axis=0), tails))
    first_sum, second_sum, count = end_sum(1, sent)
    plane_round(3)
    first_mean, second_mean = first_sum / count, second_sum / count

    def combined(v):
        return spread * (v[0] - v[1] * first_mean - v[2] * second_mean)

    put("depth_w", combined(depth_parts))
    dglu = combined(back_parts).astype(BF16).astype(F32) * counted
    dvalue = (dglu * gate).astype(BF16)
    dgate = (dglu * value * gate * (1.0 - gate)).astype(BF16)
    put("point_w", mm(XT[CHUNKS + 2], dvalue), 0, 2)
    put("point_w", mm(XT[CHUNKS + 2], dgate), 1, 2)
    put("point_b", colsum(dvalue.astype(F32)), 0)
    put("point_b", colsum(dgate.astype(F32)), 1)
    back = nt(dvalue, square("point_w", 0)) + nt(dgate, square("point_w", 1))
    put("conv_gain", colsum(back * conv_n))
    put("conv_bias", colsum(back))
    d2 = d3 * own_row + norm_back(back, rows_of("conv_gain"), conv_n, conv_i)

    low_grad = d2.astype(BF16)
    put("proj_w", mm(XT[CHUNKS + 3], low_grad))
    put("proj_b", colsum(low_grad.astype(F32)))
    begin_round(2)
    dctx = nt(low_grad, square("proj_w")).astype(BF16)
    dctx = mm(flip, dctx)
    dctx_t = dctx.T
    dctx = dctx.astype(BF16)
    du, dw = jnp.zeros((ROWS, D), F32), jnp.zeros((ROWS, D), F32)
    for h in range(HEADS):
        mask = head_mask(h)
        head = slice(HEAD_DIM * h, HEAD_DIM * (h + 1))
        prob = PR[h]
        dprob = nt(dctx * mask, VAL[...])
        dscore = prob * (dprob - jnp.sum(dprob * prob, axis=1, keepdims=True))
        low_score = dscore.astype(BF16)
        dwide = jnp.concatenate([dscore, jnp.zeros((ROWS, WIDE - LEN), F32)], axis=1)
        dwide = pltpu.roll(dwide, 0, 1, stride=1, stride_axis=0).astype(BF16)
        DVT[head, :] = mm(dctx_t[head].astype(BF16), PB[h])
        DKT[head, :] = mm(QUT[h], low_score)
        DPT[head, :] = mm(QVT[h], dwide)
        du = du + mm(low_score, KEY[...] * mask)
        dw = dw + mm(dwide, positions * mask)
        if h == 2:
            plane_round(2)
    DKA[...] = DKT[...].T
    DVA[...] = DVT[...].T
    theirs = pl.ds(pl.multiple_of(HALO_START * (1 - half), 16), ROWS)
    KS[0] = DKA[theirs, :].astype(BF16)
    KS[1] = DVA[theirs, :].astype(BF16)
    kv_copy = send(KS, KB, core_peer)
    z_round(3)
    put("content_bias", scale * colsum(du))
    put("position_bias", scale * colsum(dw))
    dquery = mm(flip, (scale * (du + dw)).astype(BF16)).astype(BF16)
    dpos = DPT[...]
    high = dpos.astype(BF16)
    rest = (dpos - high.astype(F32)).astype(BF16)
    put("pos_w", (mm(high, TB[...]) + mm(rest, TB[...])).T)
    put("query_w", mm(XT[CHUNKS + 1], dquery))
    put("query_b", colsum(dquery.astype(F32)))
    kv_copy.wait_recv()
    dkey = ((DKA[window, :] + KB[0].astype(F32)) * own_row).astype(BF16)
    dval = ((DVA[window, :] + KB[1].astype(F32)) * own_row).astype(BF16)
    put("key_w", mm(XT[CHUNKS + 1], dkey))
    put("value_w", mm(XT[CHUNKS + 1], dval))
    put("value_b", colsum(dval.astype(F32)))
    begin_round(1, (1,))
    back = (
        nt(dquery, square("query_w"))
        + nt(dkey, square("key_w"))
        + nt(dval, square("value_w"))
    )
    scaled, inverse = normed(X1[window, :])
    put("att_gain", colsum(back * scaled))
    put("att_bias", colsum(back))
    d1 = d2 + norm_back(back, rows_of("att_gain"), scaled, inverse)

    d0, first_out_weights, first_in_weights = feed_back(
        d1,
        "first",
        lambda j: HID1[j, window, :],
        lambda j: XT[j],
        NRM1[window, :],
        INV1[window, :],
        lambda: XT[CHUNKS],
        False,
    )
    first_out_weights()
    plane_round(1, (1,))
    begin_round(1, (0,))
    first_in_weights()
    begin_round(0)
    plane_round(1, (0,))
    launch_grad, finish_grad = return_frames(d0, IS, grad_out)
    plane_round(0)
    launch_grad()
    z_round(2)
    z_round(1, (1,))
    z_round(1, (0,))
    z_round(0)

    if fast:
        drain(1, (0,))
        drain(1, (1,))
        for goal in range(4):

            @pl.when(z != goal)
            def _(goal=goal):
                z_copy(goal, z).wait_send()

        total = R3[z].astype(F32)
        for j in range(3):
            remote(
                R3.at[0], RZ.at[other_z[j]], 0, z_recv + other_z[j], core_peer
            ).wait_recv()
            total = total + RZ[other_z[j]].astype(F32)
        WM[0:MAIN, :] = total[0:MAIN]
        GT[0:MAIN, :] = rows_of_tails(total[MAIN:BLOCK])
        mains = [WM[pl.ds(i, 14, stride=8), :] for i in range(8)]
        tails = [GT[pl.ds(i, 14, stride=8), :] for i in range(8)]
        for i in range(9):
            row_i = turned(tails[max(i - 1, 0)], TAIL * (i - 1))
            if i < 8:
                row_i = jnp.where(lane >= TAIL * i, turned(mains[i], TAIL * i), row_i)
            if i > 0:
                v = turned(mains[i - 1], TAIL * (i - 1))
                row_i = jnp.where(lane < TAIL * (i - 1), v, row_i)
            WT[pl.ds(i, 14, stride=9), :] = row_i
        for i in range(15):
            flat_out[pl.ds(1024 * i, 1024)] = WT[8 * i : 8 * i + 8, :].reshape(1024)
        rest = LOCAL_SIZE - 15 * 1024
        flat_out[pl.ds(15 * 1024, rest)] = WT[120:128, :].reshape(1024)[0:rest]

    finish_out()
    finish_grad()
    for made in waits:
        made.wait_send()


def hand_over(first, second, third, first_out, second_out, third_out):
    first_out[...] = first[...]
    second_out[...] = second[...]
    third_out[...] = third[...]


def local(inputs, flat_params, lengths, cotangent):
    n_utt, n_tm = lax.axis_size("utt"), lax.axis_size("tm")
    size = flat_params.shape[0]
    fast = n_utt == 8 and n_tm == 4 and size == LOCAL_SIZE
    table = jnp.asarray(reversed_tables())
    turned = jax.ShapeDtypeStruct((2, D, LOCAL), F32)
    padded = jax.ShapeDtypeStruct((PADDED, 128), F32)
    vmem = pltpu.VMEM
    in_vmem = pl.BlockSpec(memory_space=pltpu.VMEM)
    anywhere = pl.BlockSpec(memory_space=pl.ANY)
    if fast:
        operands = [flat_params]
        results = [turned, turned, jax.ShapeDtypeStruct((size,), F32)]
        scratch = [vmem((PADDED, 128), F32)] * 4 + [
            vmem((size,), F32),
            vmem((4, 2, 2, 2, BLOCK, 128), BF16),
            vmem((4, 2, 2, 2, BLOCK, 128), BF16),
            vmem((4, 2, 2, BLOCK, 128), BF16),
            vmem((4, 3, BLOCK, 128), BF16),
            vmem((4, BLOCK, 128), BF16),
            vmem((4, BLOCK, 128), BF16),
            vmem((4, 2, 2, BLOCK, 128), BF16),
        ]
    else:
        rows = lax.all_gather(flat_params, ("utt", "tm"), axis=0, tiled=True).reshape(TOTAL, D)
        operands = [
            jnp.pad(rows[:, :128], ((0, PADDED - TOTAL), (0, 0))),
            jnp.pad(rows[:, 128:], ((0, PADDED - TOTAL), (0, 128 - TAIL))),
        ]
        results = [turned, turned, padded, padded]
        scratch = []
    others = 31 if fast else 3 + n_utt - 1
    copies = 128 + 2 * others
    scratch = scratch + [
        vmem((2, D, LOCAL), BF16),
        vmem((2, D, LOCAL), BF16),
        vmem((4, D, LOCAL), BF16),
        vmem((4, D, LOCAL), BF16),
        vmem((WIDE, D), BF16),
        vmem((LEN, D), F32),
        vmem((LEN, D), F32),
        vmem((2, D, LOCAL), F32),
        vmem((2, D, LOCAL), F32),
        vmem((len(SQUARES), D, D), BF16),
        vmem((CHUNKS, LEN, D), F32),
        vmem((CHUNKS, LEN, D), BF16),
        vmem((LEN, D), F32),
        vmem((LEN, 1), F32),
        vmem((LEN, D), BF16),
        vmem((LEN, D), F32),
        vmem((LEN, D), BF16),
        vmem((CHUNKS, ROWS, D), F32),
        vmem((CHUNKS, ROWS, D), BF16),
        vmem((LEN, D), BF16),
        vmem((LEN, D), BF16),
        vmem((HEADS, ROWS, LEN), F32),
        vmem((HEADS, ROWS, LEN), BF16),
        vmem((HEADS, HEAD_DIM, ROWS), BF16),
        vmem((HEADS, HEAD_DIM, ROWS), BF16),
        vmem((CHUNKS + 4, D, ROWS), BF16),
        vmem((D, LEN), F32),
        vmem((D, LEN), F32),
        vmem((D, WIDE), F32),
        vmem((LEN, D), F32),
        vmem((LEN, D), F32),
        vmem((ROWS + 2 * EDGE, 128), F32),
        vmem((64, 128), F32),
        vmem((ROWS + 2 * EDGE, 128), F32),
        vmem((64, 128), F32),
        vmem((288, 128), F32),
        vmem((2, ROWS, D), BF16),
        vmem((2, ROWS, D), BF16),
        vmem((2, 2, 8, 128), F32),
        vmem((2, others, 8, 128), F32),
        pltpu.SMEM((2,), jnp.int32),
        pltpu.SemaphoreType.DMA((copies,)),
        pltpu.SemaphoreType.DMA((copies,)),
        pltpu.SemaphoreType.DMA((5,)),
    ]
    got = pl.pallas_call(
        functools.partial(kernel, n_utt, fast),
        out_shape=results,
        in_specs=[anywhere] * 4
        + [anywhere if fast else in_vmem] * len(operands),
        out_specs=[in_vmem] * len(results),
        scratch_shapes=scratch,
        compiler_params=pltpu.CompilerParams(
            collective_id=0, has_side_effects=True, vmem_limit_bytes=56 * 1024 * 1024
        ),
    )(lengths, jnp.swapaxes(inputs, 1, 2), jnp.swapaxes(cotangent, 1, 2), table, *operands)
    if fast:
        out, grad, grad_params = pl.pallas_call(
            hand_over,
            out_shape=results,
            in_specs=[in_vmem] * 3,
            out_specs=[in_vmem] * 3,
        )(*got)
    else:
        out, grad = got[:2]
        rows = jnp.concatenate([got[2][:TOTAL], got[3][:TOTAL, :TAIL]], axis=1)
        grad_params = lax.psum_scatter(
            rows.reshape(-1), ("utt", "tm"), scatter_dimension=0, tiled=True
        )
    return jnp.swapaxes(out, 1, 2), jnp.swapaxes(grad, 1, 2), grad_params


def solution(mesh):
    return jax.shard_map(
        local,
        mesh=mesh,
        in_specs=(P("utt", "tm", None), P(("utt", "tm")), P("utt"), P("utt", "tm", None)),
        out_specs=(P("utt", "tm", None), P("utt", "tm", None), P(("utt", "tm"))),
        check_vma=False,
    )
```

```python
import functools
import math

import jax
import jax.numpy as jnp
import ml_dtypes
import numpy as np
from jax import lax
from jax.experimental import pallas as pl
from jax.experimental.pallas import tpu as pltpu
from jax.sharding import PartitionSpec as P

D = 144
HEADS = 4
FF = 576
KERNEL = 32
HEAD_DIM = 36
LEN = 400
EPS = 1e-05
NEGATIVE = -1e30

CHUNKS = FF // D
LEFT = (KERNEL - 1) // 2
LOCAL = 100
HALF = 200
ROWS = 240
HALO_START = LEN - ROWS
WIDE = 640
STRIP = 48
EDGE = 16
TAIL = D - 128
BLOCK = 128
MAIN = 112
LOCAL_SIZE = 110 * D

F32 = jnp.float32
BF16 = jnp.bfloat16
MESH = pl.DeviceIdType.MESH


def param_rows():
    def feed(prefix):
        return [
            (prefix + "_gain", 1),
            (prefix + "_bias", 1),
            (prefix + "_w_in", D * CHUNKS),
            (prefix + "_b_in", CHUNKS),
            (prefix + "_w_out", FF),
            (prefix + "_b_out", 1),
        ]

    middle = [
        ("att_gain", 1),
        ("att_bias", 1),
        ("query_w", D),
        ("query_b", 1),
        ("key_w", D),
        ("value_w", D),
        ("value_b", 1),
        ("pos_w", D),
        ("content_bias", 1),
        ("position_bias", 1),
        ("proj_w", D),
        ("proj_b", 1),
        ("conv_gain", 1),
        ("conv_bias", 1),
        ("point_w", 2 * D),
        ("point_b", 2),
        ("depth_w", KERNEL),
        ("batch_gain", 1),
        ("batch_bias", 1),
        ("mix_w", D),
        ("mix_b", 1),
    ]
    entries = feed("first") + middle + feed("second") + [("final_gain", 1), ("final_bias", 1)]
    rows = {}
    position = 0
    for name, count in entries:
        rows[name] = position
        position += count
    return rows, position


ROW, USED = param_rows()
TOTAL = 3520
PADDED = TOTAL + 8
SQUARES = (
    [("first_w_in", c, CHUNKS) for c in range(CHUNKS)]
    + [("first_w_out", c * D, 1) for c in range(CHUNKS)]
    + [("second_w_in", c, CHUNKS) for c in range(CHUNKS)]
    + [("second_w_out", c * D, 1) for c in range(CHUNKS)]
    + [("query_w", 0, 1), ("key_w", 0, 1), ("value_w", 0, 1), ("pos_w", 0, 1), ("proj_w", 0, 1)]
    + [("point_w", 0, 2), ("point_w", 1, 2), ("mix_w", 0, 1)]
)
SQUARE = {(name, shift): i for i, (name, shift, unused) in enumerate(SQUARES)}


def reversed_tables():
    distance = np.arange(2 * LEN - 1, dtype=np.float32) - np.float32(LEN - 1)
    steps = np.arange(D // 2, dtype=np.float32)
    frequency = np.exp(np.float32(-math.log(10000.0)) * steps * np.float32(2.0) / np.float32(D))
    angles = (distance[:, None] * frequency[None, :].astype(np.float32)).astype(np.float32)
    table = np.concatenate([np.sin(angles), np.cos(angles)], axis=1).astype(ml_dtypes.bfloat16)
    both = np.zeros((2, WIDE, D), ml_dtypes.bfloat16)
    for half in range(2):
        top = HALO_START * half + ROWS - 1 + LEN - 1
        both[half, : ROWS + LEN - 1] = table[top - (ROWS + LEN - 1) + 1 : top + 1][::-1]
    return both


def mm(a, b):
    return jnp.dot(a, b, preferred_element_type=F32)


def nt(a, b):
    return lax.dot_general(a, b, (((1,), (1,)), ((), ())), preferred_element_type=F32)


def tn(a, b):
    return lax.dot_general(a, b, (((0,), (0,)), ((), ())), preferred_element_type=F32)


def sigmoid(v):
    return 0.5 * jnp.tanh(0.5 * v) + 0.5


def silu(v):
    s = sigmoid(v)
    active = v * s
    return active, s + s * (v - active)


def mean(v):
    return jnp.sum(v, axis=1, keepdims=True) * (1.0 / D)


def normed(v):
    centered = v - mean(v)
    inverse = lax.rsqrt(mean(centered * centered) + EPS)
    return centered * inverse, inverse


def norm_back(grad, gain, scaled, inverse):
    e = grad * gain
    return inverse * (e - mean(e) - scaled * mean(e * scaled))


def colsum(v):
    return jnp.sum(v, axis=0, keepdims=True)


def join(main, tail):
    return jnp.concatenate([main, tail[:, :TAIL]], axis=1)


def kernel(n_utt, fast, lens_in, x_in, cot_in, tab, *refs):
    refs = list(refs)
    take = lambda count: [refs.pop(0) for unused in range(count)]
    if fast:
        (flat_in,) = take(1)
        out, grad_out, flat_out = take(3)
        WM, WT, GM, GT = take(4)
        (FLAT, GB, LB, R1, R2, R3, RZ, ACC) = take(8)
    else:
        WM, WT = take(2)
        out, grad_out, GM, GT = take(4)
    (XS, CS, XB, CB, TB, XF, CF, OS, IS, WS) = take(10)
    (HID1, ACT1, NRM1, INV1, LOW1, X1, A2, HID2, ACT2) = take(9)
    (KEY, VAL, PR, PD, WD, WB, LS, PB, QUT, QVT, XT, DKT, DVT, DPT, DKA, DVA, GLM, GLT, VM, VT, CT) = take(21)
    (KS, KB, BS, BB, lens, send_sem, recv_sem, local_sem) = take(8)

    utt = lax.axis_index("utt")
    tm = lax.axis_index("tm")
    x, c = tm // 2, tm % 2
    z, y = utt // 2, utt % 2
    unit, half = x, c
    start = pl.multiple_of(HALO_START * half, 16)

    used = [0]
    waits = []

    def slots(count):
        at = used[0]
        used[0] += count
        return at

    def remote(src, dst, send_at, recv_at, device):
        return pltpu.make_async_remote_copy(
            src_ref=src,
            dst_ref=dst,
            send_sem=send_sem.at[send_at],
            recv_sem=recv_sem.at[recv_at],
            device_id=device,
            device_id_type=MESH,
        )

    def send(src, dst, device, send_at=None, recv_at=None):
        if send_at is None:
            send_at = recv_at = slots(1)
        made = remote(src, dst, send_at, recv_at, device)
        made.start()
        waits.append(made)
        return made

    core_peer = (utt, 2 * x + 1 - c)
    x_peer = (utt, 2 * (1 - x) + c)
    cross_peer = (utt, 2 * (1 - x) + 1 - c)
    y_peer = (2 * z + 1 - y, tm)
    xy_peer = (2 * z + 1 - y, 2 * (1 - x) + c)
    plane = [x_peer, y_peer, xy_peer]
    plane_at = [(y, 1 - x), (1 - y, x), (1 - y, 1 - x)]
    z_at = [z, z + 1 - 2 * (z % 2), (z + 2) % 4, 3 - z]
    other_z = [j + (j - z + 4) // 4 for j in range(3)]

    barrier = pltpu.get_barrier_semaphore()
    partners = [core_peer, x_peer, cross_peer]
    if fast:
        partners += [(2 * zz + y, tm) for zz in other_z] + [y_peer, xy_peer]
    else:
        partners += [((utt + k) % n_utt, tm) for k in range(1, n_utt)]
    for partner in partners:
        pl.semaphore_signal(barrier, inc=1, device_id=partner, device_id_type=MESH)
    fetches = [
        pltpu.make_async_copy(x_in, XS, local_sem.at[0]),
        pltpu.make_async_copy(cot_in, CS, local_sem.at[1]),
        pltpu.make_async_copy(tab.at[half], TB, local_sem.at[2]),
        pltpu.make_async_copy(lens_in, lens, local_sem.at[4]),
    ]
    if fast:
        flat_fetch = pltpu.make_async_copy(flat_in, FLAT, local_sem.at[3])
        flat_fetch.start()
    for fetch in fetches:
        fetch.start()

    lane = lax.broadcasted_iota(jnp.int32, (1, 128), 1)
    lane_d = lax.broadcasted_iota(jnp.int32, (1, D), 1)

    def lanes_of(g):
        return (lane >= TAIL * g) & (lane < TAIL * (g + 1))

    def turned(v, shift):
        return v if shift % 128 == 0 else pltpu.roll(v, shift % 128, 1)

    def tails_of(rows):
        packed = jnp.zeros((16, 128), F32)
        for g in range(7):
            packed = jnp.where(lanes_of(g), turned(rows[16 * g : 16 * g + 16], TAIL * g), packed)
        return packed

    def rows_of_tails(packed):
        return jnp.concatenate([turned(packed, -TAIL * g) for g in range(7)], axis=0)

    if fast:
        own = GB.at[z, y, x, c]
        flat_fetch.wait()
        for i in range(15):
            GM[8 * i : 8 * i + 8, :] = FLAT[pl.ds(1024 * i, 1024)].reshape(8, 128)
        rest = LOCAL_SIZE - 15 * 1024
        GM[120:128, :] = jnp.concatenate(
            [FLAT[pl.ds(15 * 1024, rest)], jnp.zeros((1024 - rest,), F32)]
        ).reshape(8, 128)
        dense = [GM[pl.ds(i, 14, stride=9), :] for i in range(9)]
        for i in range(8):
            shift = TAIL * i
            left = turned(dense[i], -shift)
            right = turned(dense[i + 1], -shift)
            WM[pl.ds(i, 14, stride=8), :] = jnp.where(lane < 128 - shift, left, right)
            WT[pl.ds(i, 14, stride=8), :] = right
        own[0:MAIN, :] = WM[0:MAIN, :].astype(BF16)
        own[MAIN:BLOCK, :] = tails_of(WT[0:MAIN, :]).astype(BF16)
        col_at, p_at, c_at = slots(4), slots(12), slots(4)

        def to_column(j):
            to = (2 * z_at[3 - j] + y, tm)
            remote(own, own, col_at, col_at + z, to).start()

        def to_plane(zz, mates):
            block = GB.at[zz, y, x, c]
            for m in range(mates):
                remote(block, block, p_at, p_at + 4 * m + zz, plane[m]).start()

        def diagonal_to_column():
            block = GB.at[z, 1 - y, 1 - x, c]
            remote(block, block, p_at, p_at + 8 + z, core_peer).wait_recv()
            for j in range(3):
                to = (2 * z_at[3 - j] + y, tm)
                remote(block, block, p_at, p_at + 8 + z, to).start()
            to_core(z, (1 - y, 1 - x))

        def from_plane(zz, mates):
            for m in range(mates):
                block = GB.at[zz, plane_at[m][0], plane_at[m][1], c]
                remote(block, block, p_at, p_at + 4 * m + zz, core_peer).wait_recv()
                to_core(zz, plane_at[m])

        def diagonal_from_column(zz):
            @pl.when(z != zz)
            def _():
                block = GB.at[zz, 1 - y, 1 - x, c]
                remote(block, block, p_at, p_at + 8 + zz, core_peer).wait_recv()
                to_core(zz, (1 - y, 1 - x))

        def to_core(zz, where):
            block = GB.at[zz, where[0], where[1], c]
            remote(block, block, c_at, c_at + zz, core_peer).start()

        waits.append(remote(R2.at[0], R2.at[0], col_at, col_at, core_peer))
        waits.append(remote(R2, R2, p_at, p_at, core_peer))
        waits.append(remote(GB.at[0:2], GB.at[0:2], c_at, c_at, core_peer))

        def from_core(zz):
            blocks = GB.at[zz, :, :, 1 - c]
            remote(blocks, blocks, c_at, c_at + zz, core_peer).wait_recv()
            for low_d in range(8):
                block = GB.at[zz, low_d // 4, (low_d // 2) % 2, low_d % 2]
                first = 110 * (8 * zz + low_d)
                WM[first : first + 110, :] = block[0:110, :].astype(F32)
                WT[first : first + 110, :] = rows_of_tails(block[MAIN:BLOCK, :].astype(F32))[0:110]

    pl.semaphore_wait(barrier, len(partners))
    if fast:
        for j in range(3):
            to_column(j)

    def exchange(source, target):
        return (
            send(source.at[1 - x], target.at[tm], x_peer),
            send(source.at[x], target.at[tm], core_peer),
        )

    def relay(copies, target):
        copies[0].wait_recv()
        passed = target.at[x_peer[1]]
        return copies[1], send(passed, passed, core_peer)

    def unpack_frames(copies, source, target, frames):
        for made in copies:
            made.wait_recv()
        target[tm] = source[unit]
        for k in range(4):
            frames[LOCAL * k : LOCAL * (k + 1), :] = target[k].astype(F32).T

    fetches[0].wait()
    x_copies = exchange(XS, XB)
    if fast:
        to_plane(z, 3)
        to_core(z, (y, x))
    x_copies = relay(x_copies, XB)
    if fast:
        diagonal_to_column()
        for j in range(3):
            block = GB.at[other_z[j], y, x, c]
            remote(block, block, col_at, col_at + other_z[j], core_peer).wait_recv()
            to_plane(other_z[j], 2)
            to_core(other_z[j], (y, x))
    fetches[1].wait()
    c_copies = exchange(CS, CB)

    def rows_of(name, count=1, shift=0, stride=1):
        at = ROW[name] + shift
        s = pl.ds(at, count) if stride == 1 else pl.ds(at, count, stride=stride)
        return join(WM[s, :], WT[s, :])

    def put(name, value, shift=0, stride=1):
        at = ROW[name] + shift
        count = value.shape[0]
        if stride == 1:
            GM[pl.ds(at, count), :] = value[:, :128]
            GT[pl.ds(at, count), 0:TAIL] = value[:, 128:]
        else:
            s = pl.ds(at, count, stride=stride)
            GM[s, :] = value[:, :128]
            GT[s, :] = jnp.concatenate(
                [value[:, 128:], jnp.zeros((count, 128 - TAIL), F32)], axis=1
            )

    def ready(prefixes):
        for i, (name, shift, stride) in enumerate(SQUARES):
            if name.startswith(prefixes):
                WS[i] = rows_of(name, D, shift, stride).astype(BF16)

    def square(name, shift=0):
        return WS[SQUARE[name, shift]]

    row = lax.broadcasted_iota(jnp.int32, (ROWS, 1), 0)
    frame = row + start
    own_row = ((frame >= HALF * half) & (frame < HALF * half + HALF)).astype(F32)
    own_low = own_row.astype(BF16)
    fetches[3].wait()
    length = jnp.where(unit == 0, lens[0], lens[1])
    live = (frame < length).astype(F32)
    scale = HEAD_DIM ** (-0.5)
    window = pl.ds(start, ROWS)

    if fast:
        from_plane(0, 2)
        diagonal_from_column(0)
        from_plane(1, 2)
        diagonal_from_column(1)
        from_core(0)
        from_core(1)
    unpack_frames(x_copies, XS, XB, XF)
    ready("first")
    c_copies = relay(c_copies, CB)

    def feed(v, prefix, HID, ACT):
        scaled, inverse = normed(v)
        low = (scaled * rows_of(prefix + "_gain") + rows_of(prefix + "_bias")).astype(BF16)
        total = rows_of(prefix + "_b_out")
        for j in range(CHUNKS):
            hidden = mm(low, square(prefix + "_w_in", j)) + rows_of(prefix + "_b_in", 1, j)
            if prefix == "first":
                HID[j] = hidden
                active = hidden * sigmoid(hidden)
            else:
                active, HID[j] = silu(hidden)
            active = active.astype(BF16)
            ACT[j] = active
            total = total + mm(active, square(prefix + "_w_out", j * D))
        return total, scaled, inverse, low

    v = XF[...]
    total, scaled, inverse, low = feed(v, "first", HID1, ACT1)
    NRM1[...] = scaled
    INV1[...] = inverse
    LOW1[...] = low
    x1 = v + 0.5 * total
    X1[...] = x1

    if fast:
        for zz in (2, 3):
            from_plane(zz, 2)
            diagonal_from_column(zz)
        from_core(2)
    ready(("query", "key", "value", "pos_w", "proj", "point", "mix"))
    fetches[2].wait()
    scaled, inverse = normed(x1)
    low = (scaled * rows_of("att_gain") + rows_of("att_bias")).astype(BF16)
    A2[...] = low
    KEY[...] = mm(low, square("key_w")).astype(BF16)
    VAL[...] = (mm(low, square("value_w")) + rows_of("value_b")).astype(BF16)
    a2 = A2[window, :]
    query = mm(a2, square("query_w")) + rows_of("query_b")
    qu = ((query + rows_of("content_bias")) * scale).astype(BF16)
    qv = ((query + rows_of("position_bias")) * scale).astype(BF16)
    positions = mm(TB[...], square("pos_w")).astype(BF16)
    key_bias = jnp.where(
        lax.broadcasted_iota(jnp.int32, (1, LEN), 1) < length, 0.0, NEGATIVE
    )

    def head_mask(h):
        return ((lane_d >= HEAD_DIM * h) & (lane_d < HEAD_DIM * (h + 1))).astype(BF16)

    for h in range(HEADS):
        mask = head_mask(h)
        PR[h] = nt(qu * mask, KEY[...])
        WD[h] = nt(qv * mask, positions)
    context, share = jnp.zeros((ROWS, D), F32), jnp.zeros((ROWS, D), F32)
    for h in range(HEADS):
        for lo in range(0, ROWS, STRIP):
            strip = slice(lo, lo + STRIP)
            wide = pltpu.roll(WD[h, strip, :], WIDE - ROWS + 1 + lo, 1, stride=1, stride_axis=0)
            score = PR[h, strip, :] + wide[:, :LEN] + key_bias
            score = jnp.exp(score - jnp.max(score, axis=1, keepdims=True))
            PR[h, strip, :] = score
            PB[h, strip, :] = score.astype(BF16)
        mask = head_mask(h)
        context = context + mm(PB[h], VAL[...] * mask)
        share = share + mm(PB[h], jnp.broadcast_to(mask, (LEN, D)))
    context = (context / share).astype(BF16)
    x2 = X1[window, :] + mm(context, square("proj_w")) + rows_of("proj_b")

    conv_n, conv_i = normed(x2)
    a3 = (conv_n * rows_of("conv_gain") + rows_of("conv_bias")).astype(BF16)
    value = mm(a3, square("point_w", 0)) + rows_of("point_b", 1, 0)
    gate = sigmoid(mm(a3, square("point_w", 1)) + rows_of("point_b", 1, 1))
    SEGMENT = ROWS // 8

    def segments(ref, count):
        packed = turned(ref[0:count, :], 0)
        for g in range(1, 8):
            v = turned(ref[SEGMENT * g : SEGMENT * g + count, :], TAIL * g)
            packed = jnp.where(lane >= TAIL * g, v, packed)
        return packed

    def unsegmented(v):
        for g in range(8):
            CT[SEGMENT * g : SEGMENT * (g + 1), :] = turned(v, -TAIL * g)[0:SEGMENT]
        return CT[0:ROWS, :]

    def lay(v, main, tail):
        for lo, hi in ((0, EDGE), (EDGE + ROWS, 2 * EDGE + ROWS)):
            main[lo:hi, :] = jnp.zeros((hi - lo, 128), F32)
            CT[lo:hi, :] = jnp.zeros((hi - lo, 128), F32)
        main[EDGE : EDGE + ROWS, :] = v[:, :128]
        CT[EDGE : EDGE + ROWS, 0:TAIL] = v[:, 128:]
        tail[...] = segments(CT, 64)

    def convolved(main, tail, first):
        blocks = []
        for lo in range(0, ROWS, 80):
            total = depth_m[0:1] * main[pl.ds(lo + first(0), 80), :]
            for o in range(1, KERNEL):
                total = total + depth_m[o : o + 1] * main[pl.ds(lo + first(o), 80), :]
            blocks.append(total)
        total = depth_t[0:1] * tail[pl.ds(first(0), 32), :]
        for o in range(1, KERNEL):
            total = total + depth_t[o : o + 1] * tail[pl.ds(first(o), 32), :]
        return join(jnp.concatenate(blocks, axis=0), unsegmented(total))

    depth_rows = pl.ds(ROW["depth_w"], KERNEL)
    depth_m = WM[depth_rows, :]
    depth_t = jnp.where(lane < TAIL, WT[depth_rows, :], 0.0)
    for shift in (TAIL, 2 * TAIL, 4 * TAIL):
        depth_t = depth_t + turned(depth_t, shift)
    CT[2 * EDGE + ROWS :, :] = jnp.zeros((CT.shape[0] - 2 * EDGE - ROWS, 128), F32)
    lay((live * value * gate).astype(BF16).astype(F32), GLM, GLT)
    forth = lambda o: EDGE - LEFT + o
    conv = convolved(GLM, GLT, forth)

    def begin_sum(which, first, second):
        lengths = jnp.where(tm == 0, lens[0] + lens[1], 0).astype(F32)
        blank = jnp.zeros((1, 128 - TAIL), F32)
        BS[which, 0] = jnp.concatenate(
            [
                first[:, :128],
                jnp.concatenate([first[:, 128:], blank], axis=1),
                second[:, :128],
                jnp.concatenate([second[:, 128:], blank], axis=1),
                jnp.full((4, 128), lengths),
            ],
            axis=0,
        )
        if fast:
            sent, at = [], slots(1)
            for k in range(31, 0, -1):
                kz, dy, dx, dc = k // 8, (k // 4) % 2, (k // 2) % 2, k % 2
                to_y, to_x, to_c = (1 - v if d else v for v, d in ((y, dy), (x, dx), (c, dc)))
                to = (2 * z_at[kz] + to_y, 2 * to_x + to_c)
                remote(BS.at[which, 0], BB.at[which, k - 1], at, at, to).start()
            sent.append(remote(BB.at[which], BB.at[which], at, at, core_peer))
            waits.extend(sent)
        else:
            sent = [
                send(BS.at[which, 0], BB.at[which, k], mate)
                for k, mate in enumerate((x_peer, cross_peer, core_peer))
            ]
        return sent

    def end_sum(which, sent):
        def arrived(copies, at, count, total):
            for made in copies:
                made.wait_recv()
            for k in range(count):
                total = total + BB[which, at + k]
            return total

        total = arrived(sent, 0, 31 if fast else 3, BS[which, 0])
        if not fast:
            BS[which, 1] = total
            sent = [
                send(BS.at[which, 1], BB.at[which, 2 + k], ((utt + k) % n_utt, tm))
                for k in range(1, n_utt)
            ]
            total = arrived(sent, 3, n_utt - 1, total)
        return join(total[0:1], total[1:2]), join(total[2:3], total[3:4]), total[4:5, 0:1]

    counted = own_row * live
    sent = begin_sum(0, colsum(counted * conv), colsum(counted * conv * conv))
    if fast:
        from_core(3)
    ready("second")
    flip = (
        lax.broadcasted_iota(jnp.int32, (ROWS, ROWS), 0)
        + lax.broadcasted_iota(jnp.int32, (ROWS, ROWS), 1)
        == ROWS - 1
    ).astype(F32).astype(BF16)
    qu_r = mm(flip, qu).astype(BF16)
    qv_r = mm(flip, qv).astype(BF16)
    def transposed(v):
        return v.astype(F32).T.astype(BF16)

    for h in range(HEADS):
        prob = PR[h]
        prob = prob * (1.0 / jnp.sum(prob, axis=1, keepdims=True))
        high = prob.astype(BF16)
        rest = (prob - high.astype(F32)).astype(BF16)
        turned_high = mm(flip, high)
        PB[h] = turned_high.astype(BF16)
        PR[h] = turned_high + mm(flip, rest)
    for source, target in ((qu_r, QUT), (qv_r, QVT)):
        v = source.astype(F32).T
        for h in range(HEADS):
            target[h] = v[HEAD_DIM * h : HEAD_DIM * (h + 1)].astype(BF16)
    for j in range(CHUNKS):
        XT[j] = transposed(ACT1[j, window, :])
        HID1[j, 0:ROWS, :] = silu(HID1[j, window, :])[1]
    unpack_frames(c_copies, CS, CB, CF)
    for j, v in enumerate((LOW1[window, :], a2, a3, context)):
        XT[CHUNKS + j] = transposed(v)
    first_sum, second_sum, count = end_sum(0, sent)
    mu = first_sum / count
    spread = lax.rsqrt(second_sum / count - mu * mu + EPS)
    bn = (conv - mu) * spread
    zed = bn * rows_of("batch_gain") + rows_of("batch_bias")
    swished, zed_slope = silu(zed)
    swished = swished.astype(BF16)
    x3 = x2 + mm(swished, square("mix_w")) + rows_of("mix_b")

    total, second_n, second_i, second_low = feed(x3, "second", HID2, ACT2)
    x4 = x3 + 0.5 * total
    final_n, final_i = normed(x4)
    result = final_n * rows_of("final_gain") + rows_of("final_bias")

    def return_frames(v, S, B):
        send_at, recv_at = slots(2), slots(2)
        made = []
        for j in range(2):
            lo, hi = LOCAL * j, HALF - HALO_START + LOCAL * j
            S[j] = jnp.where(half == 0, v[lo : lo + LOCAL, :], v[hi : hi + LOCAL, :]).T
            made.append(
                remote(S.at[j], B.at[unit], send_at + j, recv_at + unit, (utt, 2 * half + j))
            )

        def launch():
            for j in range(2):
                away = 2 * half + j != tm

                @pl.when(away)
                def _(sent=made[j]):
                    sent.start()

                @pl.when(jnp.logical_not(away))
                def _(j=j):
                    B[unit] = S[j]

        def finish():
            for j in range(2):

                @pl.when(2 * half + j != tm)
                def _(sent=made[j]):
                    sent.wait_send()

            for u in range(2):

                @pl.when(2 * u + x != tm)
                def _(u=u):
                    remote(S.at[0], B.at[u], send_at, recv_at + u, core_peer).wait_recv()

        return launch, finish


    g0 = CF[window, :] * live
    d4 = norm_back(g0, rows_of("final_gain"), final_n, final_i)

    def feed_back(grad, prefix, slope_of, active_t, scaled, inverse, low_t, masked):
        low_grad = (0.5 * grad).astype(BF16)
        back = jnp.zeros((ROWS, D), F32)
        hidden_grads = []
        for j in range(CHUNKS):
            grad_hidden = nt(low_grad, square(prefix + "_w_out", j * D))
            grad_hidden = (grad_hidden * slope_of(j)).astype(BF16)
            hidden_grads.append(grad_hidden)
            back = back + nt(grad_hidden, square(prefix + "_w_in", j))

        def out_weights(chunks):
            kept = low_grad * own_low if masked else low_grad
            if CHUNKS - 1 in chunks:
                put(prefix + "_b_out", colsum(kept.astype(F32)))
            for j in chunks:
                put(prefix + "_w_out", mm(active_t(j), kept), j * D)

        def in_weights():
            for j in range(CHUNKS):
                grad_hidden = hidden_grads[j] * own_low if masked else hidden_grads[j]
                put(prefix + "_w_in", mm(low_t(), grad_hidden), j, CHUNKS)
                put(prefix + "_b_in", colsum(grad_hidden.astype(F32)), j)
            kept = back * own_row if masked else back
            put(prefix + "_gain", colsum(kept * scaled))
            put(prefix + "_bias", colsum(kept))

        total = grad + norm_back(back, rows_of(prefix + "_gain"), scaled, inverse)
        return total, out_weights, in_weights

    d3, second_out_weights, second_in_weights = feed_back(
        d4,
        "second",
        lambda j: HID2[j],
        lambda j: transposed(ACT2[j]),
        second_n,
        second_i,
        lambda: transposed(second_low),
        True,
    )

    if fast:
        z_send, z_recv = slots(4), slots(4)
        stage = {}

        def add(a, b):
            return a.astype(F32) + b.astype(F32)

        def begin_round(goal):
            for d in range(8):
                first = 110 * (8 * goal + d)
                block = LB.at[goal, d // 4, (d // 2) % 2, d % 2]
                block[0:MAIN, :] = GM[first : first + MAIN, :].astype(BF16)
                block[MAIN:BLOCK, :] = tails_of(GT[first : first + MAIN, :]).astype(BF16)
            stage[goal] = send(LB.at[goal, :, :, 1 - c], R1.at[goal], core_peer)

        def plane_round(goal):
            stage[goal].wait_recv()
            for yy in range(2):
                for xx in range(2):
                    ACC[goal, yy, xx] = add(LB[goal, yy, xx, c], R1[goal, yy, xx]).astype(BF16)
            at = slots(1)
            for m in range(3):
                block = ACC.at[goal, plane_at[m][0], plane_at[m][1]]
                remote(block, R2.at[goal, m], at, at, plane[m]).start()
            stage[goal] = remote(R2.at[goal], R2.at[goal], at, at, core_peer)
            waits.append(stage[goal])

        def z_copy(goal, sender):
            return remote(
                R3.at[goal], RZ.at[sender], z_send + goal, z_recv + sender, (2 * goal + y, tm)
            )

        def z_round(goal):
            stage[goal].wait_recv()
            total = add(ACC[goal, y, x], R2[goal, 0]) + add(R2[goal, 1], R2[goal, 2])
            R3[goal] = total.astype(BF16)

            @pl.when(z != goal)
            def _():
                z_copy(goal, z).start()

    else:
        begin_round = plane_round = z_round = lambda goal: None

    low_grad = d3.astype(BF16)
    dzed = nt(low_grad, square("mix_w")).astype(BF16).astype(F32)
    dzed = dzed * zed_slope
    e = dzed * rows_of("batch_gain")
    e_own = e * counted
    sent = begin_sum(1, colsum(e_own), colsum(e_own * bn))
    launch_out, finish_out = return_frames(result, OS, out)
    launch_out()
    GM[USED:, :] = jnp.zeros((PADDED - USED, 128), F32)
    GT[USED:, :] = jnp.zeros((PADDED - USED, 128), F32)
    g0_own = g0 * own_row
    put("final_gain", colsum(g0_own * final_n))
    put("final_bias", colsum(g0_own))
    second_out_weights(range(CHUNKS))
    second_in_weights()
    begin_round(3)
    kept = low_grad * own_low
    put("mix_w", tn(swished, kept))
    put("mix_b", colsum(kept.astype(F32)))
    dzed_own = dzed * own_row
    put("batch_gain", colsum(dzed_own * bn))
    put("batch_bias", colsum(dzed_own))
    parts = (e, jnp.broadcast_to(live, (ROWS, D)), live * bn)
    back_parts, depth_parts = [], []
    for i, v in enumerate(parts):
        lay(v, VM, VT)
        back_parts.append(convolved(VM, VT, lambda o: EDGE + LEFT - o))
        kept = v * own_row
        kept_m = kept[:, :128]
        CT[0:ROWS, 0:TAIL] = kept[:, 128:]
        segment_row = lax.broadcasted_iota(jnp.int32, (32, 1), 0) < SEGMENT
        kept_t = jnp.where(segment_row, segments(CT, 32), 0.0)
        mains, tails = [], []
        for o in range(KERNEL):
            mains.append(colsum(kept_m * GLM[pl.ds(forth(o), ROWS), :]))
            tails.append(colsum(kept_t * GLT[pl.ds(forth(o), 32), :]))
        tails = jnp.concatenate(tails, axis=0)
        for shift in (4 * TAIL, 2 * TAIL, TAIL):
            tails = tails + turned(tails, shift)
        depth_parts.append(join(jnp.concatenate(mains, axis=0), tails))
    first_sum, second_sum, count = end_sum(1, sent)
    plane_round(3)
    first_mean, second_mean = first_sum / count, second_sum / count

    def combined(v):
        return spread * (v[0] - v[1] * first_mean - v[2] * second_mean)

    dglu = combined(back_parts).astype(BF16).astype(F32) * counted
    dvalue = (dglu * gate).astype(BF16)
    dgate = (dglu * value * gate * (1.0 - gate)).astype(BF16)
    back = nt(dvalue, square("point_w", 0)) + nt(dgate, square("point_w", 1))
    conv_back = back
    d2 = d3 * own_row + norm_back(back, rows_of("conv_gain"), conv_n, conv_i)

    low_grad = d2.astype(BF16)
    dproj = low_grad
    dctx = nt(low_grad, square("proj_w")).astype(BF16)
    dctx = mm(flip, dctx)
    dctx_t = dctx.T
    dctx = dctx.astype(BF16)
    for h in range(HEADS):
        PD[h] = nt(dctx * head_mask(h), VAL[...])
    du, dw = jnp.zeros((ROWS, D), F32), jnp.zeros((ROWS, D), F32)
    for h in range(HEADS):
        for lo in range(0, ROWS, STRIP):
            strip = slice(lo, lo + STRIP)
            prob, dprob = PR[h, strip, :], PD[h, strip, :]
            dscore = prob * (dprob - jnp.sum(dprob * prob, axis=1, keepdims=True))
            LS[h, strip, :] = dscore.astype(BF16)
            wide = jnp.concatenate([dscore, jnp.zeros((STRIP, WIDE - LEN), F32)], axis=1)
            wide = pltpu.roll(wide, lo, 1, stride=1, stride_axis=0)
            WB[h, strip, :] = wide.astype(BF16)
        mask = head_mask(h)
        head = slice(HEAD_DIM * h, HEAD_DIM * (h + 1))
        DVT[head, :] = mm(dctx_t[head].astype(BF16), PB[h])
        DKT[head, :] = mm(QUT[h], LS[h])
        DPT[head, :] = mm(QVT[h], WB[h])
        du = du + mm(LS[h], KEY[...] * mask)
        dw = dw + mm(WB[h], positions * mask)
    DKA[...] = DKT[...].T
    DVA[...] = DVT[...].T
    theirs = pl.ds(pl.multiple_of(HALO_START * (1 - half), 16), ROWS)
    KS[0] = DKA[theirs, :].astype(BF16)
    KS[1] = DVA[theirs, :].astype(BF16)
    kv_copy = send(KS, KB, core_peer)
    dquery = mm(flip, (scale * (du + dw)).astype(BF16)).astype(BF16)
    put("depth_w", combined(depth_parts))
    put("point_w", mm(XT[CHUNKS + 2], dvalue), 0, 2)
    put("point_w", mm(XT[CHUNKS + 2], dgate), 1, 2)
    put("point_b", colsum(dvalue.astype(F32)), 0)
    put("point_b", colsum(dgate.astype(F32)), 1)
    put("conv_gain", colsum(conv_back * conv_n))
    put("conv_bias", colsum(conv_back))
    put("proj_w", mm(XT[CHUNKS + 3], dproj))
    put("proj_b", colsum(dproj.astype(F32)))
    z_round(3)
    begin_round(2)
    kv_copy.wait_recv()
    dkey = ((DKA[window, :] + KB[0].astype(F32)) * own_row).astype(BF16)
    dval = ((DVA[window, :] + KB[1].astype(F32)) * own_row).astype(BF16)
    back = (
        nt(dquery, square("query_w"))
        + nt(dkey, square("key_w"))
        + nt(dval, square("value_w"))
    )
    att_n, att_i = normed(X1[window, :])
    att_back = back
    d1 = d2 + norm_back(back, rows_of("att_gain"), att_n, att_i)

    d0, first_out_weights, first_in_weights = feed_back(
        d1,
        "first",
        lambda j: HID1[j, 0:ROWS, :],
        lambda j: XT[j],
        NRM1[window, :],
        INV1[window, :],
        lambda: XT[CHUNKS],
        False,
    )
    first_in_weights()
    first_out_weights(range(CHUNKS - 1))
    begin_round(0)
    first_out_weights(range(CHUNKS - 1, CHUNKS))
    put("query_w", mm(XT[CHUNKS + 1], dquery))
    put("query_b", colsum(dquery.astype(F32)))
    put("key_w", mm(XT[CHUNKS + 1], dkey))
    put("value_w", mm(XT[CHUNKS + 1], dval))
    put("value_b", colsum(dval.astype(F32)))
    put("att_gain", colsum(att_back * att_n))
    put("att_bias", colsum(att_back))
    plane_round(0)
    dpos = DPT[...]
    high = dpos.astype(BF16)
    rest = (dpos - high.astype(F32)).astype(BF16)
    put("pos_w", (mm(high, TB[...]) + mm(rest, TB[...])).T)
    put("content_bias", scale * colsum(du))
    put("position_bias", scale * colsum(dw))
    begin_round(1)
    launch_grad, finish_grad = return_frames(d0, IS, grad_out)
    plane_round(2)
    plane_round(1)
    launch_grad()
    z_round(0)
    z_round(2)
    z_round(1)

    finish_out()
    finish_grad()
    for made in waits:
        made.wait_send()
    if fast:
        for goal in range(4):

            @pl.when(z != goal)
            def _(goal=goal):
                z_copy(goal, z).wait_send()

        total = R3[z].astype(F32)
        for j in range(3):
            remote(
                R3.at[0], RZ.at[other_z[j]], 0, z_recv + other_z[j], core_peer
            ).wait_recv()
            total = total + RZ[other_z[j]].astype(F32)
        WM[0:MAIN, :] = total[0:MAIN]
        GT[0:MAIN, :] = rows_of_tails(total[MAIN:BLOCK])
        mains = [WM[pl.ds(i, 14, stride=8), :] for i in range(8)]
        tails = [GT[pl.ds(i, 14, stride=8), :] for i in range(8)]
        for i in range(9):
            row_i = turned(tails[max(i - 1, 0)], TAIL * (i - 1))
            if i < 8:
                row_i = jnp.where(lane >= TAIL * i, turned(mains[i], TAIL * i), row_i)
            if i > 0:
                v = turned(mains[i - 1], TAIL * (i - 1))
                row_i = jnp.where(lane < TAIL * (i - 1), v, row_i)
            WT[pl.ds(i, 14, stride=9), :] = row_i
        for i in range(15):
            flat_out[pl.ds(1024 * i, 1024)] = WT[8 * i : 8 * i + 8, :].reshape(1024)
        rest = LOCAL_SIZE - 15 * 1024
        flat_out[pl.ds(15 * 1024, rest)] = WT[120:128, :].reshape(1024)[0:rest]


def hand_over(first, second, third, first_out, second_out, third_out):
    first_out[...] = first[...]
    second_out[...] = second[...]
    third_out[...] = third[...]


def local(inputs, flat_params, lengths, cotangent):
    n_utt, n_tm = lax.axis_size("utt"), lax.axis_size("tm")
    size = flat_params.shape[0]
    fast = n_utt == 8 and n_tm == 4 and size == LOCAL_SIZE
    table = jnp.asarray(reversed_tables())
    turned = jax.ShapeDtypeStruct((2, D, LOCAL), F32)
    padded = jax.ShapeDtypeStruct((PADDED, 128), F32)
    vmem = pltpu.VMEM
    in_vmem = pl.BlockSpec(memory_space=pltpu.VMEM)
    anywhere = pl.BlockSpec(memory_space=pl.ANY)
    if fast:
        operands = [flat_params]
        results = [turned, turned, jax.ShapeDtypeStruct((size,), F32)]
        scratch = [vmem((PADDED, 128), F32)] * 4 + [
            vmem((size,), F32),
            vmem((4, 2, 2, 2, BLOCK, 128), BF16),
            vmem((4, 2, 2, 2, BLOCK, 128), BF16),
            vmem((4, 2, 2, BLOCK, 128), BF16),
            vmem((4, 3, BLOCK, 128), BF16),
            vmem((4, BLOCK, 128), BF16),
            vmem((4, BLOCK, 128), BF16),
            vmem((4, 2, 2, BLOCK, 128), BF16),
        ]
    else:
        rows = lax.all_gather(flat_params, ("utt", "tm"), axis=0, tiled=True).reshape(TOTAL, D)
        operands = [
            jnp.pad(rows[:, :128], ((0, PADDED - TOTAL), (0, 0))),
            jnp.pad(rows[:, 128:], ((0, PADDED - TOTAL), (0, 128 - TAIL))),
        ]
        results = [turned, turned, padded, padded]
        scratch = []
    others = 31 if fast else 3 + n_utt - 1
    copies = 128 + 2 * others
    scratch = scratch + [
        vmem((2, D, LOCAL), BF16),
        vmem((2, D, LOCAL), BF16),
        vmem((4, D, LOCAL), BF16),
        vmem((4, D, LOCAL), BF16),
        vmem((WIDE, D), BF16),
        vmem((LEN, D), F32),
        vmem((LEN, D), F32),
        vmem((2, D, LOCAL), F32),
        vmem((2, D, LOCAL), F32),
        vmem((len(SQUARES), D, D), BF16),
        vmem((CHUNKS, LEN, D), F32),
        vmem((CHUNKS, LEN, D), BF16),
        vmem((LEN, D), F32),
        vmem((LEN, 1), F32),
        vmem((LEN, D), BF16),
        vmem((LEN, D), F32),
        vmem((LEN, D), BF16),
        vmem((CHUNKS, ROWS, D), F32),
        vmem((CHUNKS, ROWS, D), BF16),
        vmem((LEN, D), BF16),
        vmem((LEN, D), BF16),
        vmem((HEADS, ROWS, LEN), F32),
        vmem((HEADS, ROWS, LEN), F32),
        vmem((HEADS, ROWS, WIDE), F32),
        vmem((HEADS, ROWS, WIDE), BF16),
        vmem((HEADS, ROWS, LEN), BF16),
        vmem((HEADS, ROWS, LEN), BF16),
        vmem((HEADS, HEAD_DIM, ROWS), BF16),
        vmem((HEADS, HEAD_DIM, ROWS), BF16),
        vmem((CHUNKS + 4, D, ROWS), BF16),
        vmem((D, LEN), F32),
        vmem((D, LEN), F32),
        vmem((D, WIDE), F32),
        vmem((LEN, D), F32),
        vmem((LEN, D), F32),
        vmem((ROWS + 2 * EDGE, 128), F32),
        vmem((64, 128), F32),
        vmem((ROWS + 2 * EDGE, 128), F32),
        vmem((64, 128), F32),
        vmem((288, 128), F32),
        vmem((2, ROWS, D), BF16),
        vmem((2, ROWS, D), BF16),
        vmem((2, 2, 8, 128), F32),
        vmem((2, others, 8, 128), F32),
        pltpu.SMEM((2,), jnp.int32),
        pltpu.SemaphoreType.DMA((copies,)),
        pltpu.SemaphoreType.DMA((copies,)),
        pltpu.SemaphoreType.DMA((5,)),
    ]
    got = pl.pallas_call(
        functools.partial(kernel, n_utt, fast),
        out_shape=results,
        in_specs=[anywhere] * 4
        + [anywhere if fast else in_vmem] * len(operands),
        out_specs=[in_vmem] * len(results),
        scratch_shapes=scratch,
        compiler_params=pltpu.CompilerParams(
            collective_id=0, has_side_effects=True, vmem_limit_bytes=56 * 1024 * 1024
        ),
    )(lengths, jnp.swapaxes(inputs, 1, 2), jnp.swapaxes(cotangent, 1, 2), table, *operands)
    if fast:
        out, grad, grad_params = pl.pallas_call(
            hand_over,
            out_shape=results,
            in_specs=[in_vmem] * 3,
            out_specs=[in_vmem] * 3,
        )(*got)
    else:
        out, grad = got[:2]
        rows = jnp.concatenate([got[2][:TOTAL], got[3][:TOTAL, :TAIL]], axis=1)
        grad_params = lax.psum_scatter(
            rows.reshape(-1), ("utt", "tm"), scatter_dimension=0, tiled=True
        )
    return jnp.swapaxes(out, 1, 2), jnp.swapaxes(grad, 1, 2), grad_params


def solution(mesh):
    return jax.shard_map(
        local,
        mesh=mesh,
        in_specs=(P("utt", "tm", None), P(("utt", "tm")), P("utt"), P("utt", "tm", None)),
        out_specs=(P("utt", "tm", None), P("utt", "tm", None), P(("utt", "tm"))),
        check_vma=False,
    )
```

```python
import functools
import math

import jax
import jax.numpy as jnp
import ml_dtypes
import numpy as np
from jax import lax
from jax.experimental import pallas as pl
from jax.experimental.pallas import tpu as pltpu
from jax.sharding import PartitionSpec as P

D = 144
HEADS = 4
FF = 576
KERNEL = 32
HEAD_DIM = 36
LEN = 400
EPS = 1e-05
NEGATIVE = -1e30

CHUNKS = FF // D
LEFT = (KERNEL - 1) // 2
LOCAL = 100
HALF = 200
ROWS = 240
HALO_START = LEN - ROWS
WIDE = 640
STRIP = 48
EDGE = 16
TAIL = D - 128
BLOCK = 128
MAIN = 112
LOCAL_SIZE = 110 * D

F32 = jnp.float32
BF16 = jnp.bfloat16
MESH = pl.DeviceIdType.MESH


def param_rows():
    def feed(prefix):
        return [
            (prefix + "_gain", 1),
            (prefix + "_bias", 1),
            (prefix + "_w_in", D * CHUNKS),
            (prefix + "_b_in", CHUNKS),
            (prefix + "_w_out", FF),
            (prefix + "_b_out", 1),
        ]

    middle = [
        ("att_gain", 1),
        ("att_bias", 1),
        ("query_w", D),
        ("query_b", 1),
        ("key_w", D),
        ("value_w", D),
        ("value_b", 1),
        ("pos_w", D),
        ("content_bias", 1),
        ("position_bias", 1),
        ("proj_w", D),
        ("proj_b", 1),
        ("conv_gain", 1),
        ("conv_bias", 1),
        ("point_w", 2 * D),
        ("point_b", 2),
        ("depth_w", KERNEL),
        ("batch_gain", 1),
        ("batch_bias", 1),
        ("mix_w", D),
        ("mix_b", 1),
    ]
    entries = feed("first") + middle + feed("second") + [("final_gain", 1), ("final_bias", 1)]
    rows = {}
    position = 0
    for name, count in entries:
        rows[name] = position
        position += count
    return rows, position


ROW, USED = param_rows()
TOTAL = 3520
PADDED = TOTAL + 8
SQUARES = (
    [("first_w_in", c, CHUNKS) for c in range(CHUNKS)]
    + [("first_w_out", c * D, 1) for c in range(CHUNKS)]
    + [("second_w_in", c, CHUNKS) for c in range(CHUNKS)]
    + [("second_w_out", c * D, 1) for c in range(CHUNKS)]
    + [("query_w", 0, 1), ("key_w", 0, 1), ("value_w", 0, 1), ("pos_w", 0, 1), ("proj_w", 0, 1)]
    + [("point_w", 0, 2), ("point_w", 1, 2), ("mix_w", 0, 1)]
)
SQUARE = {(name, shift): i for i, (name, shift, unused) in enumerate(SQUARES)}


def reversed_tables():
    distance = np.arange(2 * LEN - 1, dtype=np.float32) - np.float32(LEN - 1)
    steps = np.arange(D // 2, dtype=np.float32)
    frequency = np.exp(np.float32(-math.log(10000.0)) * steps * np.float32(2.0) / np.float32(D))
    angles = (distance[:, None] * frequency[None, :].astype(np.float32)).astype(np.float32)
    table = np.concatenate([np.sin(angles), np.cos(angles)], axis=1).astype(ml_dtypes.bfloat16)
    both = np.zeros((2, WIDE, D), ml_dtypes.bfloat16)
    for half in range(2):
        top = HALO_START * half + ROWS - 1 + LEN - 1
        both[half, : ROWS + LEN - 1] = table[top - (ROWS + LEN - 1) + 1 : top + 1][::-1]
    return both


def mm(a, b):
    return jnp.dot(a, b, preferred_element_type=F32)


def nt(a, b):
    return lax.dot_general(a, b, (((1,), (1,)), ((), ())), preferred_element_type=F32)


def tn(a, b):
    return lax.dot_general(a, b, (((0,), (0,)), ((), ())), preferred_element_type=F32)


def sigmoid(v):
    return 0.5 * jnp.tanh(0.5 * v) + 0.5


def silu(v):
    s = sigmoid(v)
    active = v * s
    return active, s + s * (v - active)


def mean(v):
    return jnp.sum(v, axis=1, keepdims=True) * (1.0 / D)


def normed(v):
    centered = v - mean(v)
    inverse = lax.rsqrt(mean(centered * centered) + EPS)
    return centered * inverse, inverse


def norm_back(grad, gain, scaled, inverse):
    e = grad * gain
    return inverse * (e - mean(e) - scaled * mean(e * scaled))


def colsum(v):
    return jnp.sum(v, axis=0, keepdims=True)


def join(main, tail):
    return jnp.concatenate([main, tail[:, :TAIL]], axis=1)


def kernel(n_utt, fast, lens_in, x_in, cot_in, tab, *refs):
    refs = list(refs)
    take = lambda count: [refs.pop(0) for unused in range(count)]
    if fast:
        (flat_in,) = take(1)
        out, grad_out, flat_out = take(3)
        WM, WT, GM, GT = take(4)
        (FLAT, GB, LB, R1, R2, R3, RZ, ACC) = take(8)
    else:
        WM, WT = take(2)
        out, grad_out, GM, GT = take(4)
    (XS, CS, XB, CB, TB, XF, CF, OS, IS, WS) = take(10)
    (HID1, ACT1, NRM1, INV1, LOW1, X1, A2, HID2, ACT2) = take(9)
    (KEY, VAL, PR, PD, WD, WB, LS, PB, QUT, QVT, XT, DKT, DVT, DPT, DKA, DVA, GLM, GLT, VM, VT, CT) = take(21)
    (KS, KB, BS, BB, lens, send_sem, recv_sem, local_sem) = take(8)

    utt = lax.axis_index("utt")
    tm = lax.axis_index("tm")
    x, c = tm // 2, tm % 2
    z, y = utt // 2, utt % 2
    unit, half = x, c
    start = pl.multiple_of(HALO_START * half, 16)

    used = [0]
    waits = []

    def slots(count):
        at = used[0]
        used[0] += count
        return at

    def remote(src, dst, send_at, recv_at, device):
        return pltpu.make_async_remote_copy(
            src_ref=src,
            dst_ref=dst,
            send_sem=send_sem.at[send_at],
            recv_sem=recv_sem.at[recv_at],
            device_id=device,
            device_id_type=MESH,
        )

    def send(src, dst, device, send_at=None, recv_at=None):
        if send_at is None:
            send_at = recv_at = slots(1)
        made = remote(src, dst, send_at, recv_at, device)
        made.start()
        waits.append(made)
        return made

    core_peer = (utt, 2 * x + 1 - c)
    x_peer = (utt, 2 * (1 - x) + c)
    cross_peer = (utt, 2 * (1 - x) + 1 - c)
    y_peer = (2 * z + 1 - y, tm)
    xy_peer = (2 * z + 1 - y, 2 * (1 - x) + c)
    plane = [x_peer, y_peer, xy_peer]
    plane_at = [(y, 1 - x), (1 - y, x), (1 - y, 1 - x)]
    z_at = [z, z + 1 - 2 * (z % 2), (z + 2) % 4, 3 - z]
    other_z = [j + (j - z + 4) // 4 for j in range(3)]

    barrier = pltpu.get_barrier_semaphore()
    partners = [core_peer, x_peer, cross_peer]
    if fast:
        partners += [(2 * zz + y, tm) for zz in other_z] + [y_peer, xy_peer]
    else:
        partners += [((utt + k) % n_utt, tm) for k in range(1, n_utt)]
    for partner in partners:
        pl.semaphore_signal(barrier, inc=1, device_id=partner, device_id_type=MESH)
    fetches = [
        pltpu.make_async_copy(x_in, XS, local_sem.at[0]),
        pltpu.make_async_copy(cot_in, CS, local_sem.at[1]),
        pltpu.make_async_copy(tab.at[half], TB, local_sem.at[2]),
        pltpu.make_async_copy(lens_in, lens, local_sem.at[4]),
    ]
    if fast:
        flat_fetch = pltpu.make_async_copy(flat_in, FLAT, local_sem.at[3])
        flat_fetch.start()
    for fetch in fetches:
        fetch.start()

    lane = lax.broadcasted_iota(jnp.int32, (1, 128), 1)
    lane_d = lax.broadcasted_iota(jnp.int32, (1, D), 1)

    def lanes_of(g):
        return (lane >= TAIL * g) & (lane < TAIL * (g + 1))

    def turned(v, shift):
        return v if shift % 128 == 0 else pltpu.roll(v, shift % 128, 1)

    def tails_of(rows):
        packed = jnp.zeros((16, 128), F32)
        for g in range(7):
            packed = jnp.where(lanes_of(g), turned(rows[16 * g : 16 * g + 16], TAIL * g), packed)
        return packed

    def rows_of_tails(packed):
        return jnp.concatenate([turned(packed, -TAIL * g) for g in range(7)], axis=0)

    if fast:
        own = GB.at[z, y, x, c]
        flat_fetch.wait()
        for i in range(15):
            GM[8 * i : 8 * i + 8, :] = FLAT[pl.ds(1024 * i, 1024)].reshape(8, 128)
        rest = LOCAL_SIZE - 15 * 1024
        GM[120:128, :] = jnp.concatenate(
            [FLAT[pl.ds(15 * 1024, rest)], jnp.zeros((1024 - rest,), F32)]
        ).reshape(8, 128)
        dense = [GM[pl.ds(i, 14, stride=9), :] for i in range(9)]
        for i in range(8):
            shift = TAIL * i
            left = turned(dense[i], -shift)
            right = turned(dense[i + 1], -shift)
            WM[pl.ds(i, 14, stride=8), :] = jnp.where(lane < 128 - shift, left, right)
            WT[pl.ds(i, 14, stride=8), :] = right
        own[0:MAIN, :] = WM[0:MAIN, :].astype(BF16)
        own[MAIN:BLOCK, :] = tails_of(WT[0:MAIN, :]).astype(BF16)
        col_at, p_at, c_at = slots(4), slots(12), slots(4)

        def to_column(j):
            to = (2 * z_at[3 - j] + y, tm)
            remote(own, own, col_at, col_at + z, to).start()

        def to_plane(zz, mates):
            block = GB.at[zz, y, x, c]
            for m in range(mates):
                remote(block, block, p_at, p_at + 4 * m + zz, plane[m]).start()

        def diagonal_to_column():
            block = GB.at[z, 1 - y, 1 - x, c]
            remote(block, block, p_at, p_at + 8 + z, core_peer).wait_recv()
            for j in range(3):
                to = (2 * z_at[3 - j] + y, tm)
                remote(block, block, p_at, p_at + 8 + z, to).start()
            to_core(z, (1 - y, 1 - x))

        def from_plane(zz, mates):
            for m in range(mates):
                block = GB.at[zz, plane_at[m][0], plane_at[m][1], c]
                remote(block, block, p_at, p_at + 4 * m + zz, core_peer).wait_recv()
                to_core(zz, plane_at[m])

        def diagonal_from_column(zz):
            @pl.when(z != zz)
            def _():
                block = GB.at[zz, 1 - y, 1 - x, c]
                remote(block, block, p_at, p_at + 8 + zz, core_peer).wait_recv()
                to_core(zz, (1 - y, 1 - x))

        def to_core(zz, where):
            block = GB.at[zz, where[0], where[1], c]
            remote(block, block, c_at, c_at + zz, core_peer).start()

        waits.append(remote(R2.at[0], R2.at[0], col_at, col_at, core_peer))
        waits.append(remote(R2, R2, p_at, p_at, core_peer))
        waits.append(remote(GB.at[0:2], GB.at[0:2], c_at, c_at, core_peer))

        def from_core(zz):
            blocks = GB.at[zz, :, :, 1 - c]
            remote(blocks, blocks, c_at, c_at + zz, core_peer).wait_recv()
            for low_d in range(8):
                block = GB.at[zz, low_d // 4, (low_d // 2) % 2, low_d % 2]
                first = 110 * (8 * zz + low_d)
                WM[first : first + 110, :] = block[0:110, :].astype(F32)
                WT[first : first + 110, :] = rows_of_tails(block[MAIN:BLOCK, :].astype(F32))[0:110]

    pl.semaphore_wait(barrier, len(partners))
    if fast:
        for j in range(3):
            to_column(j)

    def exchange(source, target):
        return (
            send(source.at[1 - x], target.at[tm], x_peer),
            send(source.at[x], target.at[tm], core_peer),
        )

    def relay(copies, target):
        copies[0].wait_recv()
        passed = target.at[x_peer[1]]
        return copies[1], send(passed, passed, core_peer)

    def unpack_frames(copies, source, target, frames):
        for made in copies:
            made.wait_recv()
        target[tm] = source[unit]
        for k in range(4):
            frames[LOCAL * k : LOCAL * (k + 1), :] = target[k].astype(F32).T

    fetches[0].wait()
    x_copies = exchange(XS, XB)
    if fast:
        to_plane(z, 3)
        to_core(z, (y, x))
    x_copies = relay(x_copies, XB)
    if fast:
        diagonal_to_column()
        for j in range(3):
            block = GB.at[other_z[j], y, x, c]
            remote(block, block, col_at, col_at + other_z[j], core_peer).wait_recv()
            to_plane(other_z[j], 2)
            to_core(other_z[j], (y, x))
    fetches[1].wait()
    c_copies = exchange(CS, CB)

    def rows_of(name, count=1, shift=0, stride=1):
        at = ROW[name] + shift
        s = pl.ds(at, count) if stride == 1 else pl.ds(at, count, stride=stride)
        return join(WM[s, :], WT[s, :])

    def put(name, value, shift=0, stride=1):
        at = ROW[name] + shift
        count = value.shape[0]
        if stride == 1:
            GM[pl.ds(at, count), :] = value[:, :128]
            GT[pl.ds(at, count), 0:TAIL] = value[:, 128:]
        else:
            s = pl.ds(at, count, stride=stride)
            GM[s, :] = value[:, :128]
            GT[s, :] = jnp.concatenate(
                [value[:, 128:], jnp.zeros((count, 128 - TAIL), F32)], axis=1
            )

    def ready(prefixes):
        for i, (name, shift, stride) in enumerate(SQUARES):
            if name.startswith(prefixes):
                WS[i] = rows_of(name, D, shift, stride).astype(BF16)

    def square(name, shift=0):
        return WS[SQUARE[name, shift]]

    row = lax.broadcasted_iota(jnp.int32, (ROWS, 1), 0)
    frame = row + start
    own_row = ((frame >= HALF * half) & (frame < HALF * half + HALF)).astype(F32)
    own_low = own_row.astype(BF16)
    fetches[3].wait()
    length = jnp.where(unit == 0, lens[0], lens[1])
    live = (frame < length).astype(F32)
    scale = HEAD_DIM ** (-0.5)
    window = pl.ds(start, ROWS)

    if fast:
        from_plane(0, 2)
        diagonal_from_column(0)
        from_plane(1, 2)
        diagonal_from_column(1)
        from_core(0)
        from_core(1)
    unpack_frames(x_copies, XS, XB, XF)
    ready("first")
    c_copies = relay(c_copies, CB)

    def feed(v, prefix, HID, ACT):
        scaled, inverse = normed(v)
        low = (scaled * rows_of(prefix + "_gain") + rows_of(prefix + "_bias")).astype(BF16)
        total = rows_of(prefix + "_b_out")
        for j in range(CHUNKS):
            hidden = mm(low, square(prefix + "_w_in", j)) + rows_of(prefix + "_b_in", 1, j)
            if prefix == "first":
                HID[j] = hidden
                active = hidden * sigmoid(hidden)
            else:
                active, HID[j] = silu(hidden)
            active = active.astype(BF16)
            ACT[j] = active
            total = total + mm(active, square(prefix + "_w_out", j * D))
        return total, scaled, inverse, low

    v = XF[...]
    total, scaled, inverse, low = feed(v, "first", HID1, ACT1)
    NRM1[...] = scaled
    INV1[...] = inverse
    LOW1[...] = low
    x1 = v + 0.5 * total
    X1[...] = x1

    if fast:
        for zz in (2, 3):
            from_plane(zz, 2)
            diagonal_from_column(zz)
        from_core(2)
    ready(("query", "key", "value", "pos_w", "proj", "point", "mix"))
    fetches[2].wait()
    scaled, inverse = normed(x1)
    low = (scaled * rows_of("att_gain") + rows_of("att_bias")).astype(BF16)
    A2[...] = low
    KEY[...] = mm(low, square("key_w")).astype(BF16)
    VAL[...] = (mm(low, square("value_w")) + rows_of("value_b")).astype(BF16)
    a2 = A2[window, :]
    query = mm(a2, square("query_w")) + rows_of("query_b")
    qu = ((query + rows_of("content_bias")) * scale).astype(BF16)
    qv = ((query + rows_of("position_bias")) * scale).astype(BF16)
    positions = mm(TB[...], square("pos_w")).astype(BF16)
    key_bias = jnp.where(
        lax.broadcasted_iota(jnp.int32, (1, LEN), 1) < length, 0.0, NEGATIVE
    )

    def head_mask(h):
        return ((lane_d >= HEAD_DIM * h) & (lane_d < HEAD_DIM * (h + 1))).astype(BF16)

    for h in range(HEADS):
        mask = head_mask(h)
        PR[h] = nt(qu * mask, KEY[...])
        WD[h] = nt(qv * mask, positions)
    context, share = jnp.zeros((ROWS, D), F32), jnp.zeros((ROWS, D), F32)
    for h in range(HEADS):
        for lo in range(0, ROWS, STRIP):
            strip = slice(lo, lo + STRIP)
            wide = pltpu.roll(WD[h, strip, :], WIDE - ROWS + 1 + lo, 1, stride=1, stride_axis=0)
            score = PR[h, strip, :] + wide[:, :LEN] + key_bias
            score = jnp.exp(score - jnp.max(score, axis=1, keepdims=True))
            PR[h, strip, :] = score
            PB[h, strip, :] = score.astype(BF16)
        mask = head_mask(h)
        context = context + mm(PB[h], VAL[...] * mask)
        share = share + mm(PB[h], jnp.broadcast_to(mask, (LEN, D)))
    context = (context / share).astype(BF16)
    x2 = X1[window, :] + mm(context, square("proj_w")) + rows_of("proj_b")

    conv_n, conv_i = normed(x2)
    a3 = (conv_n * rows_of("conv_gain") + rows_of("conv_bias")).astype(BF16)
    value = mm(a3, square("point_w", 0)) + rows_of("point_b", 1, 0)
    gate = sigmoid(mm(a3, square("point_w", 1)) + rows_of("point_b", 1, 1))
    SEGMENT = ROWS // 8

    def segments(ref, count):
        packed = turned(ref[0:count, :], 0)
        for g in range(1, 8):
            v = turned(ref[SEGMENT * g : SEGMENT * g + count, :], TAIL * g)
            packed = jnp.where(lane >= TAIL * g, v, packed)
        return packed

    def unsegmented(v):
        for g in range(8):
            CT[SEGMENT * g : SEGMENT * (g + 1), :] = turned(v, -TAIL * g)[0:SEGMENT]
        return CT[0:ROWS, :]

    def lay(v, main, tail):
        for lo, hi in ((0, EDGE), (EDGE + ROWS, 2 * EDGE + ROWS)):
            main[lo:hi, :] = jnp.zeros((hi - lo, 128), F32)
            CT[lo:hi, :] = jnp.zeros((hi - lo, 128), F32)
        main[EDGE : EDGE + ROWS, :] = v[:, :128]
        CT[EDGE : EDGE + ROWS, 0:TAIL] = v[:, 128:]
        tail[...] = segments(CT, 64)

    def convolved(main, tail, first):
        blocks = []
        for lo in range(0, ROWS, 80):
            total = depth_m[0:1] * main[pl.ds(lo + first(0), 80), :]
            for o in range(1, KERNEL):
                total = total + depth_m[o : o + 1] * main[pl.ds(lo + first(o), 80), :]
            blocks.append(total)
        total = depth_t[0:1] * tail[pl.ds(first(0), 32), :]
        for o in range(1, KERNEL):
            total = total + depth_t[o : o + 1] * tail[pl.ds(first(o), 32), :]
        return join(jnp.concatenate(blocks, axis=0), unsegmented(total))

    depth_rows = pl.ds(ROW["depth_w"], KERNEL)
    depth_m = WM[depth_rows, :]
    depth_t = jnp.where(lane < TAIL, WT[depth_rows, :], 0.0)
    for shift in (TAIL, 2 * TAIL, 4 * TAIL):
        depth_t = depth_t + turned(depth_t, shift)
    CT[2 * EDGE + ROWS :, :] = jnp.zeros((CT.shape[0] - 2 * EDGE - ROWS, 128), F32)
    lay((live * value * gate).astype(BF16).astype(F32), GLM, GLT)
    forth = lambda o: EDGE - LEFT + o
    conv = convolved(GLM, GLT, forth)

    def begin_sum(which, first, second):
        lengths = jnp.where(tm == 0, lens[0] + lens[1], 0).astype(F32)
        blank = jnp.zeros((1, 128 - TAIL), F32)
        BS[which, 0] = jnp.concatenate(
            [
                first[:, :128],
                jnp.concatenate([first[:, 128:], blank], axis=1),
                second[:, :128],
                jnp.concatenate([second[:, 128:], blank], axis=1),
                jnp.full((4, 128), lengths),
            ],
            axis=0,
        )
        if fast:
            sent, at = [], slots(1)
            for k in range(31, 0, -1):
                kz, dy, dx, dc = k // 8, (k // 4) % 2, (k // 2) % 2, k % 2
                to_y, to_x, to_c = (1 - v if d else v for v, d in ((y, dy), (x, dx), (c, dc)))
                to = (2 * z_at[kz] + to_y, 2 * to_x + to_c)
                remote(BS.at[which, 0], BB.at[which, k - 1], at, at, to).start()
            sent.append(remote(BB.at[which], BB.at[which], at, at, core_peer))
            waits.extend(sent)
        else:
            sent = [
                send(BS.at[which, 0], BB.at[which, k], mate)
                for k, mate in enumerate((x_peer, cross_peer, core_peer))
            ]
        return sent

    def end_sum(which, sent):
        def arrived(copies, at, count, total):
            for made in copies:
                made.wait_recv()
            for k in range(count):
                total = total + BB[which, at + k]
            return total

        total = arrived(sent, 0, 31 if fast else 3, BS[which, 0])
        if not fast:
            BS[which, 1] = total
            sent = [
                send(BS.at[which, 1], BB.at[which, 2 + k], ((utt + k) % n_utt, tm))
                for k in range(1, n_utt)
            ]
            total = arrived(sent, 3, n_utt - 1, total)
        return join(total[0:1], total[1:2]), join(total[2:3], total[3:4]), total[4:5, 0:1]

    counted = own_row * live
    sent = begin_sum(0, colsum(counted * conv), colsum(counted * conv * conv))
    if fast:
        from_core(3)
    ready("second")
    flip = (
        lax.broadcasted_iota(jnp.int32, (ROWS, ROWS), 0)
        + lax.broadcasted_iota(jnp.int32, (ROWS, ROWS), 1)
        == ROWS - 1
    ).astype(F32).astype(BF16)
    qu_r = mm(flip, qu).astype(BF16)
    qv_r = mm(flip, qv).astype(BF16)
    def transposed(v):
        return v.astype(F32).T.astype(BF16)

    for h in range(HEADS):
        prob = PR[h]
        prob = prob * (1.0 / jnp.sum(prob, axis=1, keepdims=True))
        high = prob.astype(BF16)
        rest = (prob - high.astype(F32)).astype(BF16)
        turned_high = mm(flip, high)
        PB[h] = turned_high.astype(BF16)
        PR[h] = turned_high + mm(flip, rest)
    for source, target in ((qu_r, QUT), (qv_r, QVT)):
        v = source.astype(F32).T
        for h in range(HEADS):
            target[h] = v[HEAD_DIM * h : HEAD_DIM * (h + 1)].astype(BF16)
    for j in range(CHUNKS):
        XT[j] = transposed(ACT1[j, window, :])
        HID1[j, 0:ROWS, :] = silu(HID1[j, window, :])[1]
    unpack_frames(c_copies, CS, CB, CF)
    for j, v in enumerate((LOW1[window, :], a2, a3, context)):
        XT[CHUNKS + j] = transposed(v)
    first_sum, second_sum, count = end_sum(0, sent)
    mu = first_sum / count
    spread = lax.rsqrt(second_sum / count - mu * mu + EPS)
    bn = (conv - mu) * spread
    zed = bn * rows_of("batch_gain") + rows_of("batch_bias")
    swished, zed_slope = silu(zed)
    swished = swished.astype(BF16)
    x3 = x2 + mm(swished, square("mix_w")) + rows_of("mix_b")

    total, second_n, second_i, second_low = feed(x3, "second", HID2, ACT2)
    x4 = x3 + 0.5 * total
    final_n, final_i = normed(x4)
    result = final_n * rows_of("final_gain") + rows_of("final_bias")

    def return_frames(v, S, B):
        send_at, recv_at = slots(2), slots(2)
        made = []
        for j in range(2):
            lo, hi = LOCAL * j, HALF - HALO_START + LOCAL * j
            S[j] = jnp.where(half == 0, v[lo : lo + LOCAL, :], v[hi : hi + LOCAL, :]).T
            made.append(
                remote(S.at[j], B.at[unit], send_at + j, recv_at + unit, (utt, 2 * half + j))
            )

        def launch():
            for j in range(2):
                away = 2 * half + j != tm

                @pl.when(away)
                def _(sent=made[j]):
                    sent.start()

                @pl.when(jnp.logical_not(away))
                def _(j=j):
                    B[unit] = S[j]

        def finish():
            for j in range(2):

                @pl.when(2 * half + j != tm)
                def _(sent=made[j]):
                    sent.wait_send()

            for u in range(2):

                @pl.when(2 * u + x != tm)
                def _(u=u):
                    remote(S.at[0], B.at[u], send_at, recv_at + u, core_peer).wait_recv()

        return launch, finish


    g0 = CF[window, :] * live
    d4 = norm_back(g0, rows_of("final_gain"), final_n, final_i)

    def feed_back(grad, prefix, slope_of, active_t, scaled, inverse, low_t, masked):
        low_grad = (0.5 * grad).astype(BF16)
        back = jnp.zeros((ROWS, D), F32)
        hidden_grads = []
        for j in range(CHUNKS):
            grad_hidden = nt(low_grad, square(prefix + "_w_out", j * D))
            grad_hidden = (grad_hidden * slope_of(j)).astype(BF16)
            hidden_grads.append(grad_hidden)
            back = back + nt(grad_hidden, square(prefix + "_w_in", j))

        def out_weights(chunks):
            kept = low_grad * own_low if masked else low_grad
            if CHUNKS - 1 in chunks:
                put(prefix + "_b_out", colsum(kept.astype(F32)))
            for j in chunks:
                put(prefix + "_w_out", mm(active_t(j), kept), j * D)

        def in_weights():
            for j in range(CHUNKS):
                grad_hidden = hidden_grads[j] * own_low if masked else hidden_grads[j]
                put(prefix + "_w_in", mm(low_t(), grad_hidden), j, CHUNKS)
                put(prefix + "_b_in", colsum(grad_hidden.astype(F32)), j)
            kept = back * own_row if masked else back
            put(prefix + "_gain", colsum(kept * scaled))
            put(prefix + "_bias", colsum(kept))

        total = grad + norm_back(back, rows_of(prefix + "_gain"), scaled, inverse)
        return total, out_weights, in_weights

    d3, second_out_weights, second_in_weights = feed_back(
        d4,
        "second",
        lambda j: HID2[j],
        lambda j: transposed(ACT2[j]),
        second_n,
        second_i,
        lambda: transposed(second_low),
        True,
    )

    if fast:
        pieces = [(0, 0, 64), (0, 64, BLOCK), (1, 0, BLOCK), (2, 0, BLOCK), (3, 0, BLOCK)]
        z_send, z_recv = slots(len(pieces)), slots(4 * len(pieces))
        stage = {}

        def add(a, b):
            return a.astype(F32) + b.astype(F32)

        def pieces_of(goal):
            return [piece for piece in pieces if piece[0] == goal]

        def begin_round(goal):
            for piece in pieces_of(goal):
                lo, hi = piece[1:]
                rows = pl.ds(lo, hi - lo)
                for d in range(8):
                    first = 110 * (8 * goal + d)
                    block = LB.at[goal, d // 4, (d // 2) % 2, d % 2]
                    top = min(hi, MAIN)
                    block[lo:top, :] = GM[first + lo : first + top, :].astype(BF16)
                    if hi == BLOCK:
                        tails = tails_of(GT[first : first + MAIN, :])
                        block[MAIN:BLOCK, :] = tails.astype(BF16)
                stage[piece] = send(
                    LB.at[goal, :, :, 1 - c, rows], R1.at[goal, :, :, rows], core_peer
                )

        def plane_round(goal):
            for piece in pieces_of(goal):
                lo, hi = piece[1:]
                rows = pl.ds(lo, hi - lo)
                stage[piece].wait_recv()
                for yy in range(2):
                    for xx in range(2):
                        both = add(LB[goal, yy, xx, c, lo:hi], R1[goal, yy, xx, lo:hi])
                        ACC[goal, yy, xx, lo:hi] = both.astype(BF16)
                at = slots(1)
                for m in range(3):
                    block = ACC.at[goal, plane_at[m][0], plane_at[m][1], rows]
                    remote(block, R2.at[goal, m, rows], at, at, plane[m]).start()
                all_three = R2.at[goal, :, rows]
                stage[piece] = remote(all_three, all_three, at, at, core_peer)
                waits.append(stage[piece])

        def z_copy(piece, sender):
            goal, lo, hi = piece
            rows, index = pl.ds(lo, hi - lo), pieces.index(piece)
            return remote(
                R3.at[goal, rows],
                RZ.at[sender, rows],
                z_send + index,
                z_recv + 4 * index + sender,
                (2 * goal + y, tm),
            )

        def z_round(goal):
            for piece in pieces_of(goal):
                lo, hi = piece[1:]
                stage[piece].wait_recv()
                total = add(ACC[goal, y, x, lo:hi], R2[goal, 0, lo:hi])
                total = total + add(R2[goal, 1, lo:hi], R2[goal, 2, lo:hi])
                R3[goal, lo:hi] = total.astype(BF16)

                @pl.when(z != goal)
                def _(piece=piece):
                    z_copy(piece, z).start()

    else:
        begin_round = plane_round = z_round = lambda goal: None

    low_grad = d3.astype(BF16)
    dzed = nt(low_grad, square("mix_w")).astype(BF16).astype(F32)
    dzed = dzed * zed_slope
    e = dzed * rows_of("batch_gain")
    e_own = e * counted
    sent = begin_sum(1, colsum(e_own), colsum(e_own * bn))
    launch_out, finish_out = return_frames(result, OS, out)
    launch_out()
    GM[USED:, :] = jnp.zeros((PADDED - USED, 128), F32)
    GT[USED:, :] = jnp.zeros((PADDED - USED, 128), F32)
    g0_own = g0 * own_row
    put("final_gain", colsum(g0_own * final_n))
    put("final_bias", colsum(g0_own))
    second_out_weights(range(CHUNKS))
    second_in_weights()
    begin_round(3)
    kept = low_grad * own_low
    put("mix_w", tn(swished, kept))
    put("mix_b", colsum(kept.astype(F32)))
    dzed_own = dzed * own_row
    put("batch_gain", colsum(dzed_own * bn))
    put("batch_bias", colsum(dzed_own))
    parts = (e, jnp.broadcast_to(live, (ROWS, D)), live * bn)
    back_parts, depth_parts = [], []
    for i, v in enumerate(parts):
        lay(v, VM, VT)
        back_parts.append(convolved(VM, VT, lambda o: EDGE + LEFT - o))
        kept = v * own_row
        kept_m = kept[:, :128]
        CT[0:ROWS, 0:TAIL] = kept[:, 128:]
        segment_row = lax.broadcasted_iota(jnp.int32, (32, 1), 0) < SEGMENT
        kept_t = jnp.where(segment_row, segments(CT, 32), 0.0)
        mains, tails = [], []
        for o in range(KERNEL):
            mains.append(colsum(kept_m * GLM[pl.ds(forth(o), ROWS), :]))
            tails.append(colsum(kept_t * GLT[pl.ds(forth(o), 32), :]))
        tails = jnp.concatenate(tails, axis=0)
        for shift in (4 * TAIL, 2 * TAIL, TAIL):
            tails = tails + turned(tails, shift)
        depth_parts.append(join(jnp.concatenate(mains, axis=0), tails))
    first_sum, second_sum, count = end_sum(1, sent)
    plane_round(3)
    first_mean, second_mean = first_sum / count, second_sum / count

    def combined(v):
        return spread * (v[0] - v[1] * first_mean - v[2] * second_mean)

    dglu = combined(back_parts).astype(BF16).astype(F32) * counted
    dvalue = (dglu * gate).astype(BF16)
    dgate = (dglu * value * gate * (1.0 - gate)).astype(BF16)
    back = nt(dvalue, square("point_w", 0)) + nt(dgate, square("point_w", 1))
    conv_back = back
    d2 = d3 * own_row + norm_back(back, rows_of("conv_gain"), conv_n, conv_i)

    low_grad = d2.astype(BF16)
    dproj = low_grad
    dctx = nt(low_grad, square("proj_w")).astype(BF16)
    dctx = mm(flip, dctx)
    dctx_t = dctx.T
    dctx = dctx.astype(BF16)
    heads = [slice(HEAD_DIM * h, HEAD_DIM * (h + 1)) for h in range(HEADS)]
    theirs = pl.ds(pl.multiple_of(HALO_START * (1 - half), 16), ROWS)
    for h in range(HEADS):
        PD[h] = nt(dctx * head_mask(h), VAL[...])
        DVT[heads[h], :] = mm(dctx_t[heads[h]].astype(BF16), PB[h])
    DVA[...] = DVT[...].T
    KS[1] = DVA[theirs, :].astype(BF16)
    value_copy = send(KS.at[1], KB.at[1], core_peer)
    for h in range(HEADS):
        for lo in range(0, ROWS, STRIP):
            strip = slice(lo, lo + STRIP)
            prob, dprob = PR[h, strip, :], PD[h, strip, :]
            dscore = prob * (dprob - jnp.sum(dprob * prob, axis=1, keepdims=True))
            LS[h, strip, :] = dscore.astype(BF16)
            wide = jnp.concatenate([dscore, jnp.zeros((STRIP, WIDE - LEN), F32)], axis=1)
            wide = pltpu.roll(wide, lo, 1, stride=1, stride_axis=0)
            WB[h, strip, :] = wide.astype(BF16)
        DKT[heads[h], :] = mm(QUT[h], LS[h])
    DKA[...] = DKT[...].T
    KS[0] = DKA[theirs, :].astype(BF16)
    key_copy = send(KS.at[0], KB.at[0], core_peer)
    du, dw = jnp.zeros((ROWS, D), F32), jnp.zeros((ROWS, D), F32)
    for h in range(HEADS):
        mask = head_mask(h)
        du = du + mm(LS[h], KEY[...] * mask)
        dw = dw + mm(WB[h], positions * mask)
    dquery = mm(flip, (scale * (du + dw)).astype(BF16)).astype(BF16)
    put("depth_w", combined(depth_parts))
    put("point_w", mm(XT[CHUNKS + 2], dvalue), 0, 2)
    put("point_w", mm(XT[CHUNKS + 2], dgate), 1, 2)
    put("point_b", colsum(dvalue.astype(F32)), 0)
    put("point_b", colsum(dgate.astype(F32)), 1)
    put("conv_gain", colsum(conv_back * conv_n))
    put("conv_bias", colsum(conv_back))
    put("proj_w", mm(XT[CHUNKS + 3], dproj))
    put("proj_b", colsum(dproj.astype(F32)))
    z_round(3)
    begin_round(2)
    key_copy.wait_recv()
    value_copy.wait_recv()
    dkey = ((DKA[window, :] + KB[0].astype(F32)) * own_row).astype(BF16)
    dval = ((DVA[window, :] + KB[1].astype(F32)) * own_row).astype(BF16)
    back = (
        nt(dquery, square("query_w"))
        + nt(dkey, square("key_w"))
        + nt(dval, square("value_w"))
    )
    att_n, att_i = normed(X1[window, :])
    att_back = back
    d1 = d2 + norm_back(back, rows_of("att_gain"), att_n, att_i)

    d0, first_out_weights, first_in_weights = feed_back(
        d1,
        "first",
        lambda j: HID1[j, 0:ROWS, :],
        lambda j: XT[j],
        NRM1[window, :],
        INV1[window, :],
        lambda: XT[CHUNKS],
        False,
    )
    first_in_weights()
    first_out_weights(range(CHUNKS - 1))
    begin_round(0)
    first_out_weights(range(CHUNKS - 1, CHUNKS))
    put("query_w", mm(XT[CHUNKS + 1], dquery))
    put("query_b", colsum(dquery.astype(F32)))
    put("key_w", mm(XT[CHUNKS + 1], dkey))
    put("value_w", mm(XT[CHUNKS + 1], dval))
    put("value_b", colsum(dval.astype(F32)))
    put("att_gain", colsum(att_back * att_n))
    put("att_bias", colsum(att_back))
    plane_round(0)
    for h in range(HEADS):
        DPT[heads[h], :] = mm(QVT[h], WB[h])
    dpos = DPT[...]
    high = dpos.astype(BF16)
    rest = (dpos - high.astype(F32)).astype(BF16)
    put("pos_w", (mm(high, TB[...]) + mm(rest, TB[...])).T)
    put("content_bias", scale * colsum(du))
    put("position_bias", scale * colsum(dw))
    begin_round(1)
    launch_grad, finish_grad = return_frames(d0, IS, grad_out)
    plane_round(2)
    plane_round(1)
    launch_grad()
    z_round(0)
    z_round(2)
    z_round(1)

    finish_out()
    finish_grad()
    for made in waits:
        made.wait_send()
    if fast:
        for piece in pieces:

            @pl.when(z != piece[0])
            def _(piece=piece):
                z_copy(piece, z).wait_send()

            @pl.when(z == piece[0])
            def _(piece=piece):
                for j in range(3):
                    z_copy(piece, other_z[j]).wait_recv()

        total = R3[z].astype(F32)
        for j in range(3):
            total = total + RZ[other_z[j]].astype(F32)
        WM[0:MAIN, :] = total[0:MAIN]
        GT[0:MAIN, :] = rows_of_tails(total[MAIN:BLOCK])
        mains = [WM[pl.ds(i, 14, stride=8), :] for i in range(8)]
        tails = [GT[pl.ds(i, 14, stride=8), :] for i in range(8)]
        for i in range(9):
            row_i = turned(tails[max(i - 1, 0)], TAIL * (i - 1))
            if i < 8:
                row_i = jnp.where(lane >= TAIL * i, turned(mains[i], TAIL * i), row_i)
            if i > 0:
                v = turned(mains[i - 1], TAIL * (i - 1))
                row_i = jnp.where(lane < TAIL * (i - 1), v, row_i)
            WT[pl.ds(i, 14, stride=9), :] = row_i
        for i in range(15):
            flat_out[pl.ds(1024 * i, 1024)] = WT[8 * i : 8 * i + 8, :].reshape(1024)
        rest = LOCAL_SIZE - 15 * 1024
        flat_out[pl.ds(15 * 1024, rest)] = WT[120:128, :].reshape(1024)[0:rest]


def hand_over(first, second, third, first_out, second_out, third_out):
    first_out[...] = first[...]
    second_out[...] = second[...]
    third_out[...] = third[...]


def local(inputs, flat_params, lengths, cotangent):
    n_utt, n_tm = lax.axis_size("utt"), lax.axis_size("tm")
    size = flat_params.shape[0]
    fast = n_utt == 8 and n_tm == 4 and size == LOCAL_SIZE
    table = jnp.asarray(reversed_tables())
    turned = jax.ShapeDtypeStruct((2, D, LOCAL), F32)
    padded = jax.ShapeDtypeStruct((PADDED, 128), F32)
    vmem = pltpu.VMEM
    in_vmem = pl.BlockSpec(memory_space=pltpu.VMEM)
    anywhere = pl.BlockSpec(memory_space=pl.ANY)
    if fast:
        operands = [flat_params]
        results = [turned, turned, jax.ShapeDtypeStruct((size,), F32)]
        scratch = [vmem((PADDED, 128), F32)] * 4 + [
            vmem((size,), F32),
            vmem((4, 2, 2, 2, BLOCK, 128), BF16),
            vmem((4, 2, 2, 2, BLOCK, 128), BF16),
            vmem((4, 2, 2, BLOCK, 128), BF16),
            vmem((4, 3, BLOCK, 128), BF16),
            vmem((4, BLOCK, 128), BF16),
            vmem((4, BLOCK, 128), BF16),
            vmem((4, 2, 2, BLOCK, 128), BF16),
        ]
    else:
        rows = lax.all_gather(flat_params, ("utt", "tm"), axis=0, tiled=True).reshape(TOTAL, D)
        operands = [
            jnp.pad(rows[:, :128], ((0, PADDED - TOTAL), (0, 0))),
            jnp.pad(rows[:, 128:], ((0, PADDED - TOTAL), (0, 128 - TAIL))),
        ]
        results = [turned, turned, padded, padded]
        scratch = []
    others = 31 if fast else 3 + n_utt - 1
    copies = 128 + 2 * others
    scratch = scratch + [
        vmem((2, D, LOCAL), BF16),
        vmem((2, D, LOCAL), BF16),
        vmem((4, D, LOCAL), BF16),
        vmem((4, D, LOCAL), BF16),
        vmem((WIDE, D), BF16),
        vmem((LEN, D), F32),
        vmem((LEN, D), F32),
        vmem((2, D, LOCAL), F32),
        vmem((2, D, LOCAL), F32),
        vmem((len(SQUARES), D, D), BF16),
        vmem((CHUNKS, LEN, D), F32),
        vmem((CHUNKS, LEN, D), BF16),
        vmem((LEN, D), F32),
        vmem((LEN, 1), F32),
        vmem((LEN, D), BF16),
        vmem((LEN, D), F32),
        vmem((LEN, D), BF16),
        vmem((CHUNKS, ROWS, D), F32),
        vmem((CHUNKS, ROWS, D), BF16),
        vmem((LEN, D), BF16),
        vmem((LEN, D), BF16),
        vmem((HEADS, ROWS, LEN), F32),
        vmem((HEADS, ROWS, LEN), F32),
        vmem((HEADS, ROWS, WIDE), F32),
        vmem((HEADS, ROWS, WIDE), BF16),
        vmem((HEADS, ROWS, LEN), BF16),
        vmem((HEADS, ROWS, LEN), BF16),
        vmem((HEADS, HEAD_DIM, ROWS), BF16),
        vmem((HEADS, HEAD_DIM, ROWS), BF16),
        vmem((CHUNKS + 4, D, ROWS), BF16),
        vmem((D, LEN), F32),
        vmem((D, LEN), F32),
        vmem((D, WIDE), F32),
        vmem((LEN, D), F32),
        vmem((LEN, D), F32),
        vmem((ROWS + 2 * EDGE, 128), F32),
        vmem((64, 128), F32),
        vmem((ROWS + 2 * EDGE, 128), F32),
        vmem((64, 128), F32),
        vmem((288, 128), F32),
        vmem((2, ROWS, D), BF16),
        vmem((2, ROWS, D), BF16),
        vmem((2, 2, 8, 128), F32),
        vmem((2, others, 8, 128), F32),
        pltpu.SMEM((2,), jnp.int32),
        pltpu.SemaphoreType.DMA((copies,)),
        pltpu.SemaphoreType.DMA((copies,)),
        pltpu.SemaphoreType.DMA((5,)),
    ]
    got = pl.pallas_call(
        functools.partial(kernel, n_utt, fast),
        out_shape=results,
        in_specs=[anywhere] * 4
        + [anywhere if fast else in_vmem] * len(operands),
        out_specs=[in_vmem] * len(results),
        scratch_shapes=scratch,
        compiler_params=pltpu.CompilerParams(
            collective_id=0, has_side_effects=True, vmem_limit_bytes=56 * 1024 * 1024
        ),
    )(lengths, jnp.swapaxes(inputs, 1, 2), jnp.swapaxes(cotangent, 1, 2), table, *operands)
    if fast:
        out, grad, grad_params = pl.pallas_call(
            hand_over,
            out_shape=results,
            in_specs=[in_vmem] * 3,
            out_specs=[in_vmem] * 3,
        )(*got)
    else:
        out, grad = got[:2]
        rows = jnp.concatenate([got[2][:TOTAL], got[3][:TOTAL, :TAIL]], axis=1)
        grad_params = lax.psum_scatter(
            rows.reshape(-1), ("utt", "tm"), scatter_dimension=0, tiled=True
        )
    return jnp.swapaxes(out, 1, 2), jnp.swapaxes(grad, 1, 2), grad_params


def solution(mesh):
    return jax.shard_map(
        local,
        mesh=mesh,
        in_specs=(P("utt", "tm", None), P(("utt", "tm")), P("utt"), P("utt", "tm", None)),
        out_specs=(P("utt", "tm", None), P("utt", "tm", None), P(("utt", "tm"))),
        check_vma=False,
    )
```

```python
import functools
import math

import jax
import jax.numpy as jnp
import ml_dtypes
import numpy as np
from jax import lax
from jax.experimental import pallas as pl
from jax.experimental.pallas import tpu as pltpu
from jax.sharding import PartitionSpec as P

D = 144
HEADS = 4
FF = 576
KERNEL = 32
HEAD_DIM = 36
LEN = 400
EPS = 1e-05
NEGATIVE = -1e30

CHUNKS = FF // D
LEFT = (KERNEL - 1) // 2
LOCAL = 100
HALF = 200
ROWS = 240
HALO_START = LEN - ROWS
WIDE = 640
STRIP = 48
EDGE = 16
TAIL = D - 128
BLOCK = 128
MAIN = 112
LOCAL_SIZE = 110 * D

F32 = jnp.float32
BF16 = jnp.bfloat16
MESH = pl.DeviceIdType.MESH


def param_rows():
    def feed(prefix):
        return [
            (prefix + "_gain", 1),
            (prefix + "_bias", 1),
            (prefix + "_w_in", D * CHUNKS),
            (prefix + "_b_in", CHUNKS),
            (prefix + "_w_out", FF),
            (prefix + "_b_out", 1),
        ]

    middle = [
        ("att_gain", 1),
        ("att_bias", 1),
        ("query_w", D),
        ("query_b", 1),
        ("key_w", D),
        ("value_w", D),
        ("value_b", 1),
        ("pos_w", D),
        ("content_bias", 1),
        ("position_bias", 1),
        ("proj_w", D),
        ("proj_b", 1),
        ("conv_gain", 1),
        ("conv_bias", 1),
        ("point_w", 2 * D),
        ("point_b", 2),
        ("depth_w", KERNEL),
        ("batch_gain", 1),
        ("batch_bias", 1),
        ("mix_w", D),
        ("mix_b", 1),
    ]
    entries = feed("first") + middle + feed("second") + [("final_gain", 1), ("final_bias", 1)]
    rows = {}
    position = 0
    for name, count in entries:
        rows[name] = position
        position += count
    return rows, position


ROW, USED = param_rows()
TOTAL = 3520
PADDED = TOTAL + 32
SQUARES = (
    [("first_w_in", c, CHUNKS) for c in range(CHUNKS)]
    + [("first_w_out", c * D, 1) for c in range(CHUNKS)]
    + [("second_w_in", c, CHUNKS) for c in range(CHUNKS)]
    + [("second_w_out", c * D, 1) for c in range(CHUNKS)]
    + [("query_w", 0, 1), ("key_w", 0, 1), ("value_w", 0, 1), ("pos_w", 0, 1), ("proj_w", 0, 1)]
    + [("point_w", 0, 2), ("point_w", 1, 2), ("mix_w", 0, 1)]
)
SQUARE = {(name, shift): i for i, (name, shift, unused) in enumerate(SQUARES)}


def reversed_tables():
    distance = np.arange(2 * LEN - 1, dtype=np.float32) - np.float32(LEN - 1)
    steps = np.arange(D // 2, dtype=np.float32)
    frequency = np.exp(np.float32(-math.log(10000.0)) * steps * np.float32(2.0) / np.float32(D))
    angles = (distance[:, None] * frequency[None, :].astype(np.float32)).astype(np.float32)
    table = np.concatenate([np.sin(angles), np.cos(angles)], axis=1).astype(ml_dtypes.bfloat16)
    both = np.zeros((2, WIDE, D), ml_dtypes.bfloat16)
    for half in range(2):
        top = HALO_START * half + ROWS - 1 + LEN - 1
        both[half, : ROWS + LEN - 1] = table[top - (ROWS + LEN - 1) + 1 : top + 1][::-1]
    return both


def mm(a, b):
    return jnp.dot(a, b, preferred_element_type=F32)


def nt(a, b):
    return lax.dot_general(a, b, (((1,), (1,)), ((), ())), preferred_element_type=F32)


def tn(a, b):
    return lax.dot_general(a, b, (((0,), (0,)), ((), ())), preferred_element_type=F32)


def sigmoid(v):
    return 0.5 * jnp.tanh(0.5 * v) + 0.5


def silu(v):
    s = sigmoid(v)
    active = v * s
    return active, s + s * (v - active)


def mean(v):
    return jnp.sum(v, axis=1, keepdims=True) * (1.0 / D)


def normed(v):
    centered = v - mean(v)
    inverse = lax.rsqrt(mean(centered * centered) + EPS)
    return centered * inverse, inverse


def norm_back(grad, gain, scaled, inverse):
    e = grad * gain
    return inverse * (e - mean(e) - scaled * mean(e * scaled))


def colsum(v):
    return jnp.sum(v, axis=0, keepdims=True)


def join(main, tail):
    return jnp.concatenate([main, tail[:, :TAIL]], axis=1)


def kernel(n_utt, fast, lens_in, x_in, cot_in, tab, *refs):
    refs = list(refs)
    take = lambda count: [refs.pop(0) for unused in range(count)]
    if fast:
        (flat_in,) = take(1)
        out, grad_out, flat_out = take(3)
        WM, WT, GM, GT = take(4)
        (FLAT, GB, LB, R1, R2, R3, RZ, ACC) = take(8)
    else:
        WM, WT = take(2)
        out, grad_out, GM, GT = take(4)
    (XS, CS, XB, CB, TB, XF, CF, OS, IS, WS) = take(10)
    (HID1, ACT1, NRM1, INV1, LOW1, X1, A2, HID2, ACT2) = take(9)
    (KEY, VAL, PR, PD, WD, WB, LS, PB, QUT, QVT, XT, DKT, DVT, DPT, DKA, DVA, GLM, GLT, VM, VT, CT) = take(21)
    (KS, KB, BS, BB, lens, send_sem, recv_sem, local_sem) = take(8)

    utt = lax.axis_index("utt")
    tm = lax.axis_index("tm")
    x, c = tm // 2, tm % 2
    z, y = utt // 2, utt % 2
    unit, half = x, c
    start = pl.multiple_of(HALO_START * half, 16)

    used = [0]
    waits = []

    def slots(count):
        at = used[0]
        used[0] += count
        return at

    def remote(src, dst, send_at, recv_at, device):
        return pltpu.make_async_remote_copy(
            src_ref=src,
            dst_ref=dst,
            send_sem=send_sem.at[send_at],
            recv_sem=recv_sem.at[recv_at],
            device_id=device,
            device_id_type=MESH,
        )

    def send(src, dst, device, send_at=None, recv_at=None):
        if send_at is None:
            send_at = recv_at = slots(1)
        made = remote(src, dst, send_at, recv_at, device)
        made.start()
        waits.append(made)
        return made

    core_peer = (utt, 2 * x + 1 - c)
    x_peer = (utt, 2 * (1 - x) + c)
    cross_peer = (utt, 2 * (1 - x) + 1 - c)
    y_peer = (2 * z + 1 - y, tm)
    xy_peer = (2 * z + 1 - y, 2 * (1 - x) + c)
    plane = [x_peer, y_peer, xy_peer]
    plane_at = [(y, 1 - x), (1 - y, x), (1 - y, 1 - x)]
    z_at = [z, z + 1 - 2 * (z % 2), (z + 2) % 4, 3 - z]
    other_z = [j + (j - z + 4) // 4 for j in range(3)]

    barrier = pltpu.get_barrier_semaphore()
    partners = [core_peer, x_peer, cross_peer]
    if fast:
        partners += [(2 * zz + y, tm) for zz in other_z] + [y_peer, xy_peer]
    else:
        partners += [((utt + k) % n_utt, tm) for k in range(1, n_utt)]
    for partner in partners:
        pl.semaphore_signal(barrier, inc=1, device_id=partner, device_id_type=MESH)
    fetches = [
        pltpu.make_async_copy(x_in, XS, local_sem.at[0]),
        pltpu.make_async_copy(cot_in, CS, local_sem.at[1]),
        pltpu.make_async_copy(tab.at[half], TB, local_sem.at[2]),
        pltpu.make_async_copy(lens_in, lens, local_sem.at[4]),
    ]
    if fast:
        flat_fetch = pltpu.make_async_copy(flat_in, FLAT, local_sem.at[3])
        flat_fetch.start()
    for fetch in fetches:
        fetch.start()

    lane = lax.broadcasted_iota(jnp.int32, (1, 128), 1)
    lane_d = lax.broadcasted_iota(jnp.int32, (1, D), 1)

    def lanes_of(g):
        return (lane >= TAIL * g) & (lane < TAIL * (g + 1))

    def turned(v, shift):
        return v if shift % 128 == 0 else pltpu.roll(v, shift % 128, 1)

    def tails_of(rows):
        packed = jnp.zeros((16, 128), F32)
        for g in range(7):
            packed = jnp.where(lanes_of(g), turned(rows[16 * g : 16 * g + 16], TAIL * g), packed)
        return packed

    def rows_of_tails(packed):
        return jnp.concatenate([turned(packed, -TAIL * g) for g in range(7)], axis=0)

    if fast:
        own = GB.at[z, y, x, c]
        flat_fetch.wait()
        for i in range(15):
            GM[8 * i : 8 * i + 8, :] = FLAT[pl.ds(1024 * i, 1024)].reshape(8, 128)
        rest = LOCAL_SIZE - 15 * 1024
        GM[120:128, :] = jnp.concatenate(
            [FLAT[pl.ds(15 * 1024, rest)], jnp.zeros((1024 - rest,), F32)]
        ).reshape(8, 128)
        dense = [GM[pl.ds(i, 14, stride=9), :] for i in range(9)]
        for i in range(8):
            shift = TAIL * i
            left = turned(dense[i], -shift)
            right = turned(dense[i + 1], -shift)
            WM[pl.ds(i, 14, stride=8), :] = jnp.where(lane < 128 - shift, left, right)
            WT[pl.ds(i, 14, stride=8), :] = right
        own[0:MAIN, :] = WM[0:MAIN, :].astype(BF16)
        own[MAIN:BLOCK, :] = tails_of(WT[0:MAIN, :]).astype(BF16)
        col_at, p_at, c_at = slots(4), slots(12), slots(4)

        def to_column(j):
            to = (2 * z_at[3 - j] + y, tm)
            remote(own, own, col_at, col_at + z, to).start()

        def to_plane(zz, mates):
            block = GB.at[zz, y, x, c]
            for m in range(mates):
                remote(block, block, p_at, p_at + 4 * m + zz, plane[m]).start()

        def diagonal_to_column():
            block = GB.at[z, 1 - y, 1 - x, c]
            remote(block, block, p_at, p_at + 8 + z, core_peer).wait_recv()
            for j in range(3):
                to = (2 * z_at[3 - j] + y, tm)
                remote(block, block, p_at, p_at + 8 + z, to).start()
            to_core(z, (1 - y, 1 - x))

        def from_plane(zz, mates):
            for m in range(mates):
                block = GB.at[zz, plane_at[m][0], plane_at[m][1], c]
                remote(block, block, p_at, p_at + 4 * m + zz, core_peer).wait_recv()
                to_core(zz, plane_at[m])

        def diagonal_from_column(zz):
            @pl.when(z != zz)
            def _():
                block = GB.at[zz, 1 - y, 1 - x, c]
                remote(block, block, p_at, p_at + 8 + zz, core_peer).wait_recv()
                to_core(zz, (1 - y, 1 - x))

        def to_core(zz, where):
            block = GB.at[zz, where[0], where[1], c]
            remote(block, block, c_at, c_at + zz, core_peer).start()

        waits.append(remote(R2.at[0], R2.at[0], col_at, col_at, core_peer))
        waits.append(remote(R2, R2, p_at, p_at, core_peer))
        waits.append(remote(GB.at[0:2], GB.at[0:2], c_at, c_at, core_peer))

        def from_core(zz):
            blocks = GB.at[zz, :, :, 1 - c]
            remote(blocks, blocks, c_at, c_at + zz, core_peer).wait_recv()
            for low_d in range(8):
                block = GB.at[zz, low_d // 4, (low_d // 2) % 2, low_d % 2]
                first = 110 * (8 * zz + low_d)
                WM[first : first + 110, :] = block[0:110, :].astype(F32)
                WT[first : first + 110, :] = rows_of_tails(block[MAIN:BLOCK, :].astype(F32))[0:110]

    pl.semaphore_wait(barrier, len(partners))
    if fast:
        for j in range(3):
            to_column(j)

    def exchange(source, target):
        return (
            send(source.at[1 - x], target.at[tm], x_peer),
            send(source.at[x], target.at[tm], core_peer),
        )

    def relay(copies, target):
        copies[0].wait_recv()
        passed = target.at[x_peer[1]]
        return copies[1], send(passed, passed, core_peer)

    def unpack_frames(copies, source, target, frames):
        for made in copies:
            made.wait_recv()
        target[tm] = source[unit]
        for k in range(4):
            frames[LOCAL * k : LOCAL * (k + 1), :] = target[k].astype(F32).T

    fetches[0].wait()
    x_copies = exchange(XS, XB)
    if fast:
        to_plane(z, 3)
        to_core(z, (y, x))
    x_copies = relay(x_copies, XB)
    if fast:
        diagonal_to_column()
        for j in range(3):
            block = GB.at[other_z[j], y, x, c]
            remote(block, block, col_at, col_at + other_z[j], core_peer).wait_recv()
            to_plane(other_z[j], 2)
            to_core(other_z[j], (y, x))
    fetches[1].wait()
    c_copies = exchange(CS, CB)

    def rows_of(name, count=1, shift=0, stride=1):
        at = ROW[name] + shift
        s = pl.ds(at, count) if stride == 1 else pl.ds(at, count, stride=stride)
        return join(WM[s, :], WT[s, :])

    def put(name, value, shift=0, stride=1):
        at = ROW[name] + shift
        count = value.shape[0]
        if stride == 1:
            GM[pl.ds(at, count), :] = value[:, :128]
            GT[pl.ds(at, count), 0:TAIL] = value[:, 128:]
        else:
            s = pl.ds(at, count, stride=stride)
            GM[s, :] = value[:, :128]
            GT[s, :] = jnp.concatenate(
                [value[:, 128:], jnp.zeros((count, 128 - TAIL), F32)], axis=1
            )

    def ready(prefixes):
        for i, (name, shift, stride) in enumerate(SQUARES):
            if name.startswith(prefixes):
                WS[i] = rows_of(name, D, shift, stride).astype(BF16)

    def square(name, shift=0):
        return WS[SQUARE[name, shift]]

    row = lax.broadcasted_iota(jnp.int32, (ROWS, 1), 0)
    frame = row + start
    own_row = ((frame >= HALF * half) & (frame < HALF * half + HALF)).astype(F32)
    own_low = own_row.astype(BF16)
    fetches[3].wait()
    length = jnp.where(unit == 0, lens[0], lens[1])
    live = (frame < length).astype(F32)
    scale = HEAD_DIM ** (-0.5)
    window = pl.ds(start, ROWS)

    if fast:
        from_plane(0, 2)
        diagonal_from_column(0)
        from_plane(1, 2)
        diagonal_from_column(1)
        from_core(0)
        from_core(1)
    unpack_frames(x_copies, XS, XB, XF)
    ready("first")
    c_copies = relay(c_copies, CB)

    def feed(v, prefix, HID, ACT):
        scaled, inverse = normed(v)
        low = (scaled * rows_of(prefix + "_gain") + rows_of(prefix + "_bias")).astype(BF16)
        total = rows_of(prefix + "_b_out")
        for j in range(CHUNKS):
            hidden = mm(low, square(prefix + "_w_in", j)) + rows_of(prefix + "_b_in", 1, j)
            if prefix == "first":
                HID[j] = hidden
                active = hidden * sigmoid(hidden)
            else:
                active, HID[j] = silu(hidden)
            active = active.astype(BF16)
            ACT[j] = active
            total = total + mm(active, square(prefix + "_w_out", j * D))
        return total, scaled, inverse, low

    v = XF[0:LEN, :]
    total, scaled, inverse, low = feed(v, "first", HID1, ACT1)
    NRM1[...] = scaled
    INV1[...] = inverse
    LOW1[...] = low
    x1 = v + 0.5 * total
    X1[...] = x1

    if fast:
        for zz in (2, 3):
            from_plane(zz, 2)
            diagonal_from_column(zz)
        from_core(2)
    ready(("query", "key", "value", "pos_w", "proj", "point", "mix"))
    fetches[2].wait()
    scaled, inverse = normed(x1)
    low = (scaled * rows_of("att_gain") + rows_of("att_bias")).astype(BF16)
    A2[...] = low
    KEY[...] = mm(low, square("key_w")).astype(BF16)
    VAL[...] = (mm(low, square("value_w")) + rows_of("value_b")).astype(BF16)
    a2 = A2[window, :]
    query = mm(a2, square("query_w")) + rows_of("query_b")
    qu = ((query + rows_of("content_bias")) * scale).astype(BF16)
    qv = ((query + rows_of("position_bias")) * scale).astype(BF16)
    positions = mm(TB[...], square("pos_w")).astype(BF16)
    key_bias = jnp.where(
        lax.broadcasted_iota(jnp.int32, (1, LEN), 1) < length, 0.0, NEGATIVE
    )

    def head_mask(h):
        return ((lane_d >= HEAD_DIM * h) & (lane_d < HEAD_DIM * (h + 1))).astype(BF16)

    for h in range(HEADS):
        mask = head_mask(h)
        PR[h] = nt(qu * mask, KEY[...])
        WD[h] = nt(qv * mask, positions)
    context, share = jnp.zeros((ROWS, D), F32), jnp.zeros((ROWS, D), F32)
    for h in range(HEADS):
        for lo in range(0, ROWS, STRIP):
            strip = slice(lo, lo + STRIP)
            wide = pltpu.roll(WD[h, strip, :], WIDE - ROWS + 1 + lo, 1, stride=1, stride_axis=0)
            score = PR[h, strip, :] + wide[:, :LEN] + key_bias
            score = jnp.exp(score - jnp.max(score, axis=1, keepdims=True))
            PR[h, strip, :] = score
            PB[h, strip, :] = score.astype(BF16)
        mask = head_mask(h)
        context = context + mm(PB[h], VAL[...] * mask)
        share = share + mm(PB[h], jnp.broadcast_to(mask, (LEN, D)))
    context = (context / share).astype(BF16)
    x2 = X1[window, :] + mm(context, square("proj_w")) + rows_of("proj_b")

    conv_n, conv_i = normed(x2)
    a3 = (conv_n * rows_of("conv_gain") + rows_of("conv_bias")).astype(BF16)
    value = mm(a3, square("point_w", 0)) + rows_of("point_b", 1, 0)
    gate = sigmoid(mm(a3, square("point_w", 1)) + rows_of("point_b", 1, 1))
    SEGMENT = ROWS // 8

    def segments(ref, count):
        packed = turned(ref[0:count, :], 0)
        for g in range(1, 8):
            v = turned(ref[SEGMENT * g : SEGMENT * g + count, :], TAIL * g)
            packed = jnp.where(lane >= TAIL * g, v, packed)
        return packed

    def unsegmented(v):
        for g in range(8):
            CT[SEGMENT * g : SEGMENT * (g + 1), :] = turned(v, -TAIL * g)[0:SEGMENT]
        return CT[0:ROWS, :]

    def lay(v, main, tail):
        for lo, hi in ((0, EDGE), (EDGE + ROWS, 2 * EDGE + ROWS)):
            main[lo:hi, :] = jnp.zeros((hi - lo, 128), F32)
            CT[lo:hi, :] = jnp.zeros((hi - lo, 128), F32)
        main[EDGE : EDGE + ROWS, :] = v[:, :128]
        CT[EDGE : EDGE + ROWS, 0:TAIL] = v[:, 128:]
        tail[...] = segments(CT, 64)

    def convolved(main, tail, first):
        blocks = []
        for lo in range(0, ROWS, 80):
            total = depth_m[0:1] * main[pl.ds(lo + first(0), 80), :]
            for o in range(1, KERNEL):
                total = total + depth_m[o : o + 1] * main[pl.ds(lo + first(o), 80), :]
            blocks.append(total)
        total = depth_t[0:1] * tail[pl.ds(first(0), 32), :]
        for o in range(1, KERNEL):
            total = total + depth_t[o : o + 1] * tail[pl.ds(first(o), 32), :]
        return join(jnp.concatenate(blocks, axis=0), unsegmented(total))

    depth_rows = pl.ds(ROW["depth_w"], KERNEL)
    depth_m = WM[depth_rows, :]
    depth_t = jnp.where(lane < TAIL, WT[depth_rows, :], 0.0)
    for shift in (TAIL, 2 * TAIL, 4 * TAIL):
        depth_t = depth_t + turned(depth_t, shift)
    CT[2 * EDGE + ROWS :, :] = jnp.zeros((CT.shape[0] - 2 * EDGE - ROWS, 128), F32)
    lay((live * value * gate).astype(BF16).astype(F32), GLM, GLT)
    forth = lambda o: EDGE - LEFT + o
    conv = convolved(GLM, GLT, forth)

    def begin_sum(which, first, second):
        lengths = jnp.where(tm == 0, lens[0] + lens[1], 0).astype(F32)
        blank = jnp.zeros((1, 128 - TAIL), F32)
        BS[which, 0] = jnp.concatenate(
            [
                first[:, :128],
                jnp.concatenate([first[:, 128:], blank], axis=1),
                second[:, :128],
                jnp.concatenate([second[:, 128:], blank], axis=1),
                jnp.full((4, 128), lengths),
            ],
            axis=0,
        )
        if fast:
            sent, at = [], slots(1)
            for k in range(31, 0, -1):
                kz, dy, dx, dc = k // 8, (k // 4) % 2, (k // 2) % 2, k % 2
                to_y, to_x, to_c = (1 - v if d else v for v, d in ((y, dy), (x, dx), (c, dc)))
                to = (2 * z_at[kz] + to_y, 2 * to_x + to_c)
                remote(BS.at[which, 0], BB.at[which, k - 1], at, at, to).start()
            sent.append(remote(BB.at[which], BB.at[which], at, at, core_peer))
            waits.extend(sent)
        else:
            sent = [
                send(BS.at[which, 0], BB.at[which, k], mate)
                for k, mate in enumerate((x_peer, cross_peer, core_peer))
            ]
        return sent

    def end_sum(which, sent):
        def arrived(copies, at, count, total):
            for made in copies:
                made.wait_recv()
            for k in range(count):
                total = total + BB[which, at + k]
            return total

        total = arrived(sent, 0, 31 if fast else 3, BS[which, 0])
        if not fast:
            BS[which, 1] = total
            sent = [
                send(BS.at[which, 1], BB.at[which, 2 + k], ((utt + k) % n_utt, tm))
                for k in range(1, n_utt)
            ]
            total = arrived(sent, 3, n_utt - 1, total)
        return join(total[0:1], total[1:2]), join(total[2:3], total[3:4]), total[4:5, 0:1]

    counted = own_row * live
    sent = begin_sum(0, colsum(counted * conv), colsum(counted * conv * conv))
    if fast:
        from_core(3)
    ready("second")
    flip = (
        lax.broadcasted_iota(jnp.int32, (ROWS, ROWS), 0)
        + lax.broadcasted_iota(jnp.int32, (ROWS, ROWS), 1)
        == ROWS - 1
    ).astype(F32).astype(BF16)
    qu_r = mm(flip, qu).astype(BF16)
    qv_r = mm(flip, qv).astype(BF16)
    def transposed(v):
        return v.astype(F32).T.astype(BF16)

    for h in range(HEADS):
        prob = PR[h]
        prob = prob * (1.0 / jnp.sum(prob, axis=1, keepdims=True))
        high = prob.astype(BF16)
        rest = (prob - high.astype(F32)).astype(BF16)
        turned_high = mm(flip, high)
        PB[h] = turned_high.astype(BF16)
        PR[h] = turned_high + mm(flip, rest)
    for source, target in ((qu_r, QUT), (qv_r, QVT)):
        v = source.astype(F32).T
        for h in range(HEADS):
            target[h] = v[HEAD_DIM * h : HEAD_DIM * (h + 1)].astype(BF16)
    for j in range(CHUNKS):
        XT[j] = transposed(ACT1[j, window, :])
        HID1[j, 0:ROWS, :] = silu(HID1[j, window, :])[1]
    unpack_frames(c_copies, CS, CB, CF)
    for j, v in enumerate((LOW1[window, :], a2, a3, context)):
        XT[CHUNKS + j] = transposed(v)
    first_sum, second_sum, count = end_sum(0, sent)
    mu = first_sum / count
    spread = lax.rsqrt(second_sum / count - mu * mu + EPS)
    bn = (conv - mu) * spread
    zed = bn * rows_of("batch_gain") + rows_of("batch_bias")
    swished, zed_slope = silu(zed)
    swished = swished.astype(BF16)
    x3 = x2 + mm(swished, square("mix_w")) + rows_of("mix_b")

    total, second_n, second_i, second_low = feed(x3, "second", HID2, ACT2)
    x4 = x3 + 0.5 * total
    final_n, final_i = normed(x4)
    result = final_n * rows_of("final_gain") + rows_of("final_bias")

    def return_frames(v, S, B):
        send_at, recv_at = slots(2), slots(2)
        made = []
        for j in range(2):
            lo, hi = LOCAL * j, HALF - HALO_START + LOCAL * j
            S[j] = jnp.where(half == 0, v[lo : lo + LOCAL, :], v[hi : hi + LOCAL, :]).T
            made.append(
                remote(S.at[j], B.at[unit], send_at + j, recv_at + unit, (utt, 2 * half + j))
            )

        def launch():
            for j in range(2):
                away = 2 * half + j != tm

                @pl.when(away)
                def _(sent=made[j]):
                    sent.start()

                @pl.when(jnp.logical_not(away))
                def _(j=j):
                    B[unit] = S[j]

        def finish():
            for j in range(2):

                @pl.when(2 * half + j != tm)
                def _(sent=made[j]):
                    sent.wait_send()

            for u in range(2):

                @pl.when(2 * u + x != tm)
                def _(u=u):
                    remote(S.at[0], B.at[u], send_at, recv_at + u, core_peer).wait_recv()

        return launch, finish


    g0 = CF[window, :] * live
    d4 = norm_back(g0, rows_of("final_gain"), final_n, final_i)

    def feed_back(grad, prefix, slope_of, active_t, scaled, inverse, low_t, masked):
        low_grad = (0.5 * grad).astype(BF16)
        back = jnp.zeros((ROWS, D), F32)
        hidden_grads = []
        for j in range(CHUNKS):
            grad_hidden = nt(low_grad, square(prefix + "_w_out", j * D))
            grad_hidden = (grad_hidden * slope_of(j)).astype(BF16)
            hidden_grads.append(grad_hidden)
            back = back + nt(grad_hidden, square(prefix + "_w_in", j))

        def out_weights(chunks):
            kept = low_grad * own_low if masked else low_grad
            if CHUNKS - 1 in chunks:
                put(prefix + "_b_out", colsum(kept.astype(F32)))
            for j in chunks:
                put(prefix + "_w_out", mm(active_t(j), kept), j * D)

        def in_weights():
            for j in range(CHUNKS):
                grad_hidden = hidden_grads[j] * own_low if masked else hidden_grads[j]
                put(prefix + "_w_in", mm(low_t(), grad_hidden), j, CHUNKS)
                put(prefix + "_b_in", colsum(grad_hidden.astype(F32)), j)
            kept = back * own_row if masked else back
            put(prefix + "_gain", colsum(kept * scaled))
            put(prefix + "_bias", colsum(kept))

        total = grad + norm_back(back, rows_of(prefix + "_gain"), scaled, inverse)
        return total, out_weights, in_weights

    d3, second_out_weights, second_in_weights = feed_back(
        d4,
        "second",
        lambda j: HID2[j],
        lambda j: transposed(ACT2[j]),
        second_n,
        second_i,
        lambda: transposed(second_low),
        True,
    )

    if fast:
        pieces = [(0, 0, 64), (0, 64, BLOCK), (1, 0, BLOCK), (2, 0, BLOCK), (3, 0, BLOCK)]
        z_send, z_recv = slots(len(pieces)), slots(4 * len(pieces))
        stage = {}

        def add(a, b):
            return a.astype(F32) + b.astype(F32)

        def pieces_of(goal):
            return [piece for piece in pieces if piece[0] == goal]

        def begin_round(goal):
            for piece in pieces_of(goal):
                lo, hi = piece[1:]
                rows = pl.ds(lo, hi - lo)
                for d in range(8):
                    first = 110 * (8 * goal + d)
                    block = LB.at[goal, d // 4, (d // 2) % 2, d % 2]
                    top = min(hi, MAIN)
                    block[lo:top, :] = GM[first + lo : first + top, :].astype(BF16)
                    if hi == BLOCK:
                        tails = tails_of(GT[first : first + MAIN, :])
                        block[MAIN:BLOCK, :] = tails.astype(BF16)
                stage[piece] = send(
                    LB.at[goal, :, :, 1 - c, rows], R1.at[goal, :, :, rows], core_peer
                )

        def plane_round(goal):
            for piece in pieces_of(goal):
                lo, hi = piece[1:]
                rows = pl.ds(lo, hi - lo)
                stage[piece].wait_recv()
                for yy in range(2):
                    for xx in range(2):
                        both = add(LB[goal, yy, xx, c, lo:hi], R1[goal, yy, xx, lo:hi])
                        ACC[goal, yy, xx, lo:hi] = both.astype(BF16)
                at = slots(1)
                for m in range(3):
                    block = ACC.at[goal, plane_at[m][0], plane_at[m][1], rows]
                    remote(block, R2.at[goal, m, rows], at, at, plane[m]).start()
                all_three = R2.at[goal, :, rows]
                stage[piece] = remote(all_three, all_three, at, at, core_peer)
                waits.append(stage[piece])

        def z_copy(piece, sender):
            goal, lo, hi = piece
            rows, index = pl.ds(lo, hi - lo), pieces.index(piece)
            return remote(
                R3.at[goal, rows],
                RZ.at[sender, rows],
                z_send + index,
                z_recv + 4 * index + sender,
                (2 * goal + y, tm),
            )

        def z_round(goal):
            for piece in pieces_of(goal):
                lo, hi = piece[1:]
                stage[piece].wait_recv()
                total = add(ACC[goal, y, x, lo:hi], R2[goal, 0, lo:hi])
                total = total + add(R2[goal, 1, lo:hi], R2[goal, 2, lo:hi])
                R3[goal, lo:hi] = total.astype(BF16)

                @pl.when(z != goal)
                def _(piece=piece):
                    z_copy(piece, z).start()

    else:
        begin_round = plane_round = z_round = lambda goal: None

    low_grad = d3.astype(BF16)
    dzed = nt(low_grad, square("mix_w")).astype(BF16).astype(F32)
    dzed = dzed * zed_slope
    e = dzed * rows_of("batch_gain")
    e_own = e * counted
    sent = begin_sum(1, colsum(e_own), colsum(e_own * bn))
    launch_out, finish_out = return_frames(result, OS, out)
    launch_out()
    for V in (GM, GT):
        V[USED : USED + 8, :] = jnp.zeros((8, 128), F32)
    g0_own = g0 * own_row
    put("final_gain", colsum(g0_own * final_n))
    put("final_bias", colsum(g0_own))
    second_out_weights(range(CHUNKS))
    second_in_weights()
    begin_round(3)
    kept = low_grad * own_low
    put("mix_w", tn(swished, kept))
    put("mix_b", colsum(kept.astype(F32)))
    dzed_own = dzed * own_row
    put("batch_gain", colsum(dzed_own * bn))
    put("batch_bias", colsum(dzed_own))
    parts = (e, jnp.broadcast_to(live, (ROWS, D)), live * bn)
    back_parts, depth_parts = [], []
    for i, v in enumerate(parts):
        lay(v, VM, VT)
        back_parts.append(convolved(VM, VT, lambda o: EDGE + LEFT - o))
        kept = v * own_row
        kept_m = kept[:, :128]
        CT[0:ROWS, 0:TAIL] = kept[:, 128:]
        segment_row = lax.broadcasted_iota(jnp.int32, (32, 1), 0) < SEGMENT
        kept_t = jnp.where(segment_row, segments(CT, 32), 0.0)
        mains, tails = [], []
        for o in range(KERNEL):
            mains.append(colsum(kept_m * GLM[pl.ds(forth(o), ROWS), :]))
            tails.append(colsum(kept_t * GLT[pl.ds(forth(o), 32), :]))
        tails = jnp.concatenate(tails, axis=0)
        for shift in (4 * TAIL, 2 * TAIL, TAIL):
            tails = tails + turned(tails, shift)
        depth_parts.append(join(jnp.concatenate(mains, axis=0), tails))
    first_sum, second_sum, count = end_sum(1, sent)
    plane_round(3)
    first_mean, second_mean = first_sum / count, second_sum / count

    def combined(v):
        return spread * (v[0] - v[1] * first_mean - v[2] * second_mean)

    dglu = combined(back_parts).astype(BF16).astype(F32) * counted
    dvalue = (dglu * gate).astype(BF16)
    dgate = (dglu * value * gate * (1.0 - gate)).astype(BF16)
    back = nt(dvalue, square("point_w", 0)) + nt(dgate, square("point_w", 1))
    conv_back = back
    d2 = d3 * own_row + norm_back(back, rows_of("conv_gain"), conv_n, conv_i)

    low_grad = d2.astype(BF16)
    dproj = low_grad
    dctx = nt(low_grad, square("proj_w")).astype(BF16)
    dctx = mm(flip, dctx)
    dctx_t = dctx.T
    dctx = dctx.astype(BF16)
    heads = [slice(HEAD_DIM * h, HEAD_DIM * (h + 1)) for h in range(HEADS)]
    theirs = pl.ds(pl.multiple_of(HALO_START * (1 - half), 16), ROWS)
    for h in range(HEADS):
        PD[h] = nt(dctx * head_mask(h), VAL[...])
        DVT[heads[h], :] = mm(dctx_t[heads[h]].astype(BF16), PB[h])
    DVA[...] = DVT[0:D, :].T
    KS[1] = DVA[theirs, :].astype(BF16)
    value_copy = send(KS.at[1], KB.at[1], core_peer)
    for h in range(HEADS):
        for lo in range(0, ROWS, STRIP):
            strip = slice(lo, lo + STRIP)
            prob, dprob = PR[h, strip, :], PD[h, strip, :]
            dscore = prob * (dprob - jnp.sum(dprob * prob, axis=1, keepdims=True))
            LS[h, strip, :] = dscore.astype(BF16)
            wide = jnp.concatenate([dscore, jnp.zeros((STRIP, WIDE - LEN), F32)], axis=1)
            wide = pltpu.roll(wide, lo, 1, stride=1, stride_axis=0)
            WB[h, strip, :] = wide.astype(BF16)
        DKT[heads[h], :] = mm(QUT[h], LS[h])
    DKA[...] = DKT[0:D, :].T
    KS[0] = DKA[theirs, :].astype(BF16)
    key_copy = send(KS.at[0], KB.at[0], core_peer)
    du, dw = jnp.zeros((ROWS, D), F32), jnp.zeros((ROWS, D), F32)
    for h in range(HEADS):
        mask = head_mask(h)
        du = du + mm(LS[h], KEY[...] * mask)
        dw = dw + mm(WB[h], positions * mask)
    dquery = mm(flip, (scale * (du + dw)).astype(BF16)).astype(BF16)
    put("depth_w", combined(depth_parts))
    put("point_w", mm(XT[CHUNKS + 2], dvalue), 0, 2)
    put("point_w", mm(XT[CHUNKS + 2], dgate), 1, 2)
    put("point_b", colsum(dvalue.astype(F32)), 0)
    put("point_b", colsum(dgate.astype(F32)), 1)
    put("conv_gain", colsum(conv_back * conv_n))
    put("conv_bias", colsum(conv_back))
    put("proj_w", mm(XT[CHUNKS + 3], dproj))
    put("proj_b", colsum(dproj.astype(F32)))
    z_round(3)
    begin_round(2)
    key_copy.wait_recv()
    value_copy.wait_recv()
    dkey = ((DKA[window, :] + KB[0].astype(F32)) * own_row).astype(BF16)
    dval = ((DVA[window, :] + KB[1].astype(F32)) * own_row).astype(BF16)
    back = (
        nt(dquery, square("query_w"))
        + nt(dkey, square("key_w"))
        + nt(dval, square("value_w"))
    )
    att_n, att_i = normed(X1[window, :])
    att_back = back
    d1 = d2 + norm_back(back, rows_of("att_gain"), att_n, att_i)

    d0, first_out_weights, first_in_weights = feed_back(
        d1,
        "first",
        lambda j: HID1[j, 0:ROWS, :],
        lambda j: XT[j],
        NRM1[window, :],
        INV1[window, :],
        lambda: XT[CHUNKS],
        False,
    )
    first_in_weights()
    first_out_weights(range(CHUNKS - 1))
    begin_round(0)
    first_out_weights(range(CHUNKS - 1, CHUNKS))
    put("query_w", mm(XT[CHUNKS + 1], dquery))
    put("query_b", colsum(dquery.astype(F32)))
    put("key_w", mm(XT[CHUNKS + 1], dkey))
    put("value_w", mm(XT[CHUNKS + 1], dval))
    put("value_b", colsum(dval.astype(F32)))
    put("att_gain", colsum(att_back * att_n))
    put("att_bias", colsum(att_back))
    plane_round(0)
    for h in range(HEADS):
        DPT[heads[h], :] = mm(QVT[h], WB[h])
    dpos = DPT[0:D, :]
    high = dpos.astype(BF16)
    rest = (dpos - high.astype(F32)).astype(BF16)
    put("pos_w", (mm(high, TB[...]) + mm(rest, TB[...])).T)
    put("content_bias", scale * colsum(du))
    put("position_bias", scale * colsum(dw))
    begin_round(1)
    launch_grad, finish_grad = return_frames(d0, IS, grad_out)
    plane_round(2)
    plane_round(1)
    launch_grad()
    z_round(0)
    z_round(2)
    z_round(1)

    finish_out()
    finish_grad()
    for made in waits:
        made.wait_send()
    if fast:
        for piece in pieces:

            @pl.when(z != piece[0])
            def _(piece=piece):
                z_copy(piece, z).wait_send()

            @pl.when(z == piece[0])
            def _(piece=piece):
                for j in range(3):
                    z_copy(piece, other_z[j]).wait_recv()

        total = R3[z].astype(F32)
        for j in range(3):
            total = total + RZ[other_z[j]].astype(F32)
        WM[0:MAIN, :] = total[0:MAIN]
        GT[0:MAIN, :] = rows_of_tails(total[MAIN:BLOCK])
        mains = [WM[pl.ds(i, 14, stride=8), :] for i in range(8)]
        tails = [GT[pl.ds(i, 14, stride=8), :] for i in range(8)]
        for i in range(9):
            row_i = turned(tails[max(i - 1, 0)], TAIL * (i - 1))
            if i < 8:
                row_i = jnp.where(lane >= TAIL * i, turned(mains[i], TAIL * i), row_i)
            if i > 0:
                v = turned(mains[i - 1], TAIL * (i - 1))
                row_i = jnp.where(lane < TAIL * (i - 1), v, row_i)
            WT[pl.ds(i, 14, stride=9), :] = row_i
        for i in range(15):
            flat_out[pl.ds(1024 * i, 1024)] = WT[8 * i : 8 * i + 8, :].reshape(1024)
        rest = LOCAL_SIZE - 15 * 1024
        flat_out[pl.ds(15 * 1024, rest)] = WT[120:128, :].reshape(1024)[0:rest]


def hand_over(first, second, third, first_out, second_out, third_out):
    first_out[...] = first[...]
    second_out[...] = second[...]
    third_out[...] = third[...]


def local(inputs, flat_params, lengths, cotangent):
    n_utt, n_tm = lax.axis_size("utt"), lax.axis_size("tm")
    size = flat_params.shape[0]
    fast = n_utt == 8 and n_tm == 4 and size == LOCAL_SIZE
    table = jnp.asarray(reversed_tables())
    turned = jax.ShapeDtypeStruct((2, D, LOCAL), F32)
    padded = jax.ShapeDtypeStruct((PADDED, 128), F32)
    vmem = pltpu.VMEM
    in_vmem = pl.BlockSpec(memory_space=pltpu.VMEM)
    anywhere = pl.BlockSpec(memory_space=pl.ANY)
    if fast:
        operands = [flat_params]
        results = [turned, turned, jax.ShapeDtypeStruct((size,), F32)]
        scratch = [vmem((PADDED, 128), F32)] * 4 + [
            vmem((size,), F32),
            vmem((4, 2, 2, 2, BLOCK, 128), BF16),
            vmem((4, 2, 2, 2, BLOCK, 128), BF16),
            vmem((4, 2, 2, BLOCK, 128), BF16),
            vmem((4, 3, BLOCK, 128), BF16),
            vmem((4, BLOCK, 128), BF16),
            vmem((4, BLOCK, 128), BF16),
            vmem((4, 2, 2, BLOCK, 128), BF16),
        ]
    else:
        rows = lax.all_gather(flat_params, ("utt", "tm"), axis=0, tiled=True).reshape(TOTAL, D)
        operands = [
            jnp.pad(rows[:, :128], ((0, PADDED - TOTAL), (0, 0))),
            jnp.pad(rows[:, 128:], ((0, PADDED - TOTAL), (0, 128 - TAIL))),
        ]
        results = [turned, turned, padded, padded]
        scratch = []
    others = 31 if fast else 3 + n_utt - 1
    copies = 128 + 2 * others
    scratch = scratch + [
        vmem((2, D, LOCAL), BF16),
        vmem((2, D, LOCAL), BF16),
        vmem((4, D, LOCAL), BF16),
        vmem((4, D, LOCAL), BF16),
        vmem((WIDE, D), BF16),
        vmem((LEN + 8, D), F32),
        vmem((LEN + 8, D), F32),
        vmem((2, D, LOCAL), F32),
        vmem((2, D, LOCAL), F32),
        vmem((len(SQUARES), D, D), BF16),
        vmem((CHUNKS, LEN, D), F32),
        vmem((CHUNKS, LEN, D), BF16),
        vmem((LEN, D), F32),
        vmem((LEN, 1), F32),
        vmem((LEN, D), BF16),
        vmem((LEN, D), F32),
        vmem((LEN, D), BF16),
        vmem((CHUNKS, ROWS, D), F32),
        vmem((CHUNKS, ROWS, D), BF16),
        vmem((LEN, D), BF16),
        vmem((LEN, D), BF16),
        vmem((HEADS, ROWS, LEN), F32),
        vmem((HEADS, ROWS, LEN), F32),
        vmem((HEADS, ROWS, WIDE), F32),
        vmem((HEADS, ROWS, WIDE), BF16),
        vmem((HEADS, ROWS, LEN), BF16),
        vmem((HEADS, ROWS, LEN), BF16),
        vmem((HEADS, HEAD_DIM, ROWS), BF16),
        vmem((HEADS, HEAD_DIM, ROWS), BF16),
        vmem((CHUNKS + 4, D, ROWS), BF16),
        vmem((D + 8, LEN), F32),
        vmem((D + 8, LEN), F32),
        vmem((D + 8, WIDE), F32),
        vmem((LEN, D), F32),
        vmem((LEN, D), F32),
        vmem((ROWS + 2 * EDGE, 128), F32),
        vmem((64, 128), F32),
        vmem((ROWS + 2 * EDGE, 128), F32),
        vmem((64, 128), F32),
        vmem((288, 128), F32),
        vmem((2, ROWS, D), BF16),
        vmem((2, ROWS, D), BF16),
        vmem((2, 2, 8, 128), F32),
        vmem((2, others, 8, 128), F32),
        pltpu.SMEM((2,), jnp.int32),
        pltpu.SemaphoreType.DMA((copies,)),
        pltpu.SemaphoreType.DMA((copies,)),
        pltpu.SemaphoreType.DMA((5,)),
    ]
    got = pl.pallas_call(
        functools.partial(kernel, n_utt, fast),
        out_shape=results,
        in_specs=[anywhere] * 4
        + [anywhere if fast else in_vmem] * len(operands),
        out_specs=[in_vmem] * len(results),
        scratch_shapes=scratch,
        compiler_params=pltpu.CompilerParams(
            collective_id=0, has_side_effects=True, vmem_limit_bytes=56 * 1024 * 1024
        ),
    )(lengths, jnp.swapaxes(inputs, 1, 2), jnp.swapaxes(cotangent, 1, 2), table, *operands)
    if fast:
        out, grad, grad_params = pl.pallas_call(
            hand_over,
            out_shape=results,
            in_specs=[in_vmem] * 3,
            out_specs=[in_vmem] * 3,
        )(*got)
    else:
        out, grad = got[:2]
        rows = jnp.concatenate([got[2][:TOTAL], got[3][:TOTAL, :TAIL]], axis=1)
        grad_params = lax.psum_scatter(
            rows.reshape(-1), ("utt", "tm"), scatter_dimension=0, tiled=True
        )
    return jnp.swapaxes(out, 1, 2), jnp.swapaxes(grad, 1, 2), grad_params


def solution(mesh):
    return jax.shard_map(
        local,
        mesh=mesh,
        in_specs=(P("utt", "tm", None), P(("utt", "tm")), P("utt"), P("utt", "tm", None)),
        out_specs=(P("utt", "tm", None), P("utt", "tm", None), P(("utt", "tm"))),
        check_vma=False,
    )
```

```python
import functools
import math

import jax
import jax.numpy as jnp
import ml_dtypes
import numpy as np
from jax import lax
from jax.experimental import pallas as pl
from jax.experimental.pallas import tpu as pltpu
from jax.sharding import PartitionSpec as P

D = 144
HEADS = 4
FF = 576
KERNEL = 32
HEAD_DIM = 36
LEN = 400
EPS = 1e-05
NEGATIVE = -1e30

CHUNKS = FF // D
LEFT = (KERNEL - 1) // 2
LOCAL = 100
HALF = 200
ROWS = 240
HALO_START = LEN - ROWS
WIDE = 640
STRIP = 48
EDGE = 16
TAIL = D - 128
BLOCK = 128
MAIN = 112
LOCAL_SIZE = 110 * D

F32 = jnp.float32
BF16 = jnp.bfloat16
MESH = pl.DeviceIdType.MESH


def param_rows():
    def feed(prefix):
        return [
            (prefix + "_gain", 1),
            (prefix + "_bias", 1),
            (prefix + "_w_in", D * CHUNKS),
            (prefix + "_b_in", CHUNKS),
            (prefix + "_w_out", FF),
            (prefix + "_b_out", 1),
        ]

    middle = [
        ("att_gain", 1),
        ("att_bias", 1),
        ("query_w", D),
        ("query_b", 1),
        ("key_w", D),
        ("value_w", D),
        ("value_b", 1),
        ("pos_w", D),
        ("content_bias", 1),
        ("position_bias", 1),
        ("proj_w", D),
        ("proj_b", 1),
        ("conv_gain", 1),
        ("conv_bias", 1),
        ("point_w", 2 * D),
        ("point_b", 2),
        ("depth_w", KERNEL),
        ("batch_gain", 1),
        ("batch_bias", 1),
        ("mix_w", D),
        ("mix_b", 1),
    ]
    entries = feed("first") + middle + feed("second") + [("final_gain", 1), ("final_bias", 1)]
    rows = {}
    position = 0
    for name, count in entries:
        rows[name] = position
        position += count
    return rows, position


ROW, USED = param_rows()
TOTAL = 3520
PADDED = TOTAL + 32
SQUARES = (
    [("first_w_in", c, CHUNKS) for c in range(CHUNKS)]
    + [("first_w_out", c * D, 1) for c in range(CHUNKS)]
    + [("second_w_in", c, CHUNKS) for c in range(CHUNKS)]
    + [("second_w_out", c * D, 1) for c in range(CHUNKS)]
    + [("query_w", 0, 1), ("key_w", 0, 1), ("value_w", 0, 1), ("pos_w", 0, 1), ("proj_w", 0, 1)]
    + [("point_w", 0, 2), ("point_w", 1, 2), ("mix_w", 0, 1)]
)
SQUARE = {(name, shift): i for i, (name, shift, unused) in enumerate(SQUARES)}


def reversed_tables():
    distance = np.arange(2 * LEN - 1, dtype=np.float32) - np.float32(LEN - 1)
    steps = np.arange(D // 2, dtype=np.float32)
    frequency = np.exp(np.float32(-math.log(10000.0)) * steps * np.float32(2.0) / np.float32(D))
    angles = (distance[:, None] * frequency[None, :].astype(np.float32)).astype(np.float32)
    table = np.concatenate([np.sin(angles), np.cos(angles)], axis=1).astype(ml_dtypes.bfloat16)
    both = np.zeros((2, WIDE, D), ml_dtypes.bfloat16)
    for half in range(2):
        top = HALO_START * half + ROWS - 1 + LEN - 1
        both[half, : ROWS + LEN - 1] = table[top - (ROWS + LEN - 1) + 1 : top + 1][::-1]
    return both


def mm(a, b):
    return jnp.dot(a, b, preferred_element_type=F32)


def nt(a, b):
    return lax.dot_general(a, b, (((1,), (1,)), ((), ())), preferred_element_type=F32)


def tn(a, b):
    return lax.dot_general(a, b, (((0,), (0,)), ((), ())), preferred_element_type=F32)


def sigmoid(v):
    return 0.5 * jnp.tanh(0.5 * v) + 0.5


def silu(v):
    s = sigmoid(v)
    active = v * s
    return active, s + s * (v - active)


def mean(v):
    return jnp.sum(v, axis=1, keepdims=True) * (1.0 / D)


def normed(v):
    centered = v - mean(v)
    inverse = lax.rsqrt(mean(centered * centered) + EPS)
    return centered * inverse, inverse


def norm_back(grad, gain, scaled, inverse):
    e = grad * gain
    return inverse * (e - mean(e) - scaled * mean(e * scaled))


def colsum(v):
    return jnp.sum(v, axis=0, keepdims=True)


def join(main, tail):
    return jnp.concatenate([main, tail[:, :TAIL]], axis=1)


def kernel(n_utt, fast, lens_in, x_in, cot_in, tab, *refs):
    refs = list(refs)
    take = lambda count: [refs.pop(0) for unused in range(count)]
    if fast:
        (flat_in,) = take(1)
        out, grad_out, flat_out = take(3)
        WM, WT, GM, GT = take(4)
        (FLAT, GB, LB, R1, R2, R3, RZ, ACC) = take(8)
    else:
        WM, WT = take(2)
        out, grad_out, GM, GT = take(4)
    (XS, CS, XB, CB, TB, XF, CF, OS, IS, WS) = take(10)
    (HID1, ACT1, NRM1, INV1, LOW1, X1, A2, HID2, ACT2) = take(9)
    (KEY, VAL, PR, PD, WD, WB, LS, PB, QUT, QVT, XT, DKT, DVT, DPT, DKA, DVA, GLM, GLT, VM, VT, CT) = take(21)
    (KS, KB, BS, BB, lens, send_sem, recv_sem, local_sem) = take(8)

    utt = lax.axis_index("utt")
    tm = lax.axis_index("tm")
    x, c = tm // 2, tm % 2
    z, y = utt // 2, utt % 2
    unit, half = x, c
    start = pl.multiple_of(HALO_START * half, 16)

    used = [0]
    waits = []

    def slots(count):
        at = used[0]
        used[0] += count
        return at

    def remote(src, dst, send_at, recv_at, device):
        return pltpu.make_async_remote_copy(
            src_ref=src,
            dst_ref=dst,
            send_sem=send_sem.at[send_at],
            recv_sem=recv_sem.at[recv_at],
            device_id=device,
            device_id_type=MESH,
        )

    def send(src, dst, device, send_at=None, recv_at=None):
        if send_at is None:
            send_at = recv_at = slots(1)
        made = remote(src, dst, send_at, recv_at, device)
        made.start()
        waits.append(made)
        return made

    core_peer = (utt, 2 * x + 1 - c)
    x_peer = (utt, 2 * (1 - x) + c)
    cross_peer = (utt, 2 * (1 - x) + 1 - c)
    y_peer = (2 * z + 1 - y, tm)
    xy_peer = (2 * z + 1 - y, 2 * (1 - x) + c)
    plane = [x_peer, y_peer, xy_peer]
    plane_at = [(y, 1 - x), (1 - y, x), (1 - y, 1 - x)]
    z_at = [z, z + 1 - 2 * (z % 2), (z + 2) % 4, 3 - z]
    other_z = [j + (j - z + 4) // 4 for j in range(3)]

    barrier = pltpu.get_barrier_semaphore()
    partners = [core_peer, x_peer, cross_peer]
    if fast:
        partners += [(2 * zz + y, tm) for zz in other_z] + [y_peer, xy_peer]
    else:
        partners += [((utt + k) % n_utt, tm) for k in range(1, n_utt)]
    for partner in partners:
        pl.semaphore_signal(barrier, inc=1, device_id=partner, device_id_type=MESH)
    fetches = [
        pltpu.make_async_copy(x_in, XS, local_sem.at[0]),
        pltpu.make_async_copy(cot_in, CS, local_sem.at[1]),
        pltpu.make_async_copy(tab.at[half], TB, local_sem.at[2]),
        pltpu.make_async_copy(lens_in, lens, local_sem.at[4]),
    ]
    if fast:
        flat_fetch = pltpu.make_async_copy(flat_in, FLAT, local_sem.at[3])
        flat_fetch.start()
    for fetch in fetches:
        fetch.start()

    lane = lax.broadcasted_iota(jnp.int32, (1, 128), 1)
    lane_d = lax.broadcasted_iota(jnp.int32, (1, D), 1)

    def lanes_of(g):
        return (lane >= TAIL * g) & (lane < TAIL * (g + 1))

    def turned(v, shift):
        return v if shift % 128 == 0 else pltpu.roll(v, shift % 128, 1)

    def tails_of(rows):
        packed = jnp.zeros((16, 128), F32)
        for g in range(7):
            packed = jnp.where(lanes_of(g), turned(rows[16 * g : 16 * g + 16], TAIL * g), packed)
        return packed

    def rows_of_tails(packed):
        return jnp.concatenate([turned(packed, -TAIL * g) for g in range(7)], axis=0)

    if fast:
        own = GB.at[z, y, x, c]
        flat_fetch.wait()
        for i in range(15):
            GM[8 * i : 8 * i + 8, :] = FLAT[pl.ds(1024 * i, 1024)].reshape(8, 128)
        rest = LOCAL_SIZE - 15 * 1024
        GM[120:128, :] = jnp.concatenate(
            [FLAT[pl.ds(15 * 1024, rest)], jnp.zeros((1024 - rest,), F32)]
        ).reshape(8, 128)
        dense = [GM[pl.ds(i, 14, stride=9), :] for i in range(9)]
        for i in range(8):
            shift = TAIL * i
            left = turned(dense[i], -shift)
            right = turned(dense[i + 1], -shift)
            WM[pl.ds(i, 14, stride=8), :] = jnp.where(lane < 128 - shift, left, right)
            WT[pl.ds(i, 14, stride=8), :] = right
        own[0:MAIN, :] = WM[0:MAIN, :].astype(BF16)
        own[MAIN:BLOCK, :] = tails_of(WT[0:MAIN, :]).astype(BF16)
        col_at, p_at, c_at = slots(4), slots(12), slots(4)

        def to_column(j):
            to = (2 * z_at[3 - j] + y, tm)
            remote(own, own, col_at, col_at + z, to).start()

        def to_plane(zz, mates):
            block = GB.at[zz, y, x, c]
            for m in range(mates):
                remote(block, block, p_at, p_at + 4 * m + zz, plane[m]).start()

        def diagonal_to_column():
            block = GB.at[z, 1 - y, 1 - x, c]
            remote(block, block, p_at, p_at + 8 + z, core_peer).wait_recv()
            for j in range(3):
                to = (2 * z_at[3 - j] + y, tm)
                remote(block, block, p_at, p_at + 8 + z, to).start()
            to_core(z, (1 - y, 1 - x))

        def from_plane(zz, mates):
            for m in range(mates):
                block = GB.at[zz, plane_at[m][0], plane_at[m][1], c]
                remote(block, block, p_at, p_at + 4 * m + zz, core_peer).wait_recv()
                to_core(zz, plane_at[m])

        def diagonal_from_column(zz):
            @pl.when(z != zz)
            def _():
                block = GB.at[zz, 1 - y, 1 - x, c]
                remote(block, block, p_at, p_at + 8 + zz, core_peer).wait_recv()
                to_core(zz, (1 - y, 1 - x))

        def to_core(zz, where):
            block = GB.at[zz, where[0], where[1], c]
            remote(block, block, c_at, c_at + zz, core_peer).start()

        waits.append(remote(R2.at[0], R2.at[0], col_at, col_at, core_peer))
        waits.append(remote(R2, R2, p_at, p_at, core_peer))
        waits.append(remote(GB.at[0:2], GB.at[0:2], c_at, c_at, core_peer))

        def from_core(zz):
            blocks = GB.at[zz, :, :, 1 - c]
            remote(blocks, blocks, c_at, c_at + zz, core_peer).wait_recv()
            for low_d in range(8):
                block = GB.at[zz, low_d // 4, (low_d // 2) % 2, low_d % 2]
                first = 110 * (8 * zz + low_d)
                WM[first : first + 110, :] = block[0:110, :].astype(F32)
                WT[first : first + 110, :] = rows_of_tails(block[MAIN:BLOCK, :].astype(F32))[0:110]

    pl.semaphore_wait(barrier, len(partners))
    if fast:
        for j in range(3):
            to_column(j)

    def exchange(source, target):
        return (
            send(source.at[1 - x], target.at[tm], x_peer),
            send(source.at[x], target.at[tm], core_peer),
        )

    def relay(copies, target):
        copies[0].wait_recv()
        passed = target.at[x_peer[1]]
        return copies[1], send(passed, passed, core_peer)

    def unpack_frames(copies, source, target, frames):
        for made in copies:
            made.wait_recv()
        target[tm] = source[unit]
        for k in range(4):
            frames[LOCAL * k : LOCAL * (k + 1), :] = target[k].astype(F32).T

    fetches[0].wait()
    x_copies = exchange(XS, XB)
    if fast:
        to_plane(z, 3)
        to_core(z, (y, x))
    x_copies = relay(x_copies, XB)
    if fast:
        diagonal_to_column()
        for j in range(3):
            block = GB.at[other_z[j], y, x, c]
            remote(block, block, col_at, col_at + other_z[j], core_peer).wait_recv()
            to_plane(other_z[j], 2)
            to_core(other_z[j], (y, x))
    fetches[1].wait()
    c_copies = exchange(CS, CB)

    def rows_of(name, count=1, shift=0, stride=1):
        at = ROW[name] + shift
        s = pl.ds(at, count) if stride == 1 else pl.ds(at, count, stride=stride)
        return join(WM[s, :], WT[s, :])

    def put(name, value, shift=0, stride=1):
        at = ROW[name] + shift
        count = value.shape[0]
        if stride == 1:
            GM[pl.ds(at, count), :] = value[:, :128]
            GT[pl.ds(at, count), 0:TAIL] = value[:, 128:]
        else:
            s = pl.ds(at, count, stride=stride)
            GM[s, :] = value[:, :128]
            GT[s, :] = jnp.concatenate(
                [value[:, 128:], jnp.zeros((count, 128 - TAIL), F32)], axis=1
            )

    def ready(prefixes):
        for i, (name, shift, stride) in enumerate(SQUARES):
            if name.startswith(prefixes):
                WS[i] = rows_of(name, D, shift, stride).astype(BF16)

    def square(name, shift=0):
        return WS[SQUARE[name, shift]]

    row = lax.broadcasted_iota(jnp.int32, (ROWS, 1), 0)
    frame = row + start
    own_row = ((frame >= HALF * half) & (frame < HALF * half + HALF)).astype(F32)
    own_low = own_row.astype(BF16)
    fetches[3].wait()
    length = jnp.where(unit == 0, lens[0], lens[1])
    live = (frame < length).astype(F32)
    scale = HEAD_DIM ** (-0.5)
    window = pl.ds(start, ROWS)

    unpack_frames(x_copies, XS, XB, XF)
    first_norm = normed(XF[0:LEN, :])
    NRM1[...], INV1[...] = first_norm
    if fast:
        from_plane(0, 2)
        diagonal_from_column(0)
        from_plane(1, 2)
        diagonal_from_column(1)
        from_core(0)
        from_core(1)
    ready("first")
    c_copies = relay(c_copies, CB)

    def feed(scaled, prefix, HID, ACT):
        low = (scaled * rows_of(prefix + "_gain") + rows_of(prefix + "_bias")).astype(BF16)
        total = rows_of(prefix + "_b_out")
        for j in range(CHUNKS):
            hidden = mm(low, square(prefix + "_w_in", j)) + rows_of(prefix + "_b_in", 1, j)
            if prefix == "first":
                HID[j] = hidden
                active = hidden * sigmoid(hidden)
            else:
                active, HID[j] = silu(hidden)
            active = active.astype(BF16)
            ACT[j] = active
            total = total + mm(active, square(prefix + "_w_out", j * D))
        return total, low

    v = XF[0:LEN, :]
    total, low = feed(NRM1[...], "first", HID1, ACT1)
    LOW1[...] = low
    x1 = v + 0.5 * total
    X1[...] = x1

    if fast:
        for zz in (2, 3):
            from_plane(zz, 2)
            diagonal_from_column(zz)
        from_core(2)
    ready(("query", "key", "value", "pos_w", "proj", "point", "mix"))
    fetches[2].wait()
    scaled, inverse = normed(x1)
    low = (scaled * rows_of("att_gain") + rows_of("att_bias")).astype(BF16)
    A2[...] = low
    KEY[...] = mm(low, square("key_w")).astype(BF16)
    VAL[...] = (mm(low, square("value_w")) + rows_of("value_b")).astype(BF16)
    a2 = A2[window, :]
    query = mm(a2, square("query_w")) + rows_of("query_b")
    qu = ((query + rows_of("content_bias")) * scale).astype(BF16)
    qv = ((query + rows_of("position_bias")) * scale).astype(BF16)
    positions = mm(TB[...], square("pos_w")).astype(BF16)
    key_bias = jnp.where(
        lax.broadcasted_iota(jnp.int32, (1, LEN), 1) < length, 0.0, NEGATIVE
    )

    def head_mask(h):
        return ((lane_d >= HEAD_DIM * h) & (lane_d < HEAD_DIM * (h + 1))).astype(BF16)

    for h in range(HEADS):
        mask = head_mask(h)
        PR[h] = nt(qu * mask, KEY[...])
        WD[h] = nt(qv * mask, positions)
    context, share = jnp.zeros((ROWS, D), F32), jnp.zeros((ROWS, D), F32)
    for h in range(HEADS):
        for lo in range(0, ROWS, STRIP):
            strip = slice(lo, lo + STRIP)
            wide = pltpu.roll(WD[h, strip, :], WIDE - ROWS + 1 + lo, 1, stride=1, stride_axis=0)
            score = PR[h, strip, :] + wide[:, :LEN] + key_bias
            score = jnp.exp(score - jnp.max(score, axis=1, keepdims=True))
            PR[h, strip, :] = score
            PB[h, strip, :] = score.astype(BF16)
        mask = head_mask(h)
        context = context + mm(PB[h], VAL[...] * mask)
        share = share + mm(PB[h], jnp.broadcast_to(mask, (LEN, D)))
    context = (context / share).astype(BF16)
    x2 = X1[window, :] + mm(context, square("proj_w")) + rows_of("proj_b")

    conv_n, conv_i = normed(x2)
    a3 = (conv_n * rows_of("conv_gain") + rows_of("conv_bias")).astype(BF16)
    value = mm(a3, square("point_w", 0)) + rows_of("point_b", 1, 0)
    gate = sigmoid(mm(a3, square("point_w", 1)) + rows_of("point_b", 1, 1))
    SEGMENT = ROWS // 8

    def segments(ref, count):
        packed = turned(ref[0:count, :], 0)
        for g in range(1, 8):
            v = turned(ref[SEGMENT * g : SEGMENT * g + count, :], TAIL * g)
            packed = jnp.where(lane >= TAIL * g, v, packed)
        return packed

    def unsegmented(v):
        for g in range(8):
            CT[SEGMENT * g : SEGMENT * (g + 1), :] = turned(v, -TAIL * g)[0:SEGMENT]
        return CT[0:ROWS, :]

    def lay(v, main, tail):
        for lo, hi in ((0, EDGE), (EDGE + ROWS, 2 * EDGE + ROWS)):
            main[lo:hi, :] = jnp.zeros((hi - lo, 128), F32)
            CT[lo:hi, :] = jnp.zeros((hi - lo, 128), F32)
        main[EDGE : EDGE + ROWS, :] = v[:, :128]
        CT[EDGE : EDGE + ROWS, 0:TAIL] = v[:, 128:]
        tail[...] = segments(CT, 64)

    def convolved(main, tail, first):
        blocks = []
        for lo in range(0, ROWS, 80):
            total = depth_m[0:1] * main[pl.ds(lo + first(0), 80), :]
            for o in range(1, KERNEL):
                total = total + depth_m[o : o + 1] * main[pl.ds(lo + first(o), 80), :]
            blocks.append(total)
        total = depth_t[0:1] * tail[pl.ds(first(0), 32), :]
        for o in range(1, KERNEL):
            total = total + depth_t[o : o + 1] * tail[pl.ds(first(o), 32), :]
        return join(jnp.concatenate(blocks, axis=0), unsegmented(total))

    depth_rows = pl.ds(ROW["depth_w"], KERNEL)
    depth_m = WM[depth_rows, :]
    depth_t = jnp.where(lane < TAIL, WT[depth_rows, :], 0.0)
    for shift in (TAIL, 2 * TAIL, 4 * TAIL):
        depth_t = depth_t + turned(depth_t, shift)
    CT[2 * EDGE + ROWS :, :] = jnp.zeros((CT.shape[0] - 2 * EDGE - ROWS, 128), F32)
    lay((live * value * gate).astype(BF16).astype(F32), GLM, GLT)
    forth = lambda o: EDGE - LEFT + o
    conv = convolved(GLM, GLT, forth)

    def begin_sum(which, first, second):
        lengths = jnp.where(tm == 0, lens[0] + lens[1], 0).astype(F32)
        blank = jnp.zeros((1, 128 - TAIL), F32)
        BS[which, 0] = jnp.concatenate(
            [
                first[:, :128],
                jnp.concatenate([first[:, 128:], blank], axis=1),
                second[:, :128],
                jnp.concatenate([second[:, 128:], blank], axis=1),
                jnp.full((4, 128), lengths),
            ],
            axis=0,
        )
        if fast:
            sent, at = [], slots(1)
            for k in range(31, 0, -1):
                kz, dy, dx, dc = k // 8, (k // 4) % 2, (k // 2) % 2, k % 2
                to_y, to_x, to_c = (1 - v if d else v for v, d in ((y, dy), (x, dx), (c, dc)))
                to = (2 * z_at[kz] + to_y, 2 * to_x + to_c)
                remote(BS.at[which, 0], BB.at[which, k - 1], at, at, to).start()
            sent.append(remote(BB.at[which], BB.at[which], at, at, core_peer))
            waits.extend(sent)
        else:
            sent = [
                send(BS.at[which, 0], BB.at[which, k], mate)
                for k, mate in enumerate((x_peer, cross_peer, core_peer))
            ]
        return sent

    def end_sum(which, sent):
        def arrived(copies, at, count, total):
            for made in copies:
                made.wait_recv()
            for k in range(count):
                total = total + BB[which, at + k]
            return total

        total = arrived(sent, 0, 31 if fast else 3, BS[which, 0])
        if not fast:
            BS[which, 1] = total
            sent = [
                send(BS.at[which, 1], BB.at[which, 2 + k], ((utt + k) % n_utt, tm))
                for k in range(1, n_utt)
            ]
            total = arrived(sent, 3, n_utt - 1, total)
        return join(total[0:1], total[1:2]), join(total[2:3], total[3:4]), total[4:5, 0:1]

    counted = own_row * live
    sent = begin_sum(0, colsum(counted * conv), colsum(counted * conv * conv))
    if fast:
        from_core(3)
    ready("second")
    flip = (
        lax.broadcasted_iota(jnp.int32, (ROWS, ROWS), 0)
        + lax.broadcasted_iota(jnp.int32, (ROWS, ROWS), 1)
        == ROWS - 1
    ).astype(F32).astype(BF16)
    qu_r = mm(flip, qu).astype(BF16)
    qv_r = mm(flip, qv).astype(BF16)
    def transposed(v):
        return v.astype(F32).T.astype(BF16)

    for h in range(HEADS):
        prob = PR[h]
        prob = prob * (1.0 / jnp.sum(prob, axis=1, keepdims=True))
        high = prob.astype(BF16)
        rest = (prob - high.astype(F32)).astype(BF16)
        turned_high = mm(flip, high)
        PB[h] = turned_high.astype(BF16)
        PR[h] = turned_high + mm(flip, rest)
    for source, target in ((qu_r, QUT), (qv_r, QVT)):
        v = source.astype(F32).T
        for h in range(HEADS):
            target[h] = v[HEAD_DIM * h : HEAD_DIM * (h + 1)].astype(BF16)
    for j in range(CHUNKS):
        XT[j] = transposed(ACT1[j, window, :])
        HID1[j, 0:ROWS, :] = silu(HID1[j, window, :])[1]
    unpack_frames(c_copies, CS, CB, CF)
    for j, v in enumerate((LOW1[window, :], a2, a3, context)):
        XT[CHUNKS + j] = transposed(v)
    first_sum, second_sum, count = end_sum(0, sent)
    mu = first_sum / count
    spread = lax.rsqrt(second_sum / count - mu * mu + EPS)
    bn = (conv - mu) * spread
    zed = bn * rows_of("batch_gain") + rows_of("batch_bias")
    swished, zed_slope = silu(zed)
    swished = swished.astype(BF16)
    x3 = x2 + mm(swished, square("mix_w")) + rows_of("mix_b")

    second_n, second_i = normed(x3)
    total, second_low = feed(second_n, "second", HID2, ACT2)
    x4 = x3 + 0.5 * total
    final_n, final_i = normed(x4)
    result = final_n * rows_of("final_gain") + rows_of("final_bias")

    def return_frames(v, S, B):
        send_at, recv_at = slots(2), slots(2)
        made = []
        for j in range(2):
            lo, hi = LOCAL * j, HALF - HALO_START + LOCAL * j
            S[j] = jnp.where(half == 0, v[lo : lo + LOCAL, :], v[hi : hi + LOCAL, :]).T
            made.append(
                remote(S.at[j], B.at[unit], send_at + j, recv_at + unit, (utt, 2 * half + j))
            )

        def launch():
            for j in range(2):
                away = 2 * half + j != tm

                @pl.when(away)
                def _(sent=made[j]):
                    sent.start()

                @pl.when(jnp.logical_not(away))
                def _(j=j):
                    B[unit] = S[j]

        def finish():
            for j in range(2):

                @pl.when(2 * half + j != tm)
                def _(sent=made[j]):
                    sent.wait_send()

            for u in range(2):

                @pl.when(2 * u + x != tm)
                def _(u=u):
                    remote(S.at[0], B.at[u], send_at, recv_at + u, core_peer).wait_recv()

        return launch, finish


    g0 = CF[window, :] * live
    d4 = norm_back(g0, rows_of("final_gain"), final_n, final_i)

    def feed_back(grad, prefix, slope_of, active_t, scaled, inverse, low_t, masked):
        low_grad = (0.5 * grad).astype(BF16)
        back = jnp.zeros((ROWS, D), F32)
        hidden_grads = []
        for j in range(CHUNKS):
            grad_hidden = nt(low_grad, square(prefix + "_w_out", j * D))
            grad_hidden = (grad_hidden * slope_of(j)).astype(BF16)
            hidden_grads.append(grad_hidden)
            back = back + nt(grad_hidden, square(prefix + "_w_in", j))

        def out_weights(chunks):
            kept = low_grad * own_low if masked else low_grad
            if CHUNKS - 1 in chunks:
                put(prefix + "_b_out", colsum(kept.astype(F32)))
            for j in chunks:
                put(prefix + "_w_out", mm(active_t(j), kept), j * D)

        def in_weights():
            for j in range(CHUNKS):
                grad_hidden = hidden_grads[j] * own_low if masked else hidden_grads[j]
                put(prefix + "_w_in", mm(low_t(), grad_hidden), j, CHUNKS)
                put(prefix + "_b_in", colsum(grad_hidden.astype(F32)), j)
            kept = back * own_row if masked else back
            put(prefix + "_gain", colsum(kept * scaled))
            put(prefix + "_bias", colsum(kept))

        total = grad + norm_back(back, rows_of(prefix + "_gain"), scaled, inverse)
        return total, out_weights, in_weights

    d3, second_out_weights, second_in_weights = feed_back(
        d4,
        "second",
        lambda j: HID2[j],
        lambda j: transposed(ACT2[j]),
        second_n,
        second_i,
        lambda: transposed(second_low),
        True,
    )

    if fast:
        pieces = [(0, 0, 64), (0, 64, BLOCK), (1, 0, BLOCK), (2, 0, BLOCK), (3, 0, BLOCK)]
        z_send, z_recv = slots(len(pieces)), slots(4 * len(pieces))
        stage = {}

        def add(a, b):
            return a.astype(F32) + b.astype(F32)

        def pieces_of(goal):
            return [piece for piece in pieces if piece[0] == goal]

        def begin_round(goal):
            for piece in pieces_of(goal):
                lo, hi = piece[1:]
                rows = pl.ds(lo, hi - lo)
                for d in range(8):
                    first = 110 * (8 * goal + d)
                    block = LB.at[goal, d // 4, (d // 2) % 2, d % 2]
                    top = min(hi, MAIN)
                    block[lo:top, :] = GM[first + lo : first + top, :].astype(BF16)
                    if hi == BLOCK:
                        tails = tails_of(GT[first : first + MAIN, :])
                        block[MAIN:BLOCK, :] = tails.astype(BF16)
                stage[piece] = send(
                    LB.at[goal, :, :, 1 - c, rows], R1.at[goal, :, :, rows], core_peer
                )

        def plane_round(goal):
            for piece in pieces_of(goal):
                lo, hi = piece[1:]
                rows = pl.ds(lo, hi - lo)
                stage[piece].wait_recv()
                for yy in range(2):
                    for xx in range(2):
                        both = add(LB[goal, yy, xx, c, lo:hi], R1[goal, yy, xx, lo:hi])
                        ACC[goal, yy, xx, lo:hi] = both.astype(BF16)
                at = slots(1)
                for m in range(3):
                    block = ACC.at[goal, plane_at[m][0], plane_at[m][1], rows]
                    remote(block, R2.at[goal, m, rows], at, at, plane[m]).start()
                all_three = R2.at[goal, :, rows]
                stage[piece] = remote(all_three, all_three, at, at, core_peer)
                waits.append(stage[piece])

        def z_copy(piece, sender):
            goal, lo, hi = piece
            rows, index = pl.ds(lo, hi - lo), pieces.index(piece)
            return remote(
                R3.at[goal, rows],
                RZ.at[sender, rows],
                z_send + index,
                z_recv + 4 * index + sender,
                (2 * goal + y, tm),
            )

        def z_round(goal):
            for piece in pieces_of(goal):
                lo, hi = piece[1:]
                stage[piece].wait_recv()
                total = add(ACC[goal, y, x, lo:hi], R2[goal, 0, lo:hi])
                total = total + add(R2[goal, 1, lo:hi], R2[goal, 2, lo:hi])
                R3[goal, lo:hi] = total.astype(BF16)

                @pl.when(z != goal)
                def _(piece=piece):
                    z_copy(piece, z).start()

    else:
        begin_round = plane_round = z_round = lambda goal: None

    low_grad = d3.astype(BF16)
    dzed = nt(low_grad, square("mix_w")).astype(BF16).astype(F32)
    dzed = dzed * zed_slope
    e = dzed * rows_of("batch_gain")
    e_own = e * counted
    sent = begin_sum(1, colsum(e_own), colsum(e_own * bn))
    launch_out, finish_out = return_frames(result, OS, out)
    launch_out()
    for V in (GM, GT):
        V[USED : USED + 8, :] = jnp.zeros((8, 128), F32)
    g0_own = g0 * own_row
    put("final_gain", colsum(g0_own * final_n))
    put("final_bias", colsum(g0_own))
    second_out_weights(range(CHUNKS))
    second_in_weights()
    begin_round(3)
    kept = low_grad * own_low
    put("mix_w", tn(swished, kept))
    put("mix_b", colsum(kept.astype(F32)))
    dzed_own = dzed * own_row
    put("batch_gain", colsum(dzed_own * bn))
    put("batch_bias", colsum(dzed_own))
    parts = (e, jnp.broadcast_to(live, (ROWS, D)), live * bn)
    back_parts, depth_parts = [], []
    for i, v in enumerate(parts):
        lay(v, VM, VT)
        back_parts.append(convolved(VM, VT, lambda o: EDGE + LEFT - o))
        kept = v * own_row
        kept_m = kept[:, :128]
        CT[0:ROWS, 0:TAIL] = kept[:, 128:]
        segment_row = lax.broadcasted_iota(jnp.int32, (32, 1), 0) < SEGMENT
        kept_t = jnp.where(segment_row, segments(CT, 32), 0.0)
        mains, tails = [], []
        for o in range(KERNEL):
            mains.append(colsum(kept_m * GLM[pl.ds(forth(o), ROWS), :]))
            tails.append(colsum(kept_t * GLT[pl.ds(forth(o), 32), :]))
        tails = jnp.concatenate(tails, axis=0)
        for shift in (4 * TAIL, 2 * TAIL, TAIL):
            tails = tails + turned(tails, shift)
        depth_parts.append(join(jnp.concatenate(mains, axis=0), tails))
    first_sum, second_sum, count = end_sum(1, sent)
    plane_round(3)
    first_mean, second_mean = first_sum / count, second_sum / count

    def combined(v):
        return spread * (v[0] - v[1] * first_mean - v[2] * second_mean)

    dglu = combined(back_parts).astype(BF16).astype(F32) * counted
    dvalue = (dglu * gate).astype(BF16)
    dgate = (dglu * value * gate * (1.0 - gate)).astype(BF16)
    back = nt(dvalue, square("point_w", 0)) + nt(dgate, square("point_w", 1))
    conv_back = back
    d2 = d3 * own_row + norm_back(back, rows_of("conv_gain"), conv_n, conv_i)

    low_grad = d2.astype(BF16)
    dproj = low_grad
    dctx = nt(low_grad, square("proj_w")).astype(BF16)
    dctx = mm(flip, dctx)
    dctx_t = dctx.T
    dctx = dctx.astype(BF16)
    heads = [slice(HEAD_DIM * h, HEAD_DIM * (h + 1)) for h in range(HEADS)]
    theirs = pl.ds(pl.multiple_of(HALO_START * (1 - half), 16), ROWS)
    for h in range(HEADS):
        PD[h] = nt(dctx * head_mask(h), VAL[...])
        DVT[heads[h], :] = mm(dctx_t[heads[h]].astype(BF16), PB[h])
    DVA[...] = DVT[0:D, :].T
    KS[1] = DVA[theirs, :].astype(BF16)
    value_copy = send(KS.at[1], KB.at[1], core_peer)
    for h in range(HEADS):
        for lo in range(0, ROWS, STRIP):
            strip = slice(lo, lo + STRIP)
            prob, dprob = PR[h, strip, :], PD[h, strip, :]
            dscore = prob * (dprob - jnp.sum(dprob * prob, axis=1, keepdims=True))
            LS[h, strip, :] = dscore.astype(BF16)
            wide = jnp.concatenate([dscore, jnp.zeros((STRIP, WIDE - LEN), F32)], axis=1)
            wide = pltpu.roll(wide, lo, 1, stride=1, stride_axis=0)
            WB[h, strip, :] = wide.astype(BF16)
        DKT[heads[h], :] = mm(QUT[h], LS[h])
    DKA[...] = DKT[0:D, :].T
    KS[0] = DKA[theirs, :].astype(BF16)
    key_copy = send(KS.at[0], KB.at[0], core_peer)
    du, dw = jnp.zeros((ROWS, D), F32), jnp.zeros((ROWS, D), F32)
    for h in range(HEADS):
        mask = head_mask(h)
        du = du + mm(LS[h], KEY[...] * mask)
        dw = dw + mm(WB[h], positions * mask)
    dquery = mm(flip, (scale * (du + dw)).astype(BF16)).astype(BF16)
    put("depth_w", combined(depth_parts))
    put("point_w", mm(XT[CHUNKS + 2], dvalue), 0, 2)
    put("point_w", mm(XT[CHUNKS + 2], dgate), 1, 2)
    put("point_b", colsum(dvalue.astype(F32)), 0)
    put("point_b", colsum(dgate.astype(F32)), 1)
    put("conv_gain", colsum(conv_back * conv_n))
    put("conv_bias", colsum(conv_back))
    put("proj_w", mm(XT[CHUNKS + 3], dproj))
    put("proj_b", colsum(dproj.astype(F32)))
    z_round(3)
    begin_round(2)
    key_copy.wait_recv()
    value_copy.wait_recv()
    dkey = ((DKA[window, :] + KB[0].astype(F32)) * own_row).astype(BF16)
    dval = ((DVA[window, :] + KB[1].astype(F32)) * own_row).astype(BF16)
    back = (
        nt(dquery, square("query_w"))
        + nt(dkey, square("key_w"))
        + nt(dval, square("value_w"))
    )
    att_n, att_i = normed(X1[window, :])
    att_back = back
    d1 = d2 + norm_back(back, rows_of("att_gain"), att_n, att_i)

    d0, first_out_weights, first_in_weights = feed_back(
        d1,
        "first",
        lambda j: HID1[j, 0:ROWS, :],
        lambda j: XT[j],
        NRM1[window, :],
        INV1[window, :],
        lambda: XT[CHUNKS],
        False,
    )
    first_in_weights()
    first_out_weights(range(CHUNKS - 1))
    begin_round(0)
    first_out_weights(range(CHUNKS - 1, CHUNKS))
    put("query_w", mm(XT[CHUNKS + 1], dquery))
    put("query_b", colsum(dquery.astype(F32)))
    put("key_w", mm(XT[CHUNKS + 1], dkey))
    put("value_w", mm(XT[CHUNKS + 1], dval))
    put("value_b", colsum(dval.astype(F32)))
    put("att_gain", colsum(att_back * att_n))
    put("att_bias", colsum(att_back))
    plane_round(0)
    for h in range(HEADS):
        DPT[heads[h], :] = mm(QVT[h], WB[h])
    dpos = DPT[0:D, :]
    high = dpos.astype(BF16)
    rest = (dpos - high.astype(F32)).astype(BF16)
    put("pos_w", (mm(high, TB[...]) + mm(rest, TB[...])).T)
    put("content_bias", scale * colsum(du))
    put("position_bias", scale * colsum(dw))
    begin_round(1)
    launch_grad, finish_grad = return_frames(d0, IS, grad_out)
    plane_round(2)
    plane_round(1)
    launch_grad()
    z_round(0)
    z_round(2)
    z_round(1)

    finish_out()
    finish_grad()
    for made in waits:
        made.wait_send()
    if fast:
        for piece in pieces:

            @pl.when(z != piece[0])
            def _(piece=piece):
                z_copy(piece, z).wait_send()

            @pl.when(z == piece[0])
            def _(piece=piece):
                for j in range(3):
                    z_copy(piece, other_z[j]).wait_recv()

        total = R3[z].astype(F32)
        for j in range(3):
            total = total + RZ[other_z[j]].astype(F32)
        WM[0:MAIN, :] = total[0:MAIN]
        GT[0:MAIN, :] = rows_of_tails(total[MAIN:BLOCK])
        mains = [WM[pl.ds(i, 14, stride=8), :] for i in range(8)]
        tails = [GT[pl.ds(i, 14, stride=8), :] for i in range(8)]
        for i in range(9):
            row_i = turned(tails[max(i - 1, 0)], TAIL * (i - 1))
            if i < 8:
                row_i = jnp.where(lane >= TAIL * i, turned(mains[i], TAIL * i), row_i)
            if i > 0:
                v = turned(mains[i - 1], TAIL * (i - 1))
                row_i = jnp.where(lane < TAIL * (i - 1), v, row_i)
            WT[pl.ds(i, 14, stride=9), :] = row_i
        for i in range(15):
            flat_out[pl.ds(1024 * i, 1024)] = WT[8 * i : 8 * i + 8, :].reshape(1024)
        rest = LOCAL_SIZE - 15 * 1024
        flat_out[pl.ds(15 * 1024, rest)] = WT[120:128, :].reshape(1024)[0:rest]


def hand_over(first, second, third, first_out, second_out, third_out):
    first_out[...] = first[...]
    second_out[...] = second[...]
    third_out[...] = third[...]


def local(inputs, flat_params, lengths, cotangent):
    n_utt, n_tm = lax.axis_size("utt"), lax.axis_size("tm")
    size = flat_params.shape[0]
    fast = n_utt == 8 and n_tm == 4 and size == LOCAL_SIZE
    table = jnp.asarray(reversed_tables())
    turned = jax.ShapeDtypeStruct((2, D, LOCAL), F32)
    padded = jax.ShapeDtypeStruct((PADDED, 128), F32)
    vmem = pltpu.VMEM
    in_vmem = pl.BlockSpec(memory_space=pltpu.VMEM)
    anywhere = pl.BlockSpec(memory_space=pl.ANY)
    if fast:
        operands = [flat_params]
        results = [turned, turned, jax.ShapeDtypeStruct((size,), F32)]
        scratch = [vmem((PADDED, 128), F32)] * 4 + [
            vmem((size,), F32),
            vmem((4, 2, 2, 2, BLOCK, 128), BF16),
            vmem((4, 2, 2, 2, BLOCK, 128), BF16),
            vmem((4, 2, 2, BLOCK, 128), BF16),
            vmem((4, 3, BLOCK, 128), BF16),
            vmem((4, BLOCK, 128), BF16),
            vmem((4, BLOCK, 128), BF16),
            vmem((4, 2, 2, BLOCK, 128), BF16),
        ]
    else:
        rows = lax.all_gather(flat_params, ("utt", "tm"), axis=0, tiled=True).reshape(TOTAL, D)
        operands = [
            jnp.pad(rows[:, :128], ((0, PADDED - TOTAL), (0, 0))),
            jnp.pad(rows[:, 128:], ((0, PADDED - TOTAL), (0, 128 - TAIL))),
        ]
        results = [turned, turned, padded, padded]
        scratch = []
    others = 31 if fast else 3 + n_utt - 1
    copies = 128 + 2 * others
    scratch = scratch + [
        vmem((2, D, LOCAL), BF16),
        vmem((2, D, LOCAL), BF16),
        vmem((4, D, LOCAL), BF16),
        vmem((4, D, LOCAL), BF16),
        vmem((WIDE, D), BF16),
        vmem((LEN + 8, D), F32),
        vmem((LEN + 8, D), F32),
        vmem((2, D, LOCAL), F32),
        vmem((2, D, LOCAL), F32),
        vmem((len(SQUARES), D, D), BF16),
        vmem((CHUNKS, LEN, D), F32),
        vmem((CHUNKS, LEN, D), BF16),
        vmem((LEN, D), F32),
        vmem((LEN, 1), F32),
        vmem((LEN, D), BF16),
        vmem((LEN, D), F32),
        vmem((LEN, D), BF16),
        vmem((CHUNKS, ROWS, D), F32),
        vmem((CHUNKS, ROWS, D), BF16),
        vmem((LEN, D), BF16),
        vmem((LEN, D), BF16),
        vmem((HEADS, ROWS, LEN), F32),
        vmem((HEADS, ROWS, LEN), F32),
        vmem((HEADS, ROWS, WIDE), F32),
        vmem((HEADS, ROWS, WIDE), BF16),
        vmem((HEADS, ROWS, LEN), BF16),
        vmem((HEADS, ROWS, LEN), BF16),
        vmem((HEADS, HEAD_DIM, ROWS), BF16),
        vmem((HEADS, HEAD_DIM, ROWS), BF16),
        vmem((CHUNKS + 4, D, ROWS), BF16),
        vmem((D + 8, LEN), F32),
        vmem((D + 8, LEN), F32),
        vmem((D + 8, WIDE), F32),
        vmem((LEN, D), F32),
        vmem((LEN, D), F32),
        vmem((ROWS + 2 * EDGE, 128), F32),
        vmem((64, 128), F32),
        vmem((ROWS + 2 * EDGE, 128), F32),
        vmem((64, 128), F32),
        vmem((288, 128), F32),
        vmem((2, ROWS, D), BF16),
        vmem((2, ROWS, D), BF16),
        vmem((2, 2, 8, 128), F32),
        vmem((2, others, 8, 128), F32),
        pltpu.SMEM((2,), jnp.int32),
        pltpu.SemaphoreType.DMA((copies,)),
        pltpu.SemaphoreType.DMA((copies,)),
        pltpu.SemaphoreType.DMA((5,)),
    ]
    got = pl.pallas_call(
        functools.partial(kernel, n_utt, fast),
        out_shape=results,
        in_specs=[anywhere] * 4
        + [anywhere if fast else in_vmem] * len(operands),
        out_specs=[in_vmem] * len(results),
        scratch_shapes=scratch,
        compiler_params=pltpu.CompilerParams(
            collective_id=0, has_side_effects=True, vmem_limit_bytes=56 * 1024 * 1024
        ),
    )(lengths, jnp.swapaxes(inputs, 1, 2), jnp.swapaxes(cotangent, 1, 2), table, *operands)
    if fast:
        out, grad, grad_params = pl.pallas_call(
            hand_over,
            out_shape=results,
            in_specs=[in_vmem] * 3,
            out_specs=[in_vmem] * 3,
        )(*got)
    else:
        out, grad = got[:2]
        rows = jnp.concatenate([got[2][:TOTAL], got[3][:TOTAL, :TAIL]], axis=1)
        grad_params = lax.psum_scatter(
            rows.reshape(-1), ("utt", "tm"), scatter_dimension=0, tiled=True
        )
    return jnp.swapaxes(out, 1, 2), jnp.swapaxes(grad, 1, 2), grad_params


def solution(mesh):
    return jax.shard_map(
        local,
        mesh=mesh,
        in_specs=(P("utt", "tm", None), P(("utt", "tm")), P("utt"), P("utt", "tm", None)),
        out_specs=(P("utt", "tm", None), P("utt", "tm", None), P(("utt", "tm"))),
        check_vma=False,
    )
```

```python
import functools
import math

import jax
import jax.numpy as jnp
import ml_dtypes
import numpy as np
from jax import lax
from jax.experimental import pallas as pl
from jax.experimental.pallas import tpu as pltpu
from jax.sharding import PartitionSpec as P

D = 144
HEADS = 4
FF = 576
KERNEL = 32
HEAD_DIM = 36
LEN = 400
EPS = 1e-05
NEGATIVE = -1e30

CHUNKS = FF // D
LEFT = (KERNEL - 1) // 2
LOCAL = 100
HALF = 200
ROWS = 240
HALO_START = LEN - ROWS
WIDE = 640
STRIP = 48
EDGE = 16
TAIL = D - 128
BLOCK = 128
MAIN = 112
LOCAL_SIZE = 110 * D

F32 = jnp.float32
BF16 = jnp.bfloat16
MESH = pl.DeviceIdType.MESH


def param_rows():
    def feed(prefix):
        return [
            (prefix + "_gain", 1),
            (prefix + "_bias", 1),
            (prefix + "_w_in", D * CHUNKS),
            (prefix + "_b_in", CHUNKS),
            (prefix + "_w_out", FF),
            (prefix + "_b_out", 1),
        ]

    middle = [
        ("att_gain", 1),
        ("att_bias", 1),
        ("query_w", D),
        ("query_b", 1),
        ("key_w", D),
        ("value_w", D),
        ("value_b", 1),
        ("pos_w", D),
        ("content_bias", 1),
        ("position_bias", 1),
        ("proj_w", D),
        ("proj_b", 1),
        ("conv_gain", 1),
        ("conv_bias", 1),
        ("point_w", 2 * D),
        ("point_b", 2),
        ("depth_w", KERNEL),
        ("batch_gain", 1),
        ("batch_bias", 1),
        ("mix_w", D),
        ("mix_b", 1),
    ]
    entries = feed("first") + middle + feed("second") + [("final_gain", 1), ("final_bias", 1)]
    rows = {}
    position = 0
    for name, count in entries:
        rows[name] = position
        position += count
    return rows, position


ROW, USED = param_rows()
TOTAL = 3520
PADDED = TOTAL + 32
SQUARES = (
    [("first_w_in", c, CHUNKS) for c in range(CHUNKS)]
    + [("first_w_out", c * D, 1) for c in range(CHUNKS)]
    + [("second_w_in", c, CHUNKS) for c in range(CHUNKS)]
    + [("second_w_out", c * D, 1) for c in range(CHUNKS)]
    + [("query_w", 0, 1), ("key_w", 0, 1), ("value_w", 0, 1), ("pos_w", 0, 1), ("proj_w", 0, 1)]
    + [("point_w", 0, 2), ("point_w", 1, 2), ("mix_w", 0, 1)]
)
SQUARE = {(name, shift): i for i, (name, shift, unused) in enumerate(SQUARES)}


def reversed_tables():
    distance = np.arange(2 * LEN - 1, dtype=np.float32) - np.float32(LEN - 1)
    steps = np.arange(D // 2, dtype=np.float32)
    frequency = np.exp(np.float32(-math.log(10000.0)) * steps * np.float32(2.0) / np.float32(D))
    angles = (distance[:, None] * frequency[None, :].astype(np.float32)).astype(np.float32)
    table = np.concatenate([np.sin(angles), np.cos(angles)], axis=1).astype(ml_dtypes.bfloat16)
    both = np.zeros((2, WIDE, D), ml_dtypes.bfloat16)
    for half in range(2):
        top = HALO_START * half + ROWS - 1 + LEN - 1
        both[half, : ROWS + LEN - 1] = table[top - (ROWS + LEN - 1) + 1 : top + 1][::-1]
    return both


def mm(a, b):
    return jnp.dot(a, b, preferred_element_type=F32)


def nt(a, b):
    return lax.dot_general(a, b, (((1,), (1,)), ((), ())), preferred_element_type=F32)


def tn(a, b):
    return lax.dot_general(a, b, (((0,), (0,)), ((), ())), preferred_element_type=F32)


def sigmoid(v):
    return 0.5 * jnp.tanh(0.5 * v) + 0.5


def silu(v):
    s = sigmoid(v)
    active = v * s
    return active, s + s * (v - active)


def mean(v):
    return jnp.sum(v, axis=1, keepdims=True) * (1.0 / D)


def normed(v):
    centered = v - mean(v)
    inverse = lax.rsqrt(mean(centered * centered) + EPS)
    return centered * inverse, inverse


def norm_back(grad, gain, scaled, inverse):
    e = grad * gain
    return inverse * (e - mean(e) - scaled * mean(e * scaled))


def colsum(v):
    return jnp.sum(v, axis=0, keepdims=True)


def join(main, tail):
    return jnp.concatenate([main, tail[:, :TAIL]], axis=1)


def kernel(n_utt, fast, lens_in, x_in, cot_in, tab, *refs):
    refs = list(refs)
    take = lambda count: [refs.pop(0) for unused in range(count)]
    if fast:
        (flat_in,) = take(1)
        out, grad_out, flat_out = take(3)
        WM, WT, GM, GT = take(4)
        (FLAT, GB, LB, R1, R2, R3, RZ, ACC) = take(8)
    else:
        WM, WT = take(2)
        out, grad_out, GM, GT = take(4)
    (XS, CS, XB, CB, TB, XF, CF, OS, IS, WS) = take(10)
    (HID1, ACT1, NRM1, INV1, LOW1, X1, A2, HID2, ACT2) = take(9)
    (KEY, VAL, PR, PD, WD, WB, LS, PB, QUT, QVT, XT, DKT, DVT, DPT, DKA, DVA, GLM, GLT, VM, VT, CT) = take(21)
    (KS, KB, BS, BB, lens, send_sem, recv_sem, local_sem) = take(8)

    utt = lax.axis_index("utt")
    tm = lax.axis_index("tm")
    x, c = tm // 2, tm % 2
    z, y = utt // 2, utt % 2
    unit, half = x, c
    start = pl.multiple_of(HALO_START * half, 16)

    used = [0]
    waits = []

    def slots(count):
        at = used[0]
        used[0] += count
        return at

    def remote(src, dst, send_at, recv_at, device):
        return pltpu.make_async_remote_copy(
            src_ref=src,
            dst_ref=dst,
            send_sem=send_sem.at[send_at],
            recv_sem=recv_sem.at[recv_at],
            device_id=device,
            device_id_type=MESH,
        )

    def send(src, dst, device, send_at=None, recv_at=None):
        if send_at is None:
            send_at = recv_at = slots(1)
        made = remote(src, dst, send_at, recv_at, device)
        made.start()
        waits.append(made)
        return made

    core_peer = (utt, 2 * x + 1 - c)
    x_peer = (utt, 2 * (1 - x) + c)
    cross_peer = (utt, 2 * (1 - x) + 1 - c)
    y_peer = (2 * z + 1 - y, tm)
    xy_peer = (2 * z + 1 - y, 2 * (1 - x) + c)
    plane = [x_peer, y_peer, xy_peer]
    plane_at = [(y, 1 - x), (1 - y, x), (1 - y, 1 - x)]
    z_at = [z, z + 1 - 2 * (z % 2), (z + 2) % 4, 3 - z]
    other_z = [j + (j - z + 4) // 4 for j in range(3)]

    barrier = pltpu.get_barrier_semaphore()
    partners = [core_peer, x_peer, cross_peer]
    if fast:
        partners += [(2 * zz + y, tm) for zz in other_z] + [y_peer, xy_peer]
    else:
        partners += [((utt + k) % n_utt, tm) for k in range(1, n_utt)]
    for partner in partners:
        pl.semaphore_signal(barrier, inc=1, device_id=partner, device_id_type=MESH)
    fetches = [
        pltpu.make_async_copy(x_in, XS, local_sem.at[0]),
        pltpu.make_async_copy(cot_in, CS, local_sem.at[1]),
        pltpu.make_async_copy(tab.at[half], TB, local_sem.at[2]),
        pltpu.make_async_copy(lens_in, lens, local_sem.at[4]),
    ]
    if fast:
        flat_fetch = pltpu.make_async_copy(flat_in, FLAT, local_sem.at[3])
        flat_fetch.start()
    for fetch in fetches:
        fetch.start()

    lane = lax.broadcasted_iota(jnp.int32, (1, 128), 1)
    lane_d = lax.broadcasted_iota(jnp.int32, (1, D), 1)

    def lanes_of(g):
        return (lane >= TAIL * g) & (lane < TAIL * (g + 1))

    def turned(v, shift):
        return v if shift % 128 == 0 else pltpu.roll(v, shift % 128, 1)

    def tails_of(rows):
        packed = jnp.zeros((16, 128), F32)
        for g in range(7):
            packed = jnp.where(lanes_of(g), turned(rows[16 * g : 16 * g + 16], TAIL * g), packed)
        return packed

    def rows_of_tails(packed):
        return jnp.concatenate([turned(packed, -TAIL * g) for g in range(7)], axis=0)

    if fast:
        own = GB.at[z, y, x, c]
        flat_fetch.wait()
        for i in range(15):
            GM[8 * i : 8 * i + 8, :] = FLAT[pl.ds(1024 * i, 1024)].reshape(8, 128)
        rest = LOCAL_SIZE - 15 * 1024
        GM[120:128, :] = jnp.concatenate(
            [FLAT[pl.ds(15 * 1024, rest)], jnp.zeros((1024 - rest,), F32)]
        ).reshape(8, 128)
        dense = [GM[pl.ds(i, 14, stride=9), :] for i in range(9)]
        for i in range(8):
            shift = TAIL * i
            left = turned(dense[i], -shift)
            right = turned(dense[i + 1], -shift)
            WM[pl.ds(i, 14, stride=8), :] = jnp.where(lane < 128 - shift, left, right)
            WT[pl.ds(i, 14, stride=8), :] = right
        own[0:MAIN, :] = WM[0:MAIN, :].astype(BF16)
        own[MAIN:BLOCK, :] = tails_of(WT[0:MAIN, :]).astype(BF16)
        col_at, p_at, c_at = slots(4), slots(12), slots(4)

        def to_column(j):
            to = (2 * z_at[3 - j] + y, tm)
            remote(own, own, col_at, col_at + z, to).start()

        def to_plane(zz, mates):
            block = GB.at[zz, y, x, c]
            for m in range(mates):
                remote(block, block, p_at, p_at + 4 * m + zz, plane[m]).start()

        def diagonal_to_column():
            block = GB.at[z, 1 - y, 1 - x, c]
            remote(block, block, p_at, p_at + 8 + z, core_peer).wait_recv()
            for j in range(3):
                to = (2 * z_at[3 - j] + y, tm)
                remote(block, block, p_at, p_at + 8 + z, to).start()
            to_core(z, (1 - y, 1 - x))

        def from_plane(zz, mates):
            for m in range(mates):
                block = GB.at[zz, plane_at[m][0], plane_at[m][1], c]
                remote(block, block, p_at, p_at + 4 * m + zz, core_peer).wait_recv()
                to_core(zz, plane_at[m])

        def diagonal_from_column(zz):
            @pl.when(z != zz)
            def _():
                block = GB.at[zz, 1 - y, 1 - x, c]
                remote(block, block, p_at, p_at + 8 + zz, core_peer).wait_recv()
                to_core(zz, (1 - y, 1 - x))

        def to_core(zz, where):
            block = GB.at[zz, where[0], where[1], c]
            remote(block, block, c_at, c_at + zz, core_peer).start()

        waits.append(remote(R2.at[0], R2.at[0], col_at, col_at, core_peer))
        waits.append(remote(R2, R2, p_at, p_at, core_peer))
        waits.append(remote(GB.at[0:2], GB.at[0:2], c_at, c_at, core_peer))

        def from_core(zz):
            blocks = GB.at[zz, :, :, 1 - c]
            remote(blocks, blocks, c_at, c_at + zz, core_peer).wait_recv()
            for low_d in range(8):
                block = GB.at[zz, low_d // 4, (low_d // 2) % 2, low_d % 2]
                first = 110 * (8 * zz + low_d)
                WM[first : first + 110, :] = block[0:110, :].astype(F32)
                WT[first : first + 110, :] = rows_of_tails(block[MAIN:BLOCK, :].astype(F32))[0:110]

    pl.semaphore_wait(barrier, len(partners))
    if fast:
        for j in range(3):
            to_column(j)

    def exchange(source, target):
        return (
            send(source.at[1 - x], target.at[tm], x_peer),
            send(source.at[x], target.at[tm], core_peer),
        )

    def relay(copies, target):
        copies[0].wait_recv()
        passed = target.at[x_peer[1]]
        return copies[1], send(passed, passed, core_peer)

    def unpack_frames(copies, source, target, frames):
        for made in copies:
            made.wait_recv()
        target[tm] = source[unit]
        for k in range(4):
            frames[LOCAL * k : LOCAL * (k + 1), :] = target[k].astype(F32).T

    fetches[0].wait()
    x_copies = exchange(XS, XB)
    if fast:
        to_plane(z, 3)
        to_core(z, (y, x))
    x_copies = relay(x_copies, XB)
    if fast:
        diagonal_to_column()
        for j in range(3):
            block = GB.at[other_z[j], y, x, c]
            remote(block, block, col_at, col_at + other_z[j], core_peer).wait_recv()
            to_plane(other_z[j], 2)
            to_core(other_z[j], (y, x))
    fetches[1].wait()
    c_copies = exchange(CS, CB)

    def rows_of(name, count=1, shift=0, stride=1):
        at = ROW[name] + shift
        s = pl.ds(at, count) if stride == 1 else pl.ds(at, count, stride=stride)
        return join(WM[s, :], WT[s, :])

    def put(name, value, shift=0, stride=1):
        at = ROW[name] + shift
        count = value.shape[0]
        if stride == 1:
            GM[pl.ds(at, count), :] = value[:, :128]
            GT[pl.ds(at, count), 0:TAIL] = value[:, 128:]
        else:
            s = pl.ds(at, count, stride=stride)
            GM[s, :] = value[:, :128]
            GT[s, :] = jnp.concatenate(
                [value[:, 128:], jnp.zeros((count, 128 - TAIL), F32)], axis=1
            )

    def ready(prefixes):
        for i, (name, shift, stride) in enumerate(SQUARES):
            if name.startswith(prefixes):
                WS[i] = rows_of(name, D, shift, stride).astype(BF16)

    def square(name, shift=0):
        return WS[SQUARE[name, shift]]

    row = lax.broadcasted_iota(jnp.int32, (ROWS, 1), 0)
    frame = row + start
    own_row = ((frame >= HALF * half) & (frame < HALF * half + HALF)).astype(F32)
    own_low = own_row.astype(BF16)
    fetches[3].wait()
    length = jnp.where(unit == 0, lens[0], lens[1])
    live = (frame < length).astype(F32)
    scale = HEAD_DIM ** (-0.5)
    window = pl.ds(start, ROWS)

    unpack_frames(x_copies, XS, XB, XF)
    first_norm = normed(XF[0:LEN, :])
    NRM1[...], INV1[...] = first_norm
    if fast:
        from_plane(0, 2)
        diagonal_from_column(0)
        from_plane(1, 2)
        diagonal_from_column(1)
        from_core(0)
        from_core(1)
    ready("first")
    c_copies = relay(c_copies, CB)

    def feed(scaled, prefix, HID, ACT):
        low = (scaled * rows_of(prefix + "_gain") + rows_of(prefix + "_bias")).astype(BF16)
        total = rows_of(prefix + "_b_out")
        for j in range(CHUNKS):
            hidden = mm(low, square(prefix + "_w_in", j)) + rows_of(prefix + "_b_in", 1, j)
            if prefix == "first":
                HID[j] = hidden
                active = hidden * sigmoid(hidden)
            else:
                active, HID[j] = silu(hidden)
            active = active.astype(BF16)
            ACT[j] = active
            total = total + mm(active, square(prefix + "_w_out", j * D))
        return total, low

    v = XF[0:LEN, :]
    total, low = feed(NRM1[...], "first", HID1, ACT1)
    LOW1[...] = low
    x1 = v + 0.5 * total
    X1[...] = x1

    if fast:
        for zz in (2, 3):
            from_plane(zz, 2)
            diagonal_from_column(zz)
        from_core(2)
    ready(("query", "key", "value", "pos_w", "proj", "point", "mix"))
    fetches[2].wait()
    scaled, inverse = normed(x1)
    low = (scaled * rows_of("att_gain") + rows_of("att_bias")).astype(BF16)
    A2[...] = low
    KEY[...] = mm(low, square("key_w")).astype(BF16)
    VAL[...] = (mm(low, square("value_w")) + rows_of("value_b")).astype(BF16)
    a2 = A2[window, :]
    query = mm(a2, square("query_w")) + rows_of("query_b")
    qu = ((query + rows_of("content_bias")) * scale).astype(BF16)
    qv = ((query + rows_of("position_bias")) * scale).astype(BF16)
    positions = mm(TB[...], square("pos_w")).astype(BF16)
    key_bias = jnp.where(
        lax.broadcasted_iota(jnp.int32, (1, LEN), 1) < length, 0.0, NEGATIVE
    )

    def head_mask(h):
        return ((lane_d >= HEAD_DIM * h) & (lane_d < HEAD_DIM * (h + 1))).astype(BF16)

    for h in range(HEADS):
        mask = head_mask(h)
        PR[h] = nt(qu * mask, KEY[...])
        WD[h] = nt(qv * mask, positions)
    context, share = jnp.zeros((ROWS, D), F32), jnp.zeros((ROWS, D), F32)
    for h in range(HEADS):
        for lo in range(0, ROWS, STRIP):
            strip = slice(lo, lo + STRIP)
            wide = pltpu.roll(WD[h, strip, :], WIDE - ROWS + 1 + lo, 1, stride=1, stride_axis=0)
            score = PR[h, strip, :] + wide[:, :LEN] + key_bias
            score = jnp.exp(score - jnp.max(score, axis=1, keepdims=True))
            PR[h, strip, :] = score
            PB[h, strip, :] = score.astype(BF16)
        mask = head_mask(h)
        context = context + mm(PB[h], VAL[...] * mask)
        share = share + mm(PB[h], jnp.broadcast_to(mask, (LEN, D)))
    context = (context / share).astype(BF16)
    x2 = X1[window, :] + mm(context, square("proj_w")) + rows_of("proj_b")

    conv_n, conv_i = normed(x2)
    a3 = (conv_n * rows_of("conv_gain") + rows_of("conv_bias")).astype(BF16)
    value = mm(a3, square("point_w", 0)) + rows_of("point_b", 1, 0)
    gate = sigmoid(mm(a3, square("point_w", 1)) + rows_of("point_b", 1, 1))
    SEGMENT = ROWS // 8

    def segments(ref, count):
        packed = turned(ref[0:count, :], 0)
        for g in range(1, 8):
            v = turned(ref[SEGMENT * g : SEGMENT * g + count, :], TAIL * g)
            packed = jnp.where(lane >= TAIL * g, v, packed)
        return packed

    def unsegmented(v):
        for g in range(8):
            CT[SEGMENT * g : SEGMENT * (g + 1), :] = turned(v, -TAIL * g)[0:SEGMENT]
        return CT[0:ROWS, :]

    def lay(v, main, tail):
        for lo, hi in ((0, EDGE), (EDGE + ROWS, 2 * EDGE + ROWS)):
            main[lo:hi, :] = jnp.zeros((hi - lo, 128), F32)
            CT[lo:hi, :] = jnp.zeros((hi - lo, 128), F32)
        main[EDGE : EDGE + ROWS, :] = v[:, :128]
        CT[EDGE : EDGE + ROWS, 0:TAIL] = v[:, 128:]
        tail[...] = segments(CT, 64)

    def convolved(main, tail, first):
        blocks = []
        for lo in range(0, ROWS, 80):
            total = depth_m[0:1] * main[pl.ds(lo + first(0), 80), :]
            for o in range(1, KERNEL):
                total = total + depth_m[o : o + 1] * main[pl.ds(lo + first(o), 80), :]
            blocks.append(total)
        total = depth_t[0:1] * tail[pl.ds(first(0), 32), :]
        for o in range(1, KERNEL):
            total = total + depth_t[o : o + 1] * tail[pl.ds(first(o), 32), :]
        return join(jnp.concatenate(blocks, axis=0), unsegmented(total))

    depth_rows = pl.ds(ROW["depth_w"], KERNEL)
    depth_m = WM[depth_rows, :]
    depth_t = jnp.where(lane < TAIL, WT[depth_rows, :], 0.0)
    for shift in (TAIL, 2 * TAIL, 4 * TAIL):
        depth_t = depth_t + turned(depth_t, shift)
    CT[2 * EDGE + ROWS :, :] = jnp.zeros((CT.shape[0] - 2 * EDGE - ROWS, 128), F32)
    lay((live * value * gate).astype(BF16).astype(F32), GLM, GLT)
    forth = lambda o: EDGE - LEFT + o
    conv = convolved(GLM, GLT, forth)

    def begin_sum(which, first, second):
        lengths = jnp.where(tm == 0, lens[0] + lens[1], 0).astype(F32)
        blank = jnp.zeros((1, 128 - TAIL), F32)
        BS[which, 0] = jnp.concatenate(
            [
                first[:, :128],
                jnp.concatenate([first[:, 128:], blank], axis=1),
                second[:, :128],
                jnp.concatenate([second[:, 128:], blank], axis=1),
                jnp.full((4, 128), lengths),
            ],
            axis=0,
        )
        if fast:
            sent, at = [], slots(1)
            for k in range(31, 0, -1):
                kz, dy, dx, dc = k // 8, (k // 4) % 2, (k // 2) % 2, k % 2
                to_y, to_x, to_c = (1 - v if d else v for v, d in ((y, dy), (x, dx), (c, dc)))
                to = (2 * z_at[kz] + to_y, 2 * to_x + to_c)
                remote(BS.at[which, 0], BB.at[which, k - 1], at, at, to).start()
            sent.append(remote(BB.at[which], BB.at[which], at, at, core_peer))
            waits.extend(sent)
        else:
            sent = [
                send(BS.at[which, 0], BB.at[which, k], mate)
                for k, mate in enumerate((x_peer, cross_peer, core_peer))
            ]
        return sent

    def end_sum(which, sent):
        def arrived(copies, at, count, total):
            for made in copies:
                made.wait_recv()
            for k in range(count):
                total = total + BB[which, at + k]
            return total

        total = arrived(sent, 0, 31 if fast else 3, BS[which, 0])
        if not fast:
            BS[which, 1] = total
            sent = [
                send(BS.at[which, 1], BB.at[which, 2 + k], ((utt + k) % n_utt, tm))
                for k in range(1, n_utt)
            ]
            total = arrived(sent, 3, n_utt - 1, total)
        return join(total[0:1], total[1:2]), join(total[2:3], total[3:4]), total[4:5, 0:1]

    counted = own_row * live
    sent = begin_sum(0, colsum(counted * conv), colsum(counted * conv * conv))
    if fast:
        from_core(3)
    ready("second")
    flip = (
        lax.broadcasted_iota(jnp.int32, (ROWS, ROWS), 0)
        + lax.broadcasted_iota(jnp.int32, (ROWS, ROWS), 1)
        == ROWS - 1
    ).astype(F32).astype(BF16)
    qu_r = mm(flip, qu).astype(BF16)
    qv_r = mm(flip, qv).astype(BF16)
    def transposed(v):
        return v.astype(F32).T.astype(BF16)

    for h in range(HEADS):
        prob = PR[h]
        prob = prob * (1.0 / jnp.sum(prob, axis=1, keepdims=True))
        high = prob.astype(BF16)
        rest = (prob - high.astype(F32)).astype(BF16)
        turned_high = mm(flip, high)
        PB[h] = turned_high.astype(BF16)
        PR[h] = turned_high + mm(flip, rest)
    for source, target in ((qu_r, QUT), (qv_r, QVT)):
        v = source.astype(F32).T
        for h in range(HEADS):
            target[h] = v[HEAD_DIM * h : HEAD_DIM * (h + 1)].astype(BF16)
    for j in range(CHUNKS):
        XT[j] = transposed(ACT1[j, window, :])
        HID1[j, 0:ROWS, :] = silu(HID1[j, window, :])[1]
    unpack_frames(c_copies, CS, CB, CF)
    for j, v in enumerate((LOW1[window, :], a2, a3, context)):
        XT[CHUNKS + j] = transposed(v)
    first_sum, second_sum, count = end_sum(0, sent)
    mu = first_sum / count
    spread = lax.rsqrt(second_sum / count - mu * mu + EPS)
    bn = (conv - mu) * spread
    zed = bn * rows_of("batch_gain") + rows_of("batch_bias")
    swished, zed_slope = silu(zed)
    swished = swished.astype(BF16)
    x3 = x2 + mm(swished, square("mix_w")) + rows_of("mix_b")

    second_n, second_i = normed(x3)
    total, second_low = feed(second_n, "second", HID2, ACT2)
    x4 = x3 + 0.5 * total
    final_n, final_i = normed(x4)
    result = final_n * rows_of("final_gain") + rows_of("final_bias")

    def return_frames(v, S, B):
        send_at, recv_at = slots(2), slots(2)
        made = []
        for j in range(2):
            lo, hi = LOCAL * j, HALF - HALO_START + LOCAL * j
            S[j] = jnp.where(half == 0, v[lo : lo + LOCAL, :], v[hi : hi + LOCAL, :]).T
            made.append(
                remote(S.at[j], B.at[unit], send_at + j, recv_at + unit, (utt, 2 * half + j))
            )

        def launch():
            for j in range(2):
                away = 2 * half + j != tm

                @pl.when(away)
                def _(sent=made[j]):
                    sent.start()

                @pl.when(jnp.logical_not(away))
                def _(j=j):
                    B[unit] = S[j]

        def finish():
            for j in range(2):

                @pl.when(2 * half + j != tm)
                def _(sent=made[j]):
                    sent.wait_send()

            for u in range(2):

                @pl.when(2 * u + x != tm)
                def _(u=u):
                    remote(S.at[0], B.at[u], send_at, recv_at + u, core_peer).wait_recv()

        return launch, finish


    g0 = CF[window, :] * live
    d4 = norm_back(g0, rows_of("final_gain"), final_n, final_i)

    def feed_back(grad, prefix, slope_of, active_t, scaled, inverse, low_t, masked):
        low_grad = (0.5 * grad).astype(BF16)
        back = jnp.zeros((ROWS, D), F32)
        hidden_grads = []
        for j in range(CHUNKS):
            grad_hidden = nt(low_grad, square(prefix + "_w_out", j * D))
            grad_hidden = (grad_hidden * slope_of(j)).astype(BF16)
            hidden_grads.append(grad_hidden)
            back = back + nt(grad_hidden, square(prefix + "_w_in", j))

        def out_weights(chunks):
            kept = low_grad * own_low if masked else low_grad
            if CHUNKS - 1 in chunks:
                put(prefix + "_b_out", colsum(kept.astype(F32)))
            for j in chunks:
                put(prefix + "_w_out", mm(active_t(j), kept), j * D)

        def in_weights():
            for j in range(CHUNKS):
                grad_hidden = hidden_grads[j] * own_low if masked else hidden_grads[j]
                put(prefix + "_w_in", mm(low_t(), grad_hidden), j, CHUNKS)
                put(prefix + "_b_in", colsum(grad_hidden.astype(F32)), j)
            kept = back * own_row if masked else back
            put(prefix + "_gain", colsum(kept * scaled))
            put(prefix + "_bias", colsum(kept))

        total = grad + norm_back(back, rows_of(prefix + "_gain"), scaled, inverse)
        return total, out_weights, in_weights

    d3, second_out_weights, second_in_weights = feed_back(
        d4,
        "second",
        lambda j: HID2[j],
        lambda j: transposed(ACT2[j]),
        second_n,
        second_i,
        lambda: transposed(second_low),
        True,
    )

    if fast:
        pieces = [(0, 0, 64), (0, 64, BLOCK), (1, 0, BLOCK), (2, 0, BLOCK), (3, 0, BLOCK)]
        z_send, z_recv = slots(len(pieces)), slots(4 * len(pieces))
        stage = {}

        def add(a, b):
            return a.astype(F32) + b.astype(F32)

        def pieces_of(goal):
            return [piece for piece in pieces if piece[0] == goal]

        def begin_round(goal):
            for piece in pieces_of(goal):
                lo, hi = piece[1:]
                rows = pl.ds(lo, hi - lo)
                for d in range(8):
                    first = 110 * (8 * goal + d)
                    block = LB.at[goal, d // 4, (d // 2) % 2, d % 2]
                    top = min(hi, MAIN)
                    block[lo:top, :] = GM[first + lo : first + top, :].astype(BF16)
                    if hi == BLOCK:
                        tails = tails_of(GT[first : first + MAIN, :])
                        block[MAIN:BLOCK, :] = tails.astype(BF16)
                stage[piece] = send(
                    LB.at[goal, :, :, 1 - c, rows], R1.at[goal, :, :, rows], core_peer
                )

        def plane_round(goal):
            for piece in pieces_of(goal):
                lo, hi = piece[1:]
                rows = pl.ds(lo, hi - lo)
                stage[piece].wait_recv()
                for yy in range(2):
                    for xx in range(2):
                        both = add(LB[goal, yy, xx, c, lo:hi], R1[goal, yy, xx, lo:hi])
                        ACC[goal, yy, xx, lo:hi] = both.astype(BF16)
                at = slots(1)
                for m in range(3):
                    block = ACC.at[goal, plane_at[m][0], plane_at[m][1], rows]
                    remote(block, R2.at[goal, m, rows], at, at, plane[m]).start()
                all_three = R2.at[goal, :, rows]
                stage[piece] = remote(all_three, all_three, at, at, core_peer)
                waits.append(stage[piece])

        def z_copy(piece, sender):
            goal, lo, hi = piece
            rows, index = pl.ds(lo, hi - lo), pieces.index(piece)
            return remote(
                R3.at[goal, rows],
                RZ.at[sender, rows],
                z_send + index,
                z_recv + 4 * index + sender,
                (2 * goal + y, tm),
            )

        def z_round(goal):
            for piece in pieces_of(goal):
                lo, hi = piece[1:]
                stage[piece].wait_recv()
                total = add(ACC[goal, y, x, lo:hi], R2[goal, 0, lo:hi])
                total = total + add(R2[goal, 1, lo:hi], R2[goal, 2, lo:hi])
                R3[goal, lo:hi] = total.astype(BF16)

                @pl.when(z != goal)
                def _(piece=piece):
                    z_copy(piece, z).start()

    else:
        begin_round = plane_round = z_round = lambda goal: None

    low_grad = d3.astype(BF16)
    dzed = nt(low_grad, square("mix_w")).astype(BF16).astype(F32)
    dzed = dzed * zed_slope
    e = dzed * rows_of("batch_gain")
    e_own = e * counted
    sent = begin_sum(1, colsum(e_own), colsum(e_own * bn))
    launch_out, finish_out = return_frames(result, OS, out)
    launch_out()
    for V in (GM, GT):
        V[USED : USED + 8, :] = jnp.zeros((8, 128), F32)
    g0_own = g0 * own_row
    put("final_gain", colsum(g0_own * final_n))
    put("final_bias", colsum(g0_own))
    second_out_weights(range(CHUNKS))
    second_in_weights()
    begin_round(3)
    kept = low_grad * own_low
    put("mix_w", tn(swished, kept))
    put("mix_b", colsum(kept.astype(F32)))
    dzed_own = dzed * own_row
    put("batch_gain", colsum(dzed_own * bn))
    put("batch_bias", colsum(dzed_own))
    parts = (e, jnp.broadcast_to(live, (ROWS, D)), live * bn)
    back_parts, depth_parts = [], []
    for i, v in enumerate(parts):
        lay(v, VM, VT)
        back_parts.append(convolved(VM, VT, lambda o: EDGE + LEFT - o))
        kept = v * own_row
        kept_m = kept[:, :128]
        CT[0:ROWS, 0:TAIL] = kept[:, 128:]
        segment_row = lax.broadcasted_iota(jnp.int32, (32, 1), 0) < SEGMENT
        kept_t = jnp.where(segment_row, segments(CT, 32), 0.0)
        mains, tails = [], []
        for o in range(KERNEL):
            mains.append(colsum(kept_m * GLM[pl.ds(forth(o), ROWS), :]))
            tails.append(colsum(kept_t * GLT[pl.ds(forth(o), 32), :]))
        tails = jnp.concatenate(tails, axis=0)
        for shift in (4 * TAIL, 2 * TAIL, TAIL):
            tails = tails + turned(tails, shift)
        depth_parts.append(join(jnp.concatenate(mains, axis=0), tails))
    first_sum, second_sum, count = end_sum(1, sent)
    plane_round(3)
    first_mean, second_mean = first_sum / count, second_sum / count

    def combined(v):
        return spread * (v[0] - v[1] * first_mean - v[2] * second_mean)

    dglu = combined(back_parts).astype(BF16).astype(F32) * counted
    dvalue = (dglu * gate).astype(BF16)
    dgate = (dglu * value * gate * (1.0 - gate)).astype(BF16)
    back = nt(dvalue, square("point_w", 0)) + nt(dgate, square("point_w", 1))
    conv_back = back
    d2 = d3 * own_row + norm_back(back, rows_of("conv_gain"), conv_n, conv_i)

    low_grad = d2.astype(BF16)
    dproj = low_grad
    dctx = nt(low_grad, square("proj_w")).astype(BF16)
    dctx = mm(flip, dctx)
    dctx_t = dctx.T
    dctx = dctx.astype(BF16)
    heads = [slice(HEAD_DIM * h, HEAD_DIM * (h + 1)) for h in range(HEADS)]
    theirs = pl.ds(pl.multiple_of(HALO_START * (1 - half), 16), ROWS)
    for h in range(HEADS):
        PD[h] = nt(dctx * head_mask(h), VAL[...])
        DVT[heads[h], :] = mm(dctx_t[heads[h]].astype(BF16), PB[h])
    DVA[...] = DVT[0:D, :].T
    KS[1] = DVA[theirs, :].astype(BF16)
    value_copy = send(KS.at[1], KB.at[1], core_peer)
    for h in range(HEADS):
        for lo in range(0, ROWS, STRIP):
            strip = slice(lo, lo + STRIP)
            prob, dprob = PR[h, strip, :], PD[h, strip, :]
            dscore = prob * (dprob - jnp.sum(dprob * prob, axis=1, keepdims=True))
            LS[h, strip, :] = dscore.astype(BF16)
            wide = jnp.concatenate([dscore, jnp.zeros((STRIP, WIDE - LEN), F32)], axis=1)
            wide = pltpu.roll(wide, lo, 1, stride=1, stride_axis=0)
            WB[h, strip, :] = wide.astype(BF16)
        DKT[heads[h], :] = mm(QUT[h], LS[h])
    DKA[...] = DKT[0:D, :].T
    KS[0] = DKA[theirs, :].astype(BF16)
    key_copy = send(KS.at[0], KB.at[0], core_peer)
    du, dw = jnp.zeros((ROWS, D), F32), jnp.zeros((ROWS, D), F32)
    for h in range(HEADS):
        mask = head_mask(h)
        du = du + mm(LS[h], KEY[...] * mask)
        dw = dw + mm(WB[h], positions * mask)
    dquery = mm(flip, (scale * (du + dw)).astype(BF16)).astype(BF16)
    put("depth_w", combined(depth_parts))
    put("point_w", mm(XT[CHUNKS + 2], dvalue), 0, 2)
    put("point_w", mm(XT[CHUNKS + 2], dgate), 1, 2)
    put("point_b", colsum(dvalue.astype(F32)), 0)
    put("point_b", colsum(dgate.astype(F32)), 1)
    put("conv_gain", colsum(conv_back * conv_n))
    put("conv_bias", colsum(conv_back))
    put("proj_w", mm(XT[CHUNKS + 3], dproj))
    put("proj_b", colsum(dproj.astype(F32)))
    z_round(3)
    begin_round(2)
    att_n, att_i = normed(X1[window, :])
    key_copy.wait_recv()
    value_copy.wait_recv()
    dkey = ((DKA[window, :] + KB[0].astype(F32)) * own_row).astype(BF16)
    dval = ((DVA[window, :] + KB[1].astype(F32)) * own_row).astype(BF16)
    back = (
        nt(dquery, square("query_w"))
        + nt(dkey, square("key_w"))
        + nt(dval, square("value_w"))
    )
    att_back = back
    d1 = d2 + norm_back(back, rows_of("att_gain"), att_n, att_i)

    d0, first_out_weights, first_in_weights = feed_back(
        d1,
        "first",
        lambda j: HID1[j, 0:ROWS, :],
        lambda j: XT[j],
        NRM1[window, :],
        INV1[window, :],
        lambda: XT[CHUNKS],
        False,
    )
    first_in_weights()
    first_out_weights(range(CHUNKS - 1))
    begin_round(0)
    first_out_weights(range(CHUNKS - 1, CHUNKS))
    put("query_w", mm(XT[CHUNKS + 1], dquery))
    put("query_b", colsum(dquery.astype(F32)))
    put("key_w", mm(XT[CHUNKS + 1], dkey))
    put("value_w", mm(XT[CHUNKS + 1], dval))
    put("value_b", colsum(dval.astype(F32)))
    put("att_gain", colsum(att_back * att_n))
    put("att_bias", colsum(att_back))
    plane_round(0)
    for h in range(HEADS):
        DPT[heads[h], :] = mm(QVT[h], WB[h])
    dpos = DPT[0:D, :]
    high = dpos.astype(BF16)
    rest = (dpos - high.astype(F32)).astype(BF16)
    put("pos_w", (mm(high, TB[...]) + mm(rest, TB[...])).T)
    put("content_bias", scale * colsum(du))
    put("position_bias", scale * colsum(dw))
    begin_round(1)
    launch_grad, finish_grad = return_frames(d0, IS, grad_out)
    plane_round(2)
    plane_round(1)
    launch_grad()
    z_round(0)
    z_round(2)
    z_round(1)

    finish_out()
    finish_grad()
    for made in waits:
        made.wait_send()
    if fast:
        for piece in pieces:

            @pl.when(z != piece[0])
            def _(piece=piece):
                z_copy(piece, z).wait_send()

            @pl.when(z == piece[0])
            def _(piece=piece):
                for j in range(3):
                    z_copy(piece, other_z[j]).wait_recv()

        total = R3[z].astype(F32)
        for j in range(3):
            total = total + RZ[other_z[j]].astype(F32)
        WM[0:MAIN, :] = total[0:MAIN]
        GT[0:MAIN, :] = rows_of_tails(total[MAIN:BLOCK])
        mains = [WM[pl.ds(i, 14, stride=8), :] for i in range(8)]
        tails = [GT[pl.ds(i, 14, stride=8), :] for i in range(8)]
        for i in range(9):
            row_i = turned(tails[max(i - 1, 0)], TAIL * (i - 1))
            if i < 8:
                row_i = jnp.where(lane >= TAIL * i, turned(mains[i], TAIL * i), row_i)
            if i > 0:
                v = turned(mains[i - 1], TAIL * (i - 1))
                row_i = jnp.where(lane < TAIL * (i - 1), v, row_i)
            WT[pl.ds(i, 14, stride=9), :] = row_i
        for i in range(15):
            flat_out[pl.ds(1024 * i, 1024)] = WT[8 * i : 8 * i + 8, :].reshape(1024)
        rest = LOCAL_SIZE - 15 * 1024
        flat_out[pl.ds(15 * 1024, rest)] = WT[120:128, :].reshape(1024)[0:rest]


def hand_over(first, second, third, first_out, second_out, third_out):
    first_out[...] = first[...]
    second_out[...] = second[...]
    third_out[...] = third[...]


def local(inputs, flat_params, lengths, cotangent):
    n_utt, n_tm = lax.axis_size("utt"), lax.axis_size("tm")
    size = flat_params.shape[0]
    fast = n_utt == 8 and n_tm == 4 and size == LOCAL_SIZE
    table = jnp.asarray(reversed_tables())
    turned = jax.ShapeDtypeStruct((2, D, LOCAL), F32)
    padded = jax.ShapeDtypeStruct((PADDED, 128), F32)
    vmem = pltpu.VMEM
    in_vmem = pl.BlockSpec(memory_space=pltpu.VMEM)
    anywhere = pl.BlockSpec(memory_space=pl.ANY)
    if fast:
        operands = [flat_params]
        results = [turned, turned, jax.ShapeDtypeStruct((size,), F32)]
        scratch = [vmem((PADDED, 128), F32)] * 4 + [
            vmem((size,), F32),
            vmem((4, 2, 2, 2, BLOCK, 128), BF16),
            vmem((4, 2, 2, 2, BLOCK, 128), BF16),
            vmem((4, 2, 2, BLOCK, 128), BF16),
            vmem((4, 3, BLOCK, 128), BF16),
            vmem((4, BLOCK, 128), BF16),
            vmem((4, BLOCK, 128), BF16),
            vmem((4, 2, 2, BLOCK, 128), BF16),
        ]
    else:
        rows = lax.all_gather(flat_params, ("utt", "tm"), axis=0, tiled=True).reshape(TOTAL, D)
        operands = [
            jnp.pad(rows[:, :128], ((0, PADDED - TOTAL), (0, 0))),
            jnp.pad(rows[:, 128:], ((0, PADDED - TOTAL), (0, 128 - TAIL))),
        ]
        results = [turned, turned, padded, padded]
        scratch = []
    others = 31 if fast else 3 + n_utt - 1
    copies = 128 + 2 * others
    scratch = scratch + [
        vmem((2, D, LOCAL), BF16),
        vmem((2, D, LOCAL), BF16),
        vmem((4, D, LOCAL), BF16),
        vmem((4, D, LOCAL), BF16),
        vmem((WIDE, D), BF16),
        vmem((LEN + 8, D), F32),
        vmem((LEN + 8, D), F32),
        vmem((2, D, LOCAL), F32),
        vmem((2, D, LOCAL), F32),
        vmem((len(SQUARES), D, D), BF16),
        vmem((CHUNKS, LEN, D), F32),
        vmem((CHUNKS, LEN, D), BF16),
        vmem((LEN, D), F32),
        vmem((LEN, 1), F32),
        vmem((LEN, D), BF16),
        vmem((LEN, D), F32),
        vmem((LEN, D), BF16),
        vmem((CHUNKS, ROWS, D), F32),
        vmem((CHUNKS, ROWS, D), BF16),
        vmem((LEN, D), BF16),
        vmem((LEN, D), BF16),
        vmem((HEADS, ROWS, LEN), F32),
        vmem((HEADS, ROWS, LEN), F32),
        vmem((HEADS, ROWS, WIDE), F32),
        vmem((HEADS, ROWS, WIDE), BF16),
        vmem((HEADS, ROWS, LEN), BF16),
        vmem((HEADS, ROWS, LEN), BF16),
        vmem((HEADS, HEAD_DIM, ROWS), BF16),
        vmem((HEADS, HEAD_DIM, ROWS), BF16),
        vmem((CHUNKS + 4, D, ROWS), BF16),
        vmem((D + 8, LEN), F32),
        vmem((D + 8, LEN), F32),
        vmem((D + 8, WIDE), F32),
        vmem((LEN, D), F32),
        vmem((LEN, D), F32),
        vmem((ROWS + 2 * EDGE, 128), F32),
        vmem((64, 128), F32),
        vmem((ROWS + 2 * EDGE, 128), F32),
        vmem((64, 128), F32),
        vmem((288, 128), F32),
        vmem((2, ROWS, D), BF16),
        vmem((2, ROWS, D), BF16),
        vmem((2, 2, 8, 128), F32),
        vmem((2, others, 8, 128), F32),
        pltpu.SMEM((2,), jnp.int32),
        pltpu.SemaphoreType.DMA((copies,)),
        pltpu.SemaphoreType.DMA((copies,)),
        pltpu.SemaphoreType.DMA((5,)),
    ]
    got = pl.pallas_call(
        functools.partial(kernel, n_utt, fast),
        out_shape=results,
        in_specs=[anywhere] * 4
        + [anywhere if fast else in_vmem] * len(operands),
        out_specs=[in_vmem] * len(results),
        scratch_shapes=scratch,
        compiler_params=pltpu.CompilerParams(
            collective_id=0, has_side_effects=True, vmem_limit_bytes=56 * 1024 * 1024
        ),
    )(lengths, jnp.swapaxes(inputs, 1, 2), jnp.swapaxes(cotangent, 1, 2), table, *operands)
    if fast:
        out, grad, grad_params = pl.pallas_call(
            hand_over,
            out_shape=results,
            in_specs=[in_vmem] * 3,
            out_specs=[in_vmem] * 3,
        )(*got)
    else:
        out, grad = got[:2]
        rows = jnp.concatenate([got[2][:TOTAL], got[3][:TOTAL, :TAIL]], axis=1)
        grad_params = lax.psum_scatter(
            rows.reshape(-1), ("utt", "tm"), scatter_dimension=0, tiled=True
        )
    return jnp.swapaxes(out, 1, 2), jnp.swapaxes(grad, 1, 2), grad_params


def solution(mesh):
    return jax.shard_map(
        local,
        mesh=mesh,
        in_specs=(P("utt", "tm", None), P(("utt", "tm")), P("utt"), P("utt", "tm", None)),
        out_specs=(P("utt", "tm", None), P("utt", "tm", None), P(("utt", "tm"))),
        check_vma=False,
    )
```
